128 devices in a mesh: section: 2 (over x_lo), shard: 4 (over x_hi, core), replica: 16 (over z, y).
Axes of the slice: x: 4 (x_hi: 2, x_lo: 2; x = x_hi * 2 + x_lo), y: 4, z: 4, core: 2. Of those that a mesh axis runs over, the one named last changes fastest.
Arguments:
- tokens: bfloat16 [2, 4, 1024, 1088], P(None, 'shard', 'replica'), may hold values from -6 to 6
- cotangent: bfloat16 [2, 4, 1024, 1088], P(None, 'shard', 'replica'), may hold values from -6 to 6
- doc_ids: int32 [2, 4, 1024], P(None, 'shard', 'replica'), may hold values from 0 to 2, as said below
- gains: float32 [2, 2, 1088], P('section'), may hold values from 0.5 to 1.5
- biases: float32 [2, 6, 1088], P('section'), may hold values from -1.8 to 1.8
- up_bias: float32 [2, 4352], P('section'), may hold values from -1.8 to 1.8
- w_qkv: bfloat16 [2, 1088, 3264], P('section', 'shard'), may hold values from -0.1875 to 0.1875
- w_out: bfloat16 [2, 1088, 1088], P('section', 'shard'), may hold values from -1.5 to 1.5
- w_up: bfloat16 [2, 1088, 4352], P('section', 'shard'), may hold values from -0.1875 to 0.1875
- w_down: bfloat16 [2, 4352, 1088], P('section', 'shard'), may hold values from -0.09375 to 0.09375
Outputs:
- layer_out: bfloat16 [2, 2, 4, 1024, 1088], P('section', None, 'shard', 'replica')
- input_grad: bfloat16 [2, 2, 4, 1024, 1088], P('section', None, 'shard', 'replica')
- gains_grad: float32 [2, 2, 1088], P('section')
- biases_grad: float32 [2, 6, 1088], P('section')
- up_bias_grad: float32 [2, 4352], P('section')
- w_qkv_grad: float32 [2, 1088, 3264], P('section', 'shard')
- w_out_grad: float32 [2, 1088, 1088], P('section', 'shard')
- w_up_grad: float32 [2, 1088, 4352], P('section', 'shard')
- w_down_grad: float32 [2, 4352, 1088], P('section', 'shard')
The draws below stay inside these ranges and needn't reach their ends.
Inputs may be any that keep to these rules, and one draw needn't show every extreme that they name: `doc_ids`: within each sequence the numbers never fall; 0 covers the first 1 to 32 positions, 2 the last 1 to 32 positions, 1 all the others.
All inputs are finite; a program needn't handle non-finite values.
Results may differ from the reference program's by a relative error of at most 0.028.
Values may be sent and summed in bfloat16 or wider, within the bound.
A program may use at most 192 MiB of HBM per device.

```python
import jax
import jax.numpy as jnp
from jax import lax

D = 1088
H = 17
HD = 64
FF = 4352
LAYERS = 2
MICRO = 2
SEQ = 1024
BATCH = 4
TQ = 64


def draw_doc_ids(key, part):
    key = jax.random.fold_in(key, 11)
    first_key, last_key = jax.random.split(key)
    first_len = jax.random.randint(first_key, (MICRO, BATCH, 1), 1, TQ // 2 + 1)
    last_len = jax.random.randint(last_key, (MICRO, BATCH, 1), 1, TQ // 2 + 1)
    position = jnp.arange(SEQ, dtype=jnp.int32)[None, None, :]
    return (position >= first_len).astype(jnp.int32) + (position >= SEQ - last_len).astype(jnp.int32)


def level_of(own_key, shape, shards, smallest, largest):
    gain = 1.0
    for dim, shards_of in shards:
        draws = jax.random.uniform(jax.random.fold_in(jax.random.fold_in(own_key, 6), dim), (shards_of,), jnp.float32, smallest / len(shards), largest / len(shards))
        gain = gain * jnp.repeat(jnp.exp(draws), shape[dim] // shards_of).reshape((-1,) + (1,) * (len(shape) - 1 - dim))
    return gain


def scatter_about(rng, extent, width, bound, pieces=(), held_as=jnp.bfloat16):
    entries = width * jax.random.normal(rng, extent, jnp.float32)
    if pieces:
        entries = entries * level_of(rng, extent, pieces, -0.22, 0.18)
    return jnp.clip(entries, -bound, bound).astype(held_as)


def setup_inputs(seed: int = 0) -> dict:
    key_list = jax.random.split(jax.random.key(seed), 11)
    tokens = scatter_about(key_list[0], (MICRO, BATCH, SEQ, D), 1.0, 6.0, ((1, 4), (2, 16)))
    cotangent = scatter_about(key_list[1], (MICRO, BATCH, SEQ, D), 1.0, 6.0, ((1, 4), (2, 16)))
    doc_ids = draw_doc_ids(jax.random.fold_in(key_list[10], 71), 0)
    gains = jnp.clip(1.0 + 0.1 * jax.random.normal(key_list[3], (LAYERS, 2, D), jnp.float32), 0.5, 1.5)
    biases = scatter_about(key_list[4], (LAYERS, 6, D), 0.3, 1.8, ((0, 2),), jnp.float32)
    up_bias = scatter_about(key_list[5], (LAYERS, FF), 0.3, 1.8, ((0, 2),), jnp.float32)
    w_qkv = scatter_about(key_list[6], (LAYERS, D, 3 * D), D ** -0.5, 0.1875, ((0, 2), (1, 4)))
    w_out = scatter_about(key_list[7], (LAYERS, D, D), (max(D // 64, 1)) ** -0.5, 1.5, ((0, 2), (1, 4)))
    w_up = scatter_about(key_list[8], (LAYERS, D, FF), D ** -0.5, 0.1875, ((0, 2), (1, 4)))
    w_down = scatter_about(key_list[9], (LAYERS, FF, D), FF ** -0.5, 0.09375, ((0, 2), (1, 4)))
    return {"tokens": tokens, "cotangent": cotangent, "doc_ids": doc_ids, "gains": gains, "biases": biases, "up_bias": up_bias, "w_qkv": w_qkv, "w_out": w_out, "w_up": w_up, "w_down": w_down}


@jax.custom_vjp
def low(v):
    return lax.optimization_barrier(v.astype(jnp.bfloat16)).astype(jnp.float32)

@jax.custom_vjp
def low_back(v):
    return v

def low_keep(v):
    return (low(v), None)

def low_pass(kept, grad):
    return (grad,)

def back_keep(v):
    return (v, None)

def back_low(kept, grad):
    return (low(grad),)
low.defvjp(low_keep, low_pass)
low_back.defvjp(back_keep, back_low)
epsilon = 1e-05
highest = lax.Precision.HIGHEST

def matmul(left, right):
    return jnp.dot(left, right, precision=highest)

def layer_norm(values, gain_row, shift_row):
    centre = values - lax.optimization_barrier(jnp.mean(values, axis=-1, keepdims=True))
    inverse = lax.rsqrt(lax.optimization_barrier(jnp.mean(centre * centre, axis=-1, keepdims=True)) + epsilon)
    return centre * inverse * gain_row + shift_row

def one_layer(inputs, allowed, gain_rows, bias_rows, up_shift, w_qkv, w_out, w_up, w_down):
    length = inputs.shape[0]
    model_width = inputs.shape[1]
    act_first = low(layer_norm(inputs, gain_rows[0], bias_rows[0]))
    mixed_out = matmul(act_first, w_qkv)
    queries = low(low_back(mixed_out[:, :model_width] + bias_rows[1])).reshape(length, H, HD)
    key_rows = low(low_back(mixed_out[:, model_width:2 * model_width])).reshape(length, H, HD)
    values = low(low_back(mixed_out[:, 2 * model_width:] + bias_rows[2])).reshape(length, H, HD)
    scores = low_back(jnp.einsum('qhd,khd->hqk', queries, key_rows, precision=highest) * HD ** (-0.5))
    scores = jnp.where(allowed[None], scores, -1e+30)
    attention = low(jax.nn.softmax(scores, axis=-1))
    head_out = jnp.einsum('hqk,khd->qhd', attention, values, precision=highest).reshape(length, model_width)
    attended = low(low_back(head_out))
    residual = inputs + low_back(matmul(attended, w_out) + bias_rows[3])
    act_second = low(layer_norm(residual, gain_rows[1], bias_rows[4]))
    hidden_pre = low_back(matmul(act_second, w_up) + up_shift)
    hidden = low(jax.nn.gelu(hidden_pre, approximate=True))
    return residual + low_back(matmul(hidden, w_down) + bias_rows[5])

def forward(inputs, probe_in, allowed, gains, biases, up_bias, w_qkv, w_out, w_up, w_down):
    first_out = one_layer(inputs, allowed, gains[0], biases[0], up_bias[0], w_qkv[0], w_out[0], w_up[0], w_down[0])
    second_in = low(low_back(first_out)) + probe_in
    second_out = one_layer(second_in, allowed, gains[1], biases[1], up_bias[1], w_qkv[1], w_out[1], w_up[1], w_down[1])
    return (first_out, second_out)

def reference(tokens, cotangent, doc_ids, gains, biases, up_bias, w_qkv, w_out, w_up, w_down):
    params = tuple((member.astype(jnp.float32) for member in (gains, biases, up_bias, w_qkv, w_out, w_up, w_down)))
    seq_len = tokens.shape[2]
    model_width = tokens.shape[3]
    position = jnp.arange(seq_len, dtype=jnp.int32)
    causal = position[None, :] <= position[:, None]
    flat_tokens = tokens.reshape(-1, seq_len, model_width).astype(jnp.float32)
    flat_cot = cotangent.reshape(-1, seq_len, model_width).astype(jnp.float32)
    flat_docs = doc_ids.reshape(-1, seq_len)

    def one_sequence(totals, slices):
        inputs, grad_out, seq_docs = slices
        allowed = causal & (seq_docs[:, None] == seq_docs[None, :])
        zero_probe = jnp.zeros_like(inputs)

        def apply_all(inputs_in, probe_in, *weights_in):
            return forward(inputs_in, probe_in, allowed, *weights_in)
        results, pullback = jax.vjp(apply_all, inputs, zero_probe, *params)
        gradients = pullback((jnp.zeros_like(results[0]), grad_out))
        totals = tuple((running + update for running, update in zip(totals, gradients[2:])))
        emitted = (results[0].astype(jnp.bfloat16), results[1].astype(jnp.bfloat16), gradients[0].astype(jnp.bfloat16), gradients[1].astype(jnp.bfloat16))
        return (totals, emitted)
    zero_grads = tuple((jnp.zeros(member.shape, jnp.float32) for member in params))
    totals, emitted = lax.scan(one_sequence, zero_grads, (flat_tokens, flat_cot, flat_docs))
    layer_out = jnp.stack([emitted[0], emitted[1]]).reshape((2,) + tokens.shape)
    input_grad = jnp.stack([emitted[2], emitted[3]]).reshape((2,) + tokens.shape)
    return (layer_out, input_grad, totals[0], totals[1], totals[2], totals[3], totals[4], totals[5], totals[6])
```

```python
import functools

import jax
import jax.numpy as jnp
from jax import lax
from jax.experimental import pallas as pl
from jax.experimental.pallas import tpu as pltpu
from jax.sharding import PartitionSpec as P

MESH = pl.DeviceIdType.MESH
H = 17
HD = 64
TQ = 64
SEQ = 1024
NR = 16
D = 1088
FF = 4352
SCALE = HD ** (-0.5)
epsilon = 1e-05
masked_score = -1e30
BQ = 256
PIECE = 896
RED_ROWS = 288
HALF = 144


def layer_norm(values, gain_row, shift_row):
    centre = values - jnp.mean(values, axis=-1, keepdims=True)
    inverse = lax.rsqrt(jnp.mean(centre * centre, axis=-1, keepdims=True) + epsilon)
    normed = centre * inverse
    return (normed * gain_row + shift_row, normed, inverse)


def norm_back(grad_normed_out, normed, inverse, gain_row):
    scaled = grad_normed_out * gain_row
    middle = jnp.mean(scaled, axis=-1, keepdims=True)
    slope = jnp.mean(scaled * normed, axis=-1, keepdims=True)
    return inverse * (scaled - middle - normed * slope)


def times(left, right):
    return jnp.dot(left, right, preferred_element_type=jnp.float32)


def times_transposed(left, right):
    return lax.dot_general(
        left, right, (((1,), (1,)), ((), ())), preferred_element_type=jnp.float32
    )


def outer_sum(left, right):
    return lax.dot_general(
        left, right, (((0,), (0,)), ((), ())), preferred_element_type=jnp.float32
    )


def y_peer(me, d):
    return (me // 4) * 4 + lax.rem(lax.rem(me, 4) + d, 4)


def z_peer(me, d):
    return lax.rem(me + 4 * d, NR)


def any_peer(me, d):
    return lax.rem(me // 4 + d // 4, 4) * 4 + lax.rem(lax.rem(me, 4) + d % 4, 4)


def remote(src, dst, send, recv, where):
    return pltpu.make_async_remote_copy(
        src_ref=src,
        dst_ref=dst,
        send_sem=send,
        recv_sem=recv,
        device_id=where,
        device_id_type=MESH,
    )


def greet(places):
    barrier = pltpu.get_barrier_semaphore()
    for where in places:
        pl.semaphore_signal(barrier, inc=1, device_id=where, device_id_type=MESH)
    pl.semaphore_wait(barrier, len(places))


def swap_kernel(x, o, send, recv, local):
    me = lax.axis_index("replica")
    greet([{"replica": any_peer(me, d)} for d in range(1, NR)])
    copies = []
    for d in range(1, NR):
        to = any_peer(me, d)
        copy = remote(x.at[to], o.at[me], send.at[d], recv.at[d], {"replica": to})
        copy.start()
        copies.append(copy)
    own = pltpu.make_async_copy(x.at[me], o.at[me], local)
    own.start()
    own.wait()
    for copy in copies:
        copy.wait()


def swap(x, collective_id):
    return pl.pallas_call(
        swap_kernel,
        out_shape=jax.ShapeDtypeStruct(x.shape, x.dtype),
        in_specs=[pl.BlockSpec(memory_space=pl.ANY)],
        out_specs=pl.BlockSpec(memory_space=pl.ANY),
        scratch_shapes=[
            pltpu.SemaphoreType.DMA((NR,)),
            pltpu.SemaphoreType.DMA((NR,)),
            pltpu.SemaphoreType.DMA,
        ],
        compiler_params=pltpu.CompilerParams(collective_id=collective_id, has_side_effects=True),
        name="swap",
    )(x)


W_SHAPES = ((272, 3264), (272, 1088), (272, 4352), (1088, 1088))
W_CUTS = (1664, 512, 2176, 512)


def weights_kernel(*refs):
    ins, outs = refs[:4], refs[4:8]
    (own_s, own_r, local, xp_s, xp_r, xd_s, xd_r, a1_s, a1_r, b1_s, b1_r, a2_s, a2_r, b2_s, b2_r, f_s, f_r) = refs[8:]
    j = lax.axis_index("shard")
    me = lax.axis_index("replica")
    z, y = me // 4, lax.rem(me, 4)
    xj = lax.rem(j + 2, 4)
    cj = j + 1 - 2 * lax.rem(j, 2)
    x_place, c_place = {"shard": xj}, {"shard": cj}
    y_places = [{"replica": y_peer(me, d)} for d in (1, 2, 3)]
    z_places = [{"replica": z_peer(me, d)} for d in (1, 2, 3)]
    greet([x_place, c_place] + y_places + z_places)

    def rows(start, count):
        return pl.ds(pl.multiple_of(start, 16), count)

    waits = []
    x_pieces, x_directs = [], []
    for a, (r, n) in enumerate(W_SHAPES):
        u = r // 17
        piece = remote(ins[a].at[rows(me * u, u)], outs[a].at[rows(j * r + me * u, u)], xp_s.at[a], xp_r.at[a], x_place)
        piece.start()
        x_pieces.append(piece)
    for a, (r, n) in enumerate(W_SHAPES):
        u = r // 17
        direct = remote(ins[a].at[rows(16 * u, u)], outs[a].at[rows(j * r + 16 * u, u)], xd_s.at[a], xd_r.at[a], x_place)
        direct.start()
        x_directs.append(direct)
    for a, (r, n) in enumerate(W_SHAPES):
        copy = remote(ins[a], outs[a].at[rows(j * r, r)], own_s.at[a], own_r.at[a], c_place)
        copy.start()
        waits.append(copy)
        copy = pltpu.make_async_copy(ins[a], outs[a].at[rows(j * r, r)], local.at[a])
        copy.start()
        waits.append(copy)
    firsts = []
    for a, (r, n) in enumerate(W_SHAPES):
        u, cut = r // 17, W_CUTS[a]
        x_pieces[a].wait()
        here = rows(xj * r + me * u, u)
        part_a = outs[a].at[here, pl.ds(0, cut)]
        part_b = outs[a].at[here, pl.ds(cut, n - cut)]
        group = []
        for i in range(3):
            group.append(remote(part_a, part_a, a1_s.at[a, i], a1_r.at[a, i], y_places[i]))
            group.append(remote(part_b, part_b, b1_s.at[a, i], b1_r.at[a, i], z_places[i]))
        for copy in group:
            copy.start()
        firsts.append(group)
    seconds = []
    for a, (r, n) in enumerate(W_SHAPES):
        u, cut = r // 17, W_CUTS[a]
        for copy in firsts[a]:
            copy.wait()
        part_a = outs[a].at[rows(xj * r + z * (4 * u), 4 * u), pl.ds(0, cut)]
        group = []
        for i in range(3):
            group.append(remote(part_a, part_a, a2_s.at[a, i], a2_r.at[a, i], z_places[i]))
            for k in range(4):
                part_b = outs[a].at[rows(xj * r + (4 * k + y) * u, u), pl.ds(cut, n - cut)]
                group.append(remote(part_b, part_b, b2_s.at[a, i, k], b2_r.at[a, i, k], y_places[i]))
        for copy in group:
            copy.start()
        seconds.append(group)
    for a, (r, n) in enumerate(W_SHAPES):
        for copy in seconds[a]:
            copy.wait()
        x_directs[a].wait()
        whole = outs[a].at[rows(xj * r, r)]
        copy = remote(whole, whole, f_s.at[a], f_r.at[a], c_place)
        copy.start()
        waits.append(copy)
    for copy in waits:
        copy.wait()


def gather_weights(weights):
    dma = pltpu.SemaphoreType.DMA
    return pl.pallas_call(
        weights_kernel,
        out_shape=[jax.ShapeDtypeStruct((4 * r, n), jnp.bfloat16) for r, n in W_SHAPES],
        in_specs=[pl.BlockSpec(memory_space=pl.ANY)] * 4,
        out_specs=[pl.BlockSpec(memory_space=pl.ANY)] * 4,
        scratch_shapes=[dma((4,))] * 7 + [dma((4, 3))] * 6 + [dma((4, 3, 4))] * 2 + [dma((4,))] * 2,
        compiler_params=pltpu.CompilerParams(collective_id=1, has_side_effects=True),
        name="gather_weights",
    )(*weights)


def total_kernel(
    g, out, own_a, own_b, buf_a, buf_b, sum_a, sum_b, got_a, got_b,
    loc, r1a_s, r1a_r, r1b_s, r1b_r, r2a_s, r2a_r, r2b_s, r2b_r, g1a_s, g1a_r, g1b_s, g1b_r, g2a_s, g2a_r, g2b_s, g2b_r, fin,
):
    me = lax.axis_index("replica")
    z, y = me // 4, lax.rem(me, 4)
    y_ids = [y_peer(me, d) for d in (1, 2, 3)]
    z_ids = [z_peer(me, d) for d in (1, 2, 3)]
    y_places = [{"replica": p} for p in y_ids]
    z_places = [{"replica": p} for p in z_ids]
    greet(y_places + z_places)
    rows_a, rows_b = pl.ds(0, HALF), pl.ds(HALF, HALF)

    def columns(piece, count=1):
        return pl.ds(pl.multiple_of(piece * PIECE, 128), count * PIECE)

    def start(copies):
        for copy in copies:
            copy.start()

    def finish(copies):
        for copy in copies:
            copy.wait()

    locals_ = [
        pltpu.make_async_copy(g.at[rows_a, columns(4 * k + y)], own_a.at[k], loc.at[k])
        for k in range(4)
    ] + [pltpu.make_async_copy(g.at[rows_b, columns(4 * z, 4)], own_b, loc.at[4])]
    start(locals_)
    one_a, one_b = [], []
    for i in range(3):
        ty, tz = lax.rem(y + 1 + i, 4), lax.rem(z + 1 + i, 4)
        one_b.append(remote(g.at[rows_b, columns(4 * tz, 4)], buf_b.at[i], r1b_s.at[i], r1b_r.at[i], z_places[i]))
        for k in range(4):
            one_a.append(remote(g.at[rows_a, columns(4 * k + ty)], buf_a.at[i, k], r1a_s.at[i, k], r1a_r.at[i, k], y_places[i]))
    start(one_a)
    start(one_b)
    finish(locals_)
    finish(one_a)
    f32 = jnp.float32
    for k in range(4):
        total = own_a[k].astype(f32) + buf_a[0, k].astype(f32)
        total = total + buf_a[1, k].astype(f32) + buf_a[2, k].astype(f32)
        sum_a[k] = total.astype(jnp.bfloat16)
    two_a = []
    for i in range(3):
        tz = lax.rem(z + 1 + i, 4)
        two_a.append(remote(sum_a.at[tz], got_a.at[i], r2a_s.at[i], r2a_r.at[i], z_places[i]))
    start(two_a)
    finish(one_b)
    for k in range(4):
        part = pl.ds(k * PIECE, PIECE)
        total = own_b[:, part].astype(f32) + buf_b[0, :, part].astype(f32)
        total = total + buf_b[1, :, part].astype(f32) + buf_b[2, :, part].astype(f32)
        sum_b[k] = total.astype(jnp.bfloat16)
    two_b = []
    for i in range(3):
        ty = lax.rem(y + 1 + i, 4)
        two_b.append(remote(sum_b.at[ty], got_b.at[i], r2b_s.at[i], r2b_r.at[i], y_places[i]))
    start(two_b)
    here = columns(me)
    finish(two_a)
    total = sum_a[z].astype(f32) + got_a[0].astype(f32) + got_a[1].astype(f32) + got_a[2].astype(f32)
    own_a[0] = total.astype(jnp.bfloat16)
    back_a = [
        remote(own_a.at[0], out.at[rows_a, here], g1a_s.at[i], g1a_r.at[i], z_places[i]) for i in range(3)
    ]
    start(back_a)
    last_a = pltpu.make_async_copy(own_a.at[0], out.at[rows_a, here], fin.at[0])
    last_a.start()
    finish(two_b)
    total = sum_b[y].astype(f32) + got_b[0].astype(f32) + got_b[1].astype(f32) + got_b[2].astype(f32)
    own_a[1] = total.astype(jnp.bfloat16)
    back_b = [
        remote(own_a.at[1], out.at[rows_b, here], g1b_s.at[i], g1b_r.at[i], y_places[i]) for i in range(3)
    ]
    start(back_b)
    last_b = pltpu.make_async_copy(own_a.at[1], out.at[rows_b, here], fin.at[1])
    last_b.start()
    last_a.wait()
    finish(back_a)
    end_a, end_b = [], []
    for i in range(3):
        for k in range(4):
            part = out.at[rows_a, columns(4 * k + y)]
            end_a.append(remote(part, part, g2a_s.at[i, k], g2a_r.at[i, k], y_places[i]))
    start(end_a)
    last_b.wait()
    finish(back_b)
    for i in range(3):
        part = out.at[rows_b, columns(4 * z, 4)]
        end_b.append(remote(part, part, g2b_s.at[i], g2b_r.at[i], z_places[i]))
    start(end_b)
    finish(end_a)
    finish(end_b)


def total_over_replicas(g):
    dma = pltpu.SemaphoreType.DMA
    bf16 = jnp.bfloat16
    return pl.pallas_call(
        total_kernel,
        out_shape=jax.ShapeDtypeStruct(g.shape, g.dtype),
        in_specs=[pl.BlockSpec(memory_space=pl.ANY)],
        out_specs=pl.BlockSpec(memory_space=pl.ANY),
        scratch_shapes=[
            pltpu.VMEM((4, HALF, PIECE), bf16),
            pltpu.VMEM((HALF, 4 * PIECE), bf16),
            pltpu.VMEM((3, 4, HALF, PIECE), bf16),
            pltpu.VMEM((3, HALF, 4 * PIECE), bf16),
            pltpu.VMEM((4, HALF, PIECE), bf16),
            pltpu.VMEM((4, HALF, PIECE), bf16),
            pltpu.VMEM((3, HALF, PIECE), bf16),
            pltpu.VMEM((3, HALF, PIECE), bf16),
            dma((5,)),
            dma((3, 4)), dma((3, 4)), dma((3,)), dma((3,)),
            dma((3,)), dma((3,)), dma((3,)), dma((3,)),
            dma((3,)), dma((3,)), dma((3,)), dma((3,)),
            dma((3, 4)), dma((3, 4)), dma((3,)), dma((3,)),
            dma((2,)),
        ],
        compiler_params=pltpu.CompilerParams(
            collective_id=2, has_side_effects=True, vmem_limit_bytes=48 * 1024 * 1024
        ),
        name="total_over_replicas",
    )(g)


def lane_mask(shape, micro):
    lane = lax.broadcasted_iota(jnp.int32, shape, len(shape) - 1)
    return (lane >= HD) if micro else (lane < HD)


def allowed_block(n0, n2, first_query, queries, keys):
    i = lax.broadcasted_iota(jnp.int32, (queries, keys), 0) + first_query
    j = lax.broadcasted_iota(jnp.int32, (queries, keys), 1)
    row = lax.broadcasted_iota(jnp.int32, (queries, 1), 0) + first_query
    start = jnp.where(row >= n2, n2, jnp.where(row >= n0, n0, 0))
    return (j <= i) & (j >= start)


def scores_of(q, k, micro, allowed):
    zero = jnp.zeros((), jnp.bfloat16)
    q = jnp.where(lane_mask(q.shape, micro), q, zero)
    s = lax.dot_general(q, k, (((1,), (1,)), ((), ())), preferred_element_type=jnp.float32)
    return jnp.where(allowed, s * SCALE, masked_score)


def take(x, entry, start, count):
    return x[pl.ds(start, count), entry].reshape(count * TQ, 2 * HD)


def forward_kernel(bounds, x, q16, o, o16, lse, lse16):
    zero = jnp.zeros((), jnp.bfloat16)
    me = lax.axis_index("replica")

    def attend(q, k, v, micro, first_query):
        allowed = allowed_block(bounds[micro], bounds[2 + micro], first_query, q.shape[0], k.shape[0])
        s = scores_of(q, k, micro, allowed)
        largest = jnp.max(s, axis=-1, keepdims=True)
        e = jnp.exp(s - largest)
        summed = jnp.sum(e, axis=-1, keepdims=True)
        p = (e * (1.0 / summed)).astype(jnp.bfloat16)
        v = jnp.where(lane_mask(v.shape, micro), v, zero)
        return times(p, v), largest + jnp.log(summed)

    per = BQ // TQ
    for b in range(SEQ // BQ):
        count = (b + 1) * per
        q = take(x, 0, b * per, per)
        k = take(x, 1, 0, count)
        v = take(x, 2, 0, count)
        o0, l0 = attend(q, k, v, 0, b * BQ)
        o1, l1 = attend(q, k, v, 1, b * BQ)
        o[pl.ds(b * per, per)] = (o0 + o1).astype(jnp.bfloat16).reshape(per, TQ, 2 * HD)
        lse[pl.ds(b * BQ, BQ)] = jnp.where(lane_mask((BQ, 2 * HD), 0), l0, l1)
    q = q16[...]
    k = take(x, 3, 0, NR)
    v = take(x, 4, 0, NR)
    o0, l0 = attend(q, k, v, 0, me * TQ)
    o1, l1 = attend(q, k, v, 1, me * TQ)
    o16[...] = (o0 + o1).astype(jnp.bfloat16)
    lse16[...] = jnp.where(lane_mask((TQ, 2 * HD), 0), l0, l1)


def vmem_specs(count):
    return [pl.BlockSpec(memory_space=pltpu.VMEM)] * count


def attention_forward(bounds, x, q16):
    f32, bf16 = jnp.float32, jnp.bfloat16
    return pl.pallas_call(
        forward_kernel,
        out_shape=[
            jax.ShapeDtypeStruct((NR, TQ, 2 * HD), bf16),
            jax.ShapeDtypeStruct((TQ, 2 * HD), bf16),
            jax.ShapeDtypeStruct((SEQ, 2 * HD), f32),
            jax.ShapeDtypeStruct((TQ, 2 * HD), f32),
        ],
        in_specs=[pl.BlockSpec(memory_space=pltpu.SMEM)] + vmem_specs(2),
        out_specs=vmem_specs(4),
        compiler_params=pltpu.CompilerParams(vmem_limit_bytes=48 * 1024 * 1024),
        name="attention_forward",
    )(bounds, x, q16)


def backward_kernel(bounds, x, q16, lse, lse16, do, do16, dx, dq16, dk, dv):
    zero = jnp.zeros((), jnp.bfloat16)
    me = lax.axis_index("replica")
    bf16 = jnp.bfloat16

    def pull(q, k, v, grad, logs, micro, first_query):
        allowed = allowed_block(bounds[micro], bounds[2 + micro], first_query, q.shape[0], k.shape[0])
        s = scores_of(q, k, micro, allowed)
        soft = jnp.exp(s - logs[:, micro * HD : micro * HD + 1])
        grad = jnp.where(lane_mask(grad.shape, micro), grad, zero)
        dp = times_transposed(grad, v)
        along = jnp.sum(soft * dp, axis=-1, keepdims=True)
        ds = (soft * (dp - along)).astype(bf16)
        q = jnp.where(lane_mask(q.shape, micro), q, zero)
        k = jnp.where(lane_mask(k.shape, micro), k, zero)
        return times(ds, k), outer_sum(ds, q), outer_sum(soft.astype(bf16), grad)

    per = BQ // TQ
    for b in reversed(range(SEQ // BQ)):
        count = (b + 1) * per
        q = take(x, 0, b * per, per)
        k = take(x, 1, 0, count)
        v = take(x, 2, 0, count)
        grad = do[pl.ds(b * per, per)].reshape(BQ, 2 * HD)
        logs = lse[pl.ds(b * BQ, BQ)]
        q0, k0, v0 = pull(q, k, v, grad, logs, 0, b * BQ)
        q1, k1, v1 = pull(q, k, v, grad, logs, 1, b * BQ)
        dx[pl.ds(b * per, per), 0] = ((q0 + q1) * SCALE).astype(bf16).reshape(per, TQ, 2 * HD)
        keys = pl.ds(0, (b + 1) * BQ)
        if b == SEQ // BQ - 1:
            dk[keys] = k0 + k1
            dv[keys] = v0 + v1
        else:
            dk[keys] += k0 + k1
            dv[keys] += v0 + v1
    dx[:, 1] = (dk[...] * SCALE).astype(bf16).reshape(NR, TQ, 2 * HD)
    dx[:, 2] = dv[...].astype(bf16).reshape(NR, TQ, 2 * HD)
    q = q16[...]
    k = take(x, 3, 0, NR)
    v = take(x, 4, 0, NR)
    q0, k0, v0 = pull(q, k, v, do16[...], lse16[...], 0, me * TQ)
    q1, k1, v1 = pull(q, k, v, do16[...], lse16[...], 1, me * TQ)
    dq16[...] = ((q0 + q1) * SCALE).astype(bf16)
    dx[:, 3] = ((k0 + k1) * SCALE).astype(bf16).reshape(NR, TQ, 2 * HD)
    dx[:, 4] = (v0 + v1).astype(bf16).reshape(NR, TQ, 2 * HD)


def attention_backward(bounds, x, q16, lse, lse16, do, do16):
    f32, bf16 = jnp.float32, jnp.bfloat16
    return pl.pallas_call(
        backward_kernel,
        out_shape=[
            jax.ShapeDtypeStruct((NR, 5, TQ, 2 * HD), bf16),
            jax.ShapeDtypeStruct((TQ, 2 * HD), bf16),
        ],
        in_specs=[pl.BlockSpec(memory_space=pltpu.SMEM)] + vmem_specs(6),
        out_specs=vmem_specs(2),
        scratch_shapes=[pltpu.VMEM((SEQ, 2 * HD), f32), pltpu.VMEM((SEQ, 2 * HD), f32)],
        compiler_params=pltpu.CompilerParams(vmem_limit_bytes=48 * 1024 * 1024),
        name="attention_backward",
    )(bounds, x, q16, lse, lse16, do, do16)


def heads_first(matrix):
    n = matrix.shape[1] // HD
    return matrix.reshape(2, TQ, n, HD).transpose(2, 1, 0, 3).reshape(n, TQ, 2 * HD)


def heads_last(blocks):
    n = blocks.shape[0]
    return blocks.reshape(n, TQ, 2, HD).transpose(2, 1, 0, 3).reshape(2 * TQ, n * HD)


def layer_forward(inputs, bounds, gain_rows, bias_rows, up_shift, weights):
    w_qkv, w_out, w_up, w_down = weights
    bf16 = jnp.bfloat16
    normed_in, normed_first, inverse_first = layer_norm(inputs, gain_rows[0], bias_rows[0])
    act_first = normed_in.astype(bf16)
    mixed_out = times(act_first, w_qkv)
    shift = jnp.concatenate([bias_rows[1], jnp.zeros_like(bias_rows[1]), bias_rows[2]], axis=1)
    mixed = heads_first((mixed_out + shift).astype(bf16)).reshape(3, H, TQ, 2 * HD)
    q16 = mixed[0, H - 1]
    message = jnp.concatenate(
        [
            mixed[:, : H - 1].transpose(1, 0, 2, 3),
            jnp.broadcast_to(mixed[None, 1:, H - 1], (NR, 2, TQ, 2 * HD)),
        ],
        axis=1,
    )
    whole = swap(message.reshape(NR, 5 * TQ, 2 * HD), 3).reshape(NR, 5, TQ, 2 * HD)
    o, o16, lse, lse16 = attention_forward(bounds, whole, q16)
    o = swap(o, 4)
    attended = heads_last(jnp.concatenate([o, o16[None]], axis=0))
    residual = inputs + times(attended, w_out) + bias_rows[3]
    normed_mid, normed_second, inverse_second = layer_norm(residual, gain_rows[1], bias_rows[4])
    act_second = normed_mid.astype(bf16)
    hidden_pre = times(act_second, w_up) + up_shift
    hidden = jax.nn.gelu(hidden_pre, approximate=True).astype(bf16)
    result = residual + times(hidden, w_down) + bias_rows[5]
    kept = {
        "normed_first": normed_first,
        "inverse_first": inverse_first,
        "act_first": act_first,
        "whole": whole,
        "q16": q16,
        "lse": lse,
        "lse16": lse16,
        "attended": attended,
        "normed_second": normed_second,
        "inverse_second": inverse_second,
        "act_second": act_second,
        "hidden_pre": hidden_pre,
        "hidden": hidden,
    }
    return (result, kept)


def layer_backward(grad_out, kept, bounds, gain_rows, weights):
    w_qkv, w_out, w_up, w_down = weights
    bf16 = jnp.bfloat16
    grad_down = grad_out.astype(bf16)
    grad_hidden = times_transposed(grad_down, w_down)
    gelu_value, gelu_pull = jax.vjp(
        functools.partial(jax.nn.gelu, approximate=True), kept["hidden_pre"]
    )
    grad_pre = gelu_pull(grad_hidden)[0].astype(bf16)
    grad_second = times_transposed(grad_pre, w_up)
    grad_resid = grad_out + norm_back(
        grad_second, kept["normed_second"], kept["inverse_second"], gain_rows[1]
    )
    grad_branch = grad_resid.astype(bf16)
    grad_heads = heads_first(times_transposed(grad_branch, w_out).astype(bf16))
    do = swap(grad_heads[: H - 1], 4)
    dx, dq16 = attention_backward(
        bounds, kept["whole"], kept["q16"], kept["lse"], kept["lse16"], do, grad_heads[H - 1]
    )
    back = swap(dx.reshape(NR, 5 * TQ, 2 * HD), 3).reshape(NR, 5, TQ, 2 * HD)
    last = jnp.sum(back[:, 3:].astype(jnp.float32), axis=0).astype(bf16)
    last = jnp.concatenate([dq16[None], last], axis=0)
    parts = jnp.concatenate([back[:, :3].transpose(1, 0, 2, 3), last[:, None]], axis=1)
    grad_mixed = heads_last(parts.reshape(3 * H, TQ, 2 * HD))
    grad_first = times_transposed(grad_mixed, w_qkv)
    grad_in = grad_resid + norm_back(
        grad_first, kept["normed_first"], kept["inverse_first"], gain_rows[0]
    )
    record = {
        "grad_down": grad_down,
        "grad_pre": grad_pre,
        "grad_branch": grad_branch,
        "grad_mixed": grad_mixed,
        "grad_first": grad_first,
        "grad_second": grad_second,
    }
    return (grad_in, record)


X_ROUTE = [(j, j ^ 2) for j in range(4)]
C_ROUTE = [(j, j ^ 1) for j in range(4)]


def everyone(value):
    pair = jnp.stack([value, lax.ppermute(value, "shard", X_ROUTE)])
    other = lax.ppermute(pair, "shard", C_ROUTE)
    return jnp.concatenate([pair, other]).reshape(4 * value.shape[0], value.shape[1])


def own_columns(value):
    rows, width = value.shape
    cut = value.reshape(rows, 4, width // 4).transpose(1, 0, 2).reshape(2, 2, rows, width // 4)
    j = lax.axis_index("shard")
    upper, odd = j >= 2, lax.rem(j, 2) == 1
    mine = jnp.where(upper, cut[1], cut[0])
    theirs = lax.ppermute(jnp.where(upper, cut[0], cut[1]), "shard", X_ROUTE)
    both = jnp.stack([mine, theirs])
    keep = jnp.where(odd, both[:, 1], both[:, 0])
    give = jnp.where(odd, both[:, 0], both[:, 1])
    got = lax.ppermute(give, "shard", C_ROUTE)
    return jnp.concatenate([keep, got]).reshape(4 * rows, width // 4)


def small_row(kept, record):
    def column_sum(value):
        return jnp.sum(value.astype(jnp.float32), axis=0, keepdims=True)

    mixed = record["grad_mixed"]
    row = jnp.concatenate(
        [
            column_sum(record["grad_first"] * kept["normed_first"]),
            column_sum(record["grad_second"] * kept["normed_second"]),
            column_sum(record["grad_first"]),
            column_sum(mixed[:, :D]),
            column_sum(mixed[:, 2 * D :]),
            column_sum(record["grad_branch"]),
            column_sum(record["grad_second"]),
            column_sum(record["grad_down"]),
            column_sum(record["grad_pre"]),
        ],
        axis=1,
    )
    row = row + lax.ppermute(row, "shard", X_ROUTE)
    return row + lax.ppermute(row, "shard", C_ROUTE)


def shards(tokens, cotangent, doc_ids, gains, biases, up_bias, w_qkv, w_out, w_up, w_down):
    f32, bf16 = jnp.float32, jnp.bfloat16
    is_first = lax.axis_index("section") == 0
    weights = gather_weights((w_qkv[0], w_out[0], w_up[0], w_down[0]))
    docs = lax.all_gather(doc_ids[:, 0], "replica", axis=1, tiled=True)
    n0 = jnp.sum((docs == 0).astype(jnp.int32), axis=1)
    n2 = SEQ - jnp.sum((docs == 2).astype(jnp.int32), axis=1)
    bounds = jnp.concatenate([n0, n2])
    gain_rows = [gains[0, i : i + 1] for i in range(2)]
    bias_rows = [biases[0, i : i + 1] for i in range(6)]
    own_in = tokens.reshape(2 * TQ, D)
    own_cot = cotangent.reshape(2 * TQ, D)
    result, _ = layer_forward(own_in.astype(f32), bounds, gain_rows, bias_rows, up_bias, weights)
    inbox = lax.ppermute(result.astype(bf16), "section", [(0, 1)])
    inputs = jnp.where(is_first, own_in, inbox)
    result, kept = layer_forward(inputs.astype(f32), bounds, gain_rows, bias_rows, up_bias, weights)
    layer_out = result.astype(bf16)
    lefts = [own_columns(kept[k]) for k in ("act_first", "attended", "act_second", "hidden")]
    grad_in, _ = layer_backward(own_cot.astype(f32), kept, bounds, gain_rows, weights)
    inbox = lax.ppermute(grad_in.astype(bf16), "section", [(1, 0)])
    grad_out = jnp.where(is_first, inbox, own_cot)
    grad_in, record = layer_backward(grad_out.astype(f32), kept, bounds, gain_rows, weights)
    rights = [everyone(record[k]) for k in ("grad_mixed", "grad_branch", "grad_pre", "grad_down")]
    terms = [outer_sum(a, b).astype(bf16) for a, b in zip(lefts, rights)]
    down = terms[3].reshape(4, 272, D).transpose(1, 0, 2).reshape(272, 4 * D)
    block = jnp.concatenate([terms[0], terms[1], terms[2], down], axis=1)
    width = block.shape[1]
    row = small_row(kept, record).astype(bf16)
    block = jnp.concatenate([block, row, jnp.zeros((RED_ROWS - 273, width), bf16)], axis=0)
    block = jnp.pad(block, ((0, 0), (0, NR * PIECE - width)))
    summed = total_over_replicas(block)
    grads = summed[:272].astype(f32)
    small = summed[272].astype(f32)
    return (
        layer_out.reshape(1, 2, 1, TQ, D),
        grad_in.astype(bf16).reshape(1, 2, 1, TQ, D),
        small[: 2 * D].reshape(1, 2, D),
        small[2 * D : 8 * D].reshape(1, 6, D),
        small[8 * D : 8 * D + FF].reshape(1, FF),
        grads[None, :, : 3 * D],
        grads[None, :, 3 * D : 4 * D],
        grads[None, :, 4 * D : 8 * D],
        grads[:, 8 * D : 12 * D].reshape(272, 4, D).transpose(1, 0, 2).reshape(1, 1088, D),
    )


def solution(mesh):
    placed = (
        P(None, "shard", "replica", None),
        P(None, "shard", "replica", None),
        P(None, "shard", "replica"),
        P("section", None, None),
        P("section", None, None),
        P("section", None),
        P("section", "shard", None),
        P("section", "shard", None),
        P("section", "shard", None),
        P("section", "shard", None),
    )
    return jax.shard_map(
        shards,
        mesh=mesh,
        in_specs=placed,
        out_specs=(
            P("section", None, "shard", "replica", None),
            P("section", None, "shard", "replica", None),
            P("section", None, None),
            P("section", None, None),
            P("section", None),
            P("section", "shard", None),
            P("section", "shard", None),
            P("section", "shard", None),
            P("section", "shard", None),
        ),
        check_vma=False,
    )
```

```python
import functools

import jax
import jax.numpy as jnp
from jax import lax
from jax.experimental import pallas as pl
from jax.experimental.pallas import tpu as pltpu
from jax.sharding import PartitionSpec as P

MESH = pl.DeviceIdType.MESH
H = 17
HD = 64
TQ = 64
SEQ = 1024
NR = 16
D = 1088
FF = 4352
SCALE = HD ** (-0.5)
epsilon = 1e-05
masked_score = -1e30
BQ = 256
PIECE = 896
VMEM_BYTES = 58 * 1024 * 1024
RED_ROWS = 288
HALF = 144


def layer_norm(values, gain_row, shift_row):
    centre = values - jnp.mean(values, axis=-1, keepdims=True)
    inverse = lax.rsqrt(jnp.mean(centre * centre, axis=-1, keepdims=True) + epsilon)
    normed = centre * inverse
    return (normed * gain_row + shift_row, normed, inverse)


def norm_back(grad_normed_out, normed, inverse, gain_row):
    scaled = grad_normed_out * gain_row
    middle = jnp.mean(scaled, axis=-1, keepdims=True)
    slope = jnp.mean(scaled * normed, axis=-1, keepdims=True)
    return inverse * (scaled - middle - normed * slope)


def times(left, right):
    return jnp.dot(left, right, preferred_element_type=jnp.float32)


def times_transposed(left, right):
    return lax.dot_general(
        left, right, (((1,), (1,)), ((), ())), preferred_element_type=jnp.float32
    )


def outer_sum(left, right):
    return lax.dot_general(
        left, right, (((0,), (0,)), ((), ())), preferred_element_type=jnp.float32
    )


def y_peer(me, d):
    return (me // 4) * 4 + lax.rem(lax.rem(me, 4) + d, 4)


def z_peer(me, d):
    return lax.rem(me + 4 * d, NR)


def any_peer(me, d):
    return lax.rem(me // 4 + d // 4, 4) * 4 + lax.rem(lax.rem(me, 4) + d % 4, 4)


def remote(src, dst, send, recv, where):
    return pltpu.make_async_remote_copy(
        src_ref=src,
        dst_ref=dst,
        send_sem=send,
        recv_sem=recv,
        device_id=where,
        device_id_type=MESH,
    )


def cost(microseconds):
    return pl.CostEstimate(flops=0, bytes_accessed=int(microseconds * 3.5e6), transcendentals=0)


def greet(places):
    barrier = pltpu.get_barrier_semaphore()
    for where in places:
        pl.semaphore_signal(barrier, inc=1, device_id=where, device_id_type=MESH)
    pl.semaphore_wait(barrier, len(places))


def swap_kernel(x, o, send, recv, local):
    me = lax.axis_index("replica")
    greet([{"replica": any_peer(me, d)} for d in range(1, NR)])
    copies = []
    for d in range(1, NR):
        to = any_peer(me, d)
        copy = remote(x.at[to], o.at[me], send.at[d], recv.at[d], {"replica": to})
        copy.start()
        copies.append(copy)
    own = pltpu.make_async_copy(x.at[me], o.at[me], local)
    own.start()
    own.wait()
    for copy in copies:
        copy.wait()


def swap(x, collective_id):
    return pl.pallas_call(
        swap_kernel,
        out_shape=jax.ShapeDtypeStruct(x.shape, x.dtype),
        in_specs=[pl.BlockSpec(memory_space=pl.ANY)],
        out_specs=pl.BlockSpec(memory_space=pl.ANY),
        scratch_shapes=[
            pltpu.SemaphoreType.DMA((NR,)),
            pltpu.SemaphoreType.DMA((NR,)),
            pltpu.SemaphoreType.DMA,
        ],
        compiler_params=pltpu.CompilerParams(
            collective_id=collective_id, has_side_effects=True, vmem_limit_bytes=VMEM_BYTES
        ),
        cost_estimate=cost(16 if x.shape[1] > TQ else 9),
        name="swap",
    )(x)


W_SHAPES = ((272, 3264), (272, 1088), (272, 4352), (1088, 1088))
W_CUTS = (1664, 512, 2176, 512)


def weights_kernel(*refs):
    ins, docs, outs, all_docs, held = refs[:4], refs[4], refs[5:9], refs[9], refs[10:14]
    (own_s, own_r, local, back, xp_s, xp_r, xd_s, xd_r, f_s, f_r) = refs[14:24]
    (a1_s, a1_r, b1_s, b1_r, a2_s, a2_r, b2_s, b2_r, a3_s, a3_r, b3_s, b3_r, doc1_s, doc1_r, doc2_s, doc2_r) = refs[24:]
    j = lax.axis_index("shard")
    me = lax.axis_index("replica")
    z, y = me // 4, lax.rem(me, 4)
    xj = lax.rem(j + 2, 4)
    cj = j + 1 - 2 * lax.rem(j, 2)
    x_place, c_place = {"shard": xj}, {"shard": cj}
    y_places = [{"replica": y_peer(me, d)} for d in (1, 2, 3)]
    z_places = [{"replica": z_peer(me, d)} for d in (1, 2, 3)]
    greet([x_place, c_place] + y_places + z_places)

    def rows(start, count):
        return pl.ds(pl.multiple_of(start, 16), count)

    waits = []
    x_pieces, x_directs = [], []
    for a, (r, n) in enumerate(W_SHAPES):
        u = r // 17
        piece = remote(ins[a].at[rows(me * u, u)], outs[a].at[rows(j * r + me * u, u)], xp_s.at[a], xp_r.at[a], x_place)
        piece.start()
        x_pieces.append(piece)
    for a, (r, n) in enumerate(W_SHAPES):
        u = r // 17
        direct = remote(ins[a].at[rows(16 * u, u)], outs[a].at[rows(j * r + 16 * u, u)], xd_s.at[a], xd_r.at[a], x_place)
        direct.start()
        x_directs.append(direct)
    for a, (r, n) in enumerate(W_SHAPES):
        copy = remote(ins[a], outs[a].at[rows(j * r, r)], own_s.at[a], own_r.at[a], c_place)
        copy.start()
        waits.append(copy)
    all_docs[pl.ds(me, 1)] = docs[...][None]
    ours = all_docs.at[me]
    doc_firsts = [remote(ours, ours, doc1_s.at[i], doc1_r.at[i], y_places[i]) for i in range(3)]
    for copy in doc_firsts:
        copy.start()
    loads = [pltpu.make_async_copy(ins[a], held[a], local.at[a]) for a in range(4)]
    for copy in loads:
        copy.start()
    for a, (r, n) in enumerate(W_SHAPES):
        loads[a].wait()
        copy = pltpu.make_async_copy(held[a], outs[a].at[rows(j * r, r)], back.at[a])
        copy.start()
        waits.append(copy)
    for copy in doc_firsts:
        copy.wait()
    ours = all_docs.at[pl.ds(z * 4, 4)]
    for i in range(3):
        copy = remote(ours, ours, doc2_s.at[i], doc2_r.at[i], z_places[i])
        copy.start()
        waits.append(copy)
    firsts = []
    for a, (r, n) in enumerate(W_SHAPES):
        u, cut = r // 17, W_CUTS[a]
        x_pieces[a].wait()
        here = rows(xj * r + me * u, u)
        part_a = outs[a].at[here, pl.ds(0, cut)]
        part_b = outs[a].at[here, pl.ds(cut, n - cut)]
        group = []
        for i in range(3):
            group.append(remote(part_a, part_a, a1_s.at[a, i], a1_r.at[a, i], y_places[i]))
            group.append(remote(part_b, part_b, b1_s.at[a, i], b1_r.at[a, i], z_places[i]))
        for copy in group:
            copy.start()
        firsts.append(group)
    def row_part(a, first, half):
        r, u = W_SHAPES[a][0], W_SHAPES[a][0] // 17
        start = xj * r + lax.rem(first + 4, 4) * (4 * u) + half * (2 * u)
        return outs[a].at[rows(start, 2 * u), pl.ds(0, W_CUTS[a])]

    def column_part(a, first, k):
        (r, n), u = W_SHAPES[a], W_SHAPES[a][0] // 17
        start = xj * r + (4 * k + lax.rem(first + 4, 4)) * u
        return outs[a].at[rows(start, u), pl.ds(W_CUTS[a], n - W_CUTS[a])]

    heres = []
    for a in range(4):
        for copy in firsts[a]:
            copy.wait()
        rights, lefts = [], []
        for k in range(2):
            ref = row_part(a, z, k)
            rights.append(remote(ref, ref, a2_s.at[a, k], a2_r.at[a, k], z_places[0]))
            ref = row_part(a, z, 1 - k)
            lefts.append(remote(ref, ref, a2_s.at[a, 2 + k], a2_r.at[a, 2 + k], z_places[2]))
        for k in range(4):
            ref = column_part(a, y, k)
            rights.append(remote(ref, ref, b2_s.at[a, k], b2_r.at[a, k], y_places[0]))
            ref = column_part(a, y, 3 - k)
            lefts.append(remote(ref, ref, b2_s.at[a, 4 + k], b2_r.at[a, 4 + k], y_places[2]))
        for copy in rights + lefts:
            copy.start()
        heres.append((rights, lefts))
    for a, (r, n) in enumerate(W_SHAPES):
        rights, lefts = heres[a]
        passed = []
        rights[0].wait()
        ref = row_part(a, z - 1, 0)
        passed.append(remote(ref, ref, a3_s.at[a, 0], a3_r.at[a, 0], z_places[0]))
        lefts[0].wait()
        ref = row_part(a, z + 1, 1)
        passed.append(remote(ref, ref, a3_s.at[a, 1], a3_r.at[a, 1], z_places[2]))
        for k in range(2):
            rights[2 + k].wait()
            ref = column_part(a, y - 1, k)
            passed.append(remote(ref, ref, b3_s.at[a, k], b3_r.at[a, k], y_places[0]))
            lefts[2 + k].wait()
            ref = column_part(a, y + 1, 3 - k)
            passed.append(remote(ref, ref, b3_s.at[a, 2 + k], b3_r.at[a, 2 + k], y_places[2]))
        for copy in passed:
            copy.start()
        for copy in rights[1:2] + rights[4:] + lefts[1:2] + lefts[4:] + passed:
            copy.wait()
        x_directs[a].wait()
        whole = outs[a].at[rows(xj * r, r)]
        copy = remote(whole, whole, f_s.at[a], f_r.at[a], c_place)
        copy.start()
        waits.append(copy)
    for copy in waits:
        copy.wait()


def gather_weights(weights, docs):
    dma = pltpu.SemaphoreType.DMA
    outs = [jax.ShapeDtypeStruct((4 * r, n), jnp.bfloat16) for r, n in W_SHAPES]
    return pl.pallas_call(
        weights_kernel,
        out_shape=outs + [jax.ShapeDtypeStruct((NR, 8, 128), jnp.int32)],
        in_specs=[pl.BlockSpec(memory_space=pl.ANY)] * 4 + vmem_specs(1),
        out_specs=[pl.BlockSpec(memory_space=pl.ANY)] * 4 + vmem_specs(1),
        scratch_shapes=[pltpu.VMEM(shape, jnp.bfloat16) for shape in W_SHAPES]
        + [dma((4,))] * 10
        + [dma((4, 3))] * 4
        + [dma((4, 4))] * 2
        + [dma((4, 8))] * 2
        + [dma((4, 2))] * 2
        + [dma((4, 4))] * 2
        + [dma((3,))] * 4,
        compiler_params=pltpu.CompilerParams(
            collective_id=1, has_side_effects=True, vmem_limit_bytes=VMEM_BYTES
        ),
        name="gather_weights",
    )(*weights, docs)


def total_kernel(g, out, tr, ins, ad, part, mid, fin, p_s, p_r, q_s, q_r, m_s, m_r, n_s, n_r, e_s, e_r, w_s, w_r, loc):
    me = lax.axis_index("replica")
    z, y = me // 4, lax.rem(me, 4)
    y_places = [{"replica": y_peer(me, d)} for d in (1, 2, 3)]
    z_places = [{"replica": z_peer(me, d)} for d in (1, 2, 3)]
    greet(y_places + z_places)
    f32, bf16 = jnp.float32, jnp.bfloat16
    firsts, seconds = (y_places, z_places), (z_places, y_places)
    here, there = (y, z), (z, y)

    def at(side, first, second):
        first = lax.rem(first + 4, 4)
        piece = 4 * second + first if side == 0 else 4 * first + second
        return (pl.ds(side * HALF, HALF), pl.ds(pl.multiple_of(piece * PIECE, 128), PIECE))

    def piece_of(ref, side, first, second):
        return ref.at[at(side, first, second)]

    def value_of(side, first, second):
        return g[at(side, first, second)].astype(f32)

    opened, direct, added = [], [], []
    for s in range(2):
        t, right, left = here[s], firsts[s][0], firsts[s][2]
        group = []
        for k in range(2):
            group.append(remote(piece_of(g, s, t + 2, k), tr.at[s, 0, k], p_s.at[s, k], p_r.at[s, k], right))
            group.append(remote(piece_of(g, s, t + 2, k + 2), tr.at[s, 1, k], p_s.at[s, 2 + k], p_r.at[s, 2 + k], left))
        for copy in group:
            copy.start()
        opened.append(group)
    for s in range(2):
        t, right, left = here[s], firsts[s][0], firsts[s][2]
        group = []
        for k in range(2):
            group.append(remote(piece_of(g, s, t + 1, k + 2), ins.at[s, 0, k + 2], p_s.at[s, 4 + k], p_r.at[s, 4 + k], right))
            group.append(remote(piece_of(g, s, t - 1, k), ins.at[s, 1, k], p_s.at[s, 6 + k], p_r.at[s, 6 + k], left))
        for copy in group:
            copy.start()
        direct.append(group)
    for s in range(2):
        t, right, left = here[s], firsts[s][0], firsts[s][2]
        group = []
        for k in range(2):
            opened[s][2 * k].wait()
            ad[s, 0, k] = (tr[s, 0, k].astype(f32) + value_of(s, t + 1, k)).astype(bf16)
            copy = remote(ad.at[s, 0, k], ins.at[s, 0, k], q_s.at[s, k], q_r.at[s, k], right)
            copy.start()
            group.append(copy)
            opened[s][2 * k + 1].wait()
            ad[s, 1, k] = (tr[s, 1, k].astype(f32) + value_of(s, t - 1, k + 2)).astype(bf16)
            copy = remote(ad.at[s, 1, k], ins.at[s, 1, k + 2], q_s.at[s, 2 + k], q_r.at[s, 2 + k], left)
            copy.start()
            group.append(copy)
        added.append(group)
    middles = []
    for s in range(2):
        for copy in direct[s] + added[s]:
            copy.wait()
        for k in range(4):
            part[s, k] = (value_of(s, here[s], k) + ins[s, 0, k].astype(f32) + ins[s, 1, k].astype(f32)).astype(bf16)
        group = []
        for i in range(3):
            to = lax.rem(there[s] + 1 + i, 4)
            group.append(remote(part.at[s, to], mid.at[s, i], m_s.at[s, i], m_r.at[s, i], seconds[s][i]))
        for copy in group:
            copy.start()
        middles.append(group)
    backs = []
    for s in range(2):
        for copy in middles[s]:
            copy.wait()
        total = part[s, there[s]].astype(f32)
        for i in range(3):
            total = total + mid[s, i].astype(f32)
        fin[s] = total.astype(bf16)
        where = piece_of(out, s, here[s], there[s])
        group = [remote(fin.at[s], where, n_s.at[s, i], n_r.at[s, i], seconds[s][i]) for i in range(3)]
        group.append(pltpu.make_async_copy(fin.at[s], where, loc.at[s]))
        for copy in group:
            copy.start()
        backs.append(group)
    rights, lefts = [], []
    for s in range(2):
        t, right, left = here[s], firsts[s][0], firsts[s][2]
        for copy in backs[s]:
            copy.wait()
        to_right, to_left = [], []
        for k in range(4):
            ref = piece_of(out, s, t, k)
            to_right.append(remote(ref, ref, e_s.at[s, k], e_r.at[s, k], right))
            ref = piece_of(out, s, t, 3 - k)
            to_left.append(remote(ref, ref, e_s.at[s, 4 + k], e_r.at[s, 4 + k], left))
        for k in range(4):
            to_right[k].start()
            to_left[k].start()
        rights.append(to_right)
        lefts.append(to_left)
    passed = []
    for k in range(2):
        for s in range(2):
            t, right, left = here[s], firsts[s][0], firsts[s][2]
            rights[s][k].wait()
            ref = piece_of(out, s, t - 1, k)
            copy = remote(ref, ref, w_s.at[s, k], w_r.at[s, k], right)
            copy.start()
            passed.append(copy)
            lefts[s][k].wait()
            ref = piece_of(out, s, t + 1, 3 - k)
            copy = remote(ref, ref, w_s.at[s, 2 + k], w_r.at[s, 2 + k], left)
            copy.start()
            passed.append(copy)
    for s in range(2):
        for copy in rights[s][2:] + lefts[s][2:]:
            copy.wait()
    for copy in passed:
        copy.wait()


def total_over_replicas(g):
    dma = pltpu.SemaphoreType.DMA
    bf16 = jnp.bfloat16
    piece = (HALF, PIECE)
    return pl.pallas_call(
        total_kernel,
        out_shape=jax.ShapeDtypeStruct(g.shape, g.dtype),
        in_specs=vmem_specs(1),
        out_specs=pl.BlockSpec(memory_space=pl.ANY),
        scratch_shapes=[
            pltpu.VMEM((2, 2, 2) + piece, bf16),
            pltpu.VMEM((2, 2, 4) + piece, bf16),
            pltpu.VMEM((2, 2, 2) + piece, bf16),
            pltpu.VMEM((2, 4) + piece, bf16),
            pltpu.VMEM((2, 3) + piece, bf16),
            pltpu.VMEM((2,) + piece, bf16),
        ]
        + [dma((2, 8))] * 2
        + [dma((2, 4))] * 2
        + [dma((2, 3))] * 4
        + [dma((2, 8))] * 2
        + [dma((2, 4))] * 2
        + [dma((2,))],
        compiler_params=pltpu.CompilerParams(
            collective_id=2, has_side_effects=True, vmem_limit_bytes=VMEM_BYTES
        ),
        name="total_over_replicas",
    )(g)


def lane_mask(shape, micro):
    lane = lax.broadcasted_iota(jnp.int32, shape, len(shape) - 1)
    return (lane >= HD) if micro else (lane < HD)


def allowed_block(n0, n2, first_query, queries, keys):
    i = lax.broadcasted_iota(jnp.int32, (queries, keys), 0) + first_query
    j = lax.broadcasted_iota(jnp.int32, (queries, keys), 1)
    row = lax.broadcasted_iota(jnp.int32, (queries, 1), 0) + first_query
    start = jnp.where(row >= n2, n2, jnp.where(row >= n0, n0, 0))
    return (j <= i) & (j >= start)


def scores_of(q, k, micro, allowed):
    zero = jnp.zeros((), jnp.bfloat16)
    q = jnp.where(lane_mask(q.shape, micro), q, zero)
    s = lax.dot_general(q, k, (((1,), (1,)), ((), ())), preferred_element_type=jnp.float32)
    return jnp.where(allowed, s * SCALE, masked_score)


def take(x, entry, start, count):
    return x[pl.ds(start, count), entry].reshape(count * TQ, 2 * HD)


def forward_kernel(bounds, x, q16, o, o16, lse, lse16):
    zero = jnp.zeros((), jnp.bfloat16)
    me = lax.axis_index("replica")

    def attend(q, k, v, micro, first_query):
        allowed = allowed_block(bounds[micro], bounds[2 + micro], first_query, q.shape[0], k.shape[0])
        s = scores_of(q, k, micro, allowed)
        largest = jnp.max(s, axis=-1, keepdims=True)
        e = jnp.exp(s - largest)
        summed = jnp.sum(e, axis=-1, keepdims=True)
        p = (e * (1.0 / summed)).astype(jnp.bfloat16)
        v = jnp.where(lane_mask(v.shape, micro), v, zero)
        return times(p, v), largest + jnp.log(summed)

    per = BQ // TQ
    for b in range(SEQ // BQ):
        count = (b + 1) * per
        q = take(x, 0, b * per, per)
        k = take(x, 1, 0, count)
        v = take(x, 2, 0, count)
        o0, l0 = attend(q, k, v, 0, b * BQ)
        o1, l1 = attend(q, k, v, 1, b * BQ)
        o[pl.ds(b * per, per)] = (o0 + o1).astype(jnp.bfloat16).reshape(per, TQ, 2 * HD)
        lse[pl.ds(b * BQ, BQ)] = jnp.where(lane_mask((BQ, 2 * HD), 0), l0, l1)
    q = q16[...]
    k = take(x, 3, 0, NR)
    v = take(x, 4, 0, NR)
    o0, l0 = attend(q, k, v, 0, me * TQ)
    o1, l1 = attend(q, k, v, 1, me * TQ)
    o16[...] = (o0 + o1).astype(jnp.bfloat16)
    lse16[...] = jnp.where(lane_mask((TQ, 2 * HD), 0), l0, l1)


def vmem_specs(count):
    return [pl.BlockSpec(memory_space=pltpu.VMEM)] * count


def attention_forward(bounds, x, q16):
    f32, bf16 = jnp.float32, jnp.bfloat16
    return pl.pallas_call(
        forward_kernel,
        out_shape=[
            jax.ShapeDtypeStruct((NR, TQ, 2 * HD), bf16),
            jax.ShapeDtypeStruct((TQ, 2 * HD), bf16),
            jax.ShapeDtypeStruct((SEQ, 2 * HD), f32),
            jax.ShapeDtypeStruct((TQ, 2 * HD), f32),
        ],
        in_specs=[pl.BlockSpec(memory_space=pltpu.SMEM)] + vmem_specs(2),
        out_specs=vmem_specs(4),
        compiler_params=pltpu.CompilerParams(vmem_limit_bytes=VMEM_BYTES),
        cost_estimate=cost(5),
        name="attention_forward",
    )(bounds, x, q16)


def backward_kernel(bounds, x, q16, lse, lse16, do, do16, dx, dq16, dk, dv):
    zero = jnp.zeros((), jnp.bfloat16)
    me = lax.axis_index("replica")
    bf16 = jnp.bfloat16

    def pull(q, k, v, grad, logs, micro, first_query):
        allowed = allowed_block(bounds[micro], bounds[2 + micro], first_query, q.shape[0], k.shape[0])
        s = scores_of(q, k, micro, allowed)
        soft = jnp.exp(s - logs[:, micro * HD : micro * HD + 1])
        grad = jnp.where(lane_mask(grad.shape, micro), grad, zero)
        dp = times_transposed(grad, v)
        along = jnp.sum(soft * dp, axis=-1, keepdims=True)
        ds = (soft * (dp - along)).astype(bf16)
        q = jnp.where(lane_mask(q.shape, micro), q, zero)
        k = jnp.where(lane_mask(k.shape, micro), k, zero)
        return times(ds, k), outer_sum(ds, q), outer_sum(soft.astype(bf16), grad)

    per = BQ // TQ
    for b in reversed(range(SEQ // BQ)):
        count = (b + 1) * per
        q = take(x, 0, b * per, per)
        k = take(x, 1, 0, count)
        v = take(x, 2, 0, count)
        grad = do[pl.ds(b * per, per)].reshape(BQ, 2 * HD)
        logs = lse[pl.ds(b * BQ, BQ)]
        q0, k0, v0 = pull(q, k, v, grad, logs, 0, b * BQ)
        q1, k1, v1 = pull(q, k, v, grad, logs, 1, b * BQ)
        dx[pl.ds(b * per, per), 0] = ((q0 + q1) * SCALE).astype(bf16).reshape(per, TQ, 2 * HD)
        keys = pl.ds(0, (b + 1) * BQ)
        if b == SEQ // BQ - 1:
            dk[keys] = k0 + k1
            dv[keys] = v0 + v1
        else:
            dk[keys] += k0 + k1
            dv[keys] += v0 + v1
    dx[:, 1] = (dk[...] * SCALE).astype(bf16).reshape(NR, TQ, 2 * HD)
    dx[:, 2] = dv[...].astype(bf16).reshape(NR, TQ, 2 * HD)
    q = q16[...]
    k = take(x, 3, 0, NR)
    v = take(x, 4, 0, NR)
    q0, k0, v0 = pull(q, k, v, do16[...], lse16[...], 0, me * TQ)
    q1, k1, v1 = pull(q, k, v, do16[...], lse16[...], 1, me * TQ)
    dq16[...] = ((q0 + q1) * SCALE).astype(bf16)
    dx[:, 3] = ((k0 + k1) * SCALE).astype(bf16).reshape(NR, TQ, 2 * HD)
    dx[:, 4] = (v0 + v1).astype(bf16).reshape(NR, TQ, 2 * HD)


def attention_backward(bounds, x, q16, lse, lse16, do, do16):
    f32, bf16 = jnp.float32, jnp.bfloat16
    return pl.pallas_call(
        backward_kernel,
        out_shape=[
            jax.ShapeDtypeStruct((NR, 5, TQ, 2 * HD), bf16),
            jax.ShapeDtypeStruct((TQ, 2 * HD), bf16),
        ],
        in_specs=[pl.BlockSpec(memory_space=pltpu.SMEM)] + vmem_specs(6),
        out_specs=vmem_specs(2),
        scratch_shapes=[pltpu.VMEM((SEQ, 2 * HD), f32), pltpu.VMEM((SEQ, 2 * HD), f32)],
        compiler_params=pltpu.CompilerParams(vmem_limit_bytes=VMEM_BYTES),
        cost_estimate=cost(8),
        name="attention_backward",
    )(bounds, x, q16, lse, lse16, do, do16)


QKV = 3 * D
ENTER_BLOCK, LEAVE_BLOCK, BACK_ENTER_BLOCK = 1664, 2176, 640
LEFT_AT, LEFT_WIDTH = (0, 384, 768, 1152), 2304
EARLY_AT, EARLY_WIDTH = (0, 4352, 5504), 6656
LATE_WIDTH = 3328
SMALL = 1152


def low_lanes(shape):
    return lane_mask(shape, 0)


def to_blocks(upper, lower, odd):
    half = low_lanes(upper.shape)
    if odd:
        return jnp.where(half, pltpu.roll(upper, HD, 1), lower)
    return jnp.where(half, upper, pltpu.roll(lower, HD, 1))


def from_blocks(first, second):
    half = low_lanes(first.shape)
    upper = jnp.where(half, first, pltpu.roll(second, HD, 1))
    return upper, jnp.where(half, pltpu.roll(first, HD, 1), second)


def lines(start, count):
    return pl.ds(start, count)


def enter_kernel(x, gains, biases, w, message, q16, act, mixed):
    i = pl.program_id(0)

    @pl.when(i == 0)
    def _():
        normed, _, _ = layer_norm(x[...].astype(jnp.float32), gains[0:1], biases[0:1])
        act[...] = normed.astype(jnp.bfloat16)

    mixed[i] = times(act[...], w[...])

    @pl.when(i == pl.num_programs(0) - 1)
    def _():
        for b in range(3 * H):
            kind, head = divmod(b, H)
            i, t = divmod(b // 2, ENTER_BLOCK // 128)
            part = pl.ds(t * 128, 128)
            block = to_blocks(mixed[i, 0:TQ, part], mixed[i, TQ : 2 * TQ, part], b % 2)
            if kind != 1:
                row = 1 if kind == 0 else 2
                shift = biases[row : row + 1, head * HD : (head + 1) * HD]
                block = block + jnp.concatenate([shift, shift], axis=1)
            block = block.astype(jnp.bfloat16)
            if head < H - 1:
                message[head, kind * TQ : (kind + 1) * TQ] = block
            elif kind == 0:
                q16[...] = block
            else:
                for p in range(NR):
                    message[p, (kind + 2) * TQ : (kind + 3) * TQ] = block


def fixed(shape):
    return pl.BlockSpec(shape, lambda i: (0,) * len(shape))


def enter(x, gains, biases, w_qkv):
    bf16 = jnp.bfloat16
    steps = -(-QKV // ENTER_BLOCK)
    shapes = [(NR, 5 * TQ, 2 * HD), (TQ, 2 * HD), (2 * TQ, D)]
    return pl.pallas_call(
        enter_kernel,
        grid=(steps,),
        out_shape=[jax.ShapeDtypeStruct(shape, bf16) for shape in shapes],
        in_specs=[
            fixed(x.shape),
            fixed(gains.shape),
            fixed(biases.shape),
            pl.BlockSpec((D, ENTER_BLOCK), lambda i: (0, i)),
        ],
        out_specs=[fixed(shape) for shape in shapes],
        scratch_shapes=[pltpu.VMEM((steps, 2 * TQ, ENTER_BLOCK), jnp.float32)],
        compiler_params=pltpu.CompilerParams(vmem_limit_bytes=VMEM_BYTES),
        cost_estimate=cost(5),
        name="enter",
    )(x, gains, biases, w_qkv)


CURVE = 0.044715
ROOT = 0.7978845608028654


def leave_kernel(
    x, o, o16, act1, gains, biases, up_shift, w_out, w_up, w_down, result, resid, pre, lefts, act2, total
):
    i = pl.program_id(0)
    bf16 = jnp.bfloat16

    @pl.when(i == 0)
    def _():
        tiles = []
        for t in range(H // 2 + 1):
            first = o[2 * t] if 2 * t < H - 1 else o16[...]
            second = o[2 * t + 1] if 2 * t + 1 < H - 1 else o16[...]
            upper, lower = from_blocks(first.astype(jnp.float32), second.astype(jnp.float32))
            tiles.append(jnp.concatenate([upper, lower], axis=0))
        attended = jnp.concatenate(tiles, axis=1)[:, :D].astype(bf16)
        r = x[...].astype(jnp.float32) + times(attended, w_out[...]) + biases[3:4]
        resid[...] = r
        normed, _, _ = layer_norm(r, gains[1:2], biases[4:5])
        act2[...] = normed.astype(bf16)
        for s in range(4):
            part = slice(s * 272, (s + 1) * 272)
            for at, value in zip(LEFT_AT, (act1, attended, act2)):
                lefts[s, :, at : at + 272] = value[:, part]
        total[...] = r + biases[5:6]

    u = times(act2[...], w_up[...]) + up_shift[...]
    pre[...] = u
    g = (0.5 * u * (1.0 + jnp.tanh(ROOT * (u + CURVE * u * u * u)))).astype(bf16)
    for s in range(2):
        lefts[2 * i + s, :, LEFT_AT[3] : LEFT_AT[3] + D] = g[:, s * D : (s + 1) * D]
    total[...] += times(g, w_down[...])

    @pl.when(i == pl.num_programs(0) - 1)
    def _():
        result[...] = total[...].astype(bf16)


def leave(x, o, o16, act1, gains, biases, up_shift, weights):
    _, w_out, w_up, w_down = weights
    f32, bf16 = jnp.float32, jnp.bfloat16
    rows = 2 * TQ
    return pl.pallas_call(
        leave_kernel,
        grid=(FF // LEAVE_BLOCK,),
        out_shape=[
            jax.ShapeDtypeStruct((rows, D), bf16),
            jax.ShapeDtypeStruct((rows, D), f32),
            jax.ShapeDtypeStruct((rows, FF), f32),
            jax.ShapeDtypeStruct((4, rows, LEFT_WIDTH), bf16),
        ],
        in_specs=[
            fixed(x.shape),
            fixed(o.shape),
            fixed(o16.shape),
            fixed(act1.shape),
            fixed(gains.shape),
            fixed(biases.shape),
            pl.BlockSpec((1, LEAVE_BLOCK), lambda i: (0, i)),
            fixed(w_out.shape),
            pl.BlockSpec((D, LEAVE_BLOCK), lambda i: (0, i)),
            pl.BlockSpec((LEAVE_BLOCK, D), lambda i: (i, 0)),
        ],
        out_specs=[
            fixed((rows, D)),
            fixed((rows, D)),
            pl.BlockSpec((rows, LEAVE_BLOCK), lambda i: (0, i)),
            fixed((4, rows, LEFT_WIDTH)),
        ],
        scratch_shapes=[pltpu.VMEM((rows, D), bf16), pltpu.VMEM((rows, D), f32)],
        compiler_params=pltpu.CompilerParams(vmem_limit_bytes=VMEM_BYTES),
        cost_estimate=cost(12),
        name="leave",
    )(x, o, o16, act1, gains, biases, up_shift, w_out, w_up, w_down)


def column_sum(value):
    return jnp.sum(value, axis=0, keepdims=True)


def back_leave_kernel(
    dy, resid, pre, gains, w_out, w_up, w_down, early, grad_resid, do, do16, sums, total
):
    i = pl.program_id(0)
    f32, bf16 = jnp.float32, jnp.bfloat16

    @pl.when(i == 0)
    def _():
        total[...] = jnp.zeros_like(total)

    u = pre[...]
    grad_hidden = times_transposed(dy[...], w_down[...])
    t = jnp.tanh(ROOT * (u + CURVE * u * u * u))
    slope = 0.5 * (1.0 + t) + 0.5 * u * (1.0 - t * t) * (ROOT * (1.0 + 3.0 * CURVE * u * u))
    du = (grad_hidden * slope).astype(bf16)
    early[:, pl.ds(pl.multiple_of(i * LEAVE_BLOCK, 128), LEAVE_BLOCK)] = du
    du_sum = column_sum(du.astype(f32))
    for s in range(2):
        sums[pl.ds(4 + 2 * i + s, 1), 0:D] = du_sum[:, s * D : (s + 1) * D]
    total[...] += times_transposed(du, w_up[...])

    @pl.when(i == pl.num_programs(0) - 1)
    def _():
        da2 = total[...]
        _, normed, inverse = layer_norm(resid[...], gains[1:2], 0.0)
        dr = dy[...].astype(f32) + norm_back(da2, normed, inverse, gains[1:2])
        grad_resid[...] = dr
        db = dr.astype(bf16)
        for at in EARLY_AT[1:]:
            early[:, at + 1024 : at + 1152] = jnp.zeros((2 * TQ, 128), bf16)
        early[:, EARLY_AT[1] : EARLY_AT[1] + D] = db
        early[:, EARLY_AT[2] : EARLY_AT[2] + D] = dy[...]
        sums[0:1, 0:D] = column_sum(da2 * normed)
        sums[1:2, 0:D] = column_sum(da2)
        sums[2:3, 0:D] = column_sum(db.astype(f32))
        sums[3:4, 0:D] = column_sum(dy[...].astype(f32))
        heads = times_transposed(db, w_out[...])
        heads = jnp.concatenate([heads, jnp.zeros((2 * TQ, HD), f32)], axis=1)
        for b in range(H):
            tile = heads[:, (b // 2) * 128 : (b // 2 + 1) * 128]
            block = to_blocks(tile[0:TQ], tile[TQ : 2 * TQ], b % 2).astype(bf16)
            if b < H - 1:
                do[b] = block
            else:
                do16[...] = block


def back_leave(dy, resid, pre, gains, weights):
    _, w_out, w_up, w_down = weights
    f32, bf16 = jnp.float32, jnp.bfloat16
    rows = 2 * TQ
    shapes = [(rows, EARLY_WIDTH), (rows, D), (NR, TQ, 2 * HD), (TQ, 2 * HD), (8, SMALL)]
    types = [bf16, f32, bf16, bf16, f32]
    return pl.pallas_call(
        back_leave_kernel,
        grid=(FF // LEAVE_BLOCK,),
        out_shape=[jax.ShapeDtypeStruct(shape, t) for shape, t in zip(shapes, types)],
        in_specs=[
            fixed((rows, D)),
            fixed((rows, D)),
            pl.BlockSpec((rows, LEAVE_BLOCK), lambda i: (0, i)),
            fixed(gains.shape),
            fixed(w_out.shape),
            pl.BlockSpec((D, LEAVE_BLOCK), lambda i: (0, i)),
            pl.BlockSpec((LEAVE_BLOCK, D), lambda i: (i, 0)),
        ],
        out_specs=[fixed(shape) for shape in shapes],
        scratch_shapes=[pltpu.VMEM((rows, D), f32)],
        compiler_params=pltpu.CompilerParams(vmem_limit_bytes=VMEM_BYTES),
        cost_estimate=cost(14),
        name="back_leave",
    )(dy, resid, pre, gains, w_out, w_up, w_down)


def back_enter_kernel(x, back, dq16, grad_resid, before, gains, w, late, grad_in, sums, parts):
    i = pl.program_id(0)
    f32, bf16 = jnp.float32, jnp.bfloat16

    @pl.when(i == 0)
    def _():
        def last(kind):
            total = back[0, (kind + 2) * TQ : (kind + 3) * TQ].astype(f32)
            for p in range(1, NR):
                total = total + back[p, (kind + 2) * TQ : (kind + 3) * TQ].astype(f32)
            return total

        def block(b):
            kind, head = divmod(b, H)
            if head < H - 1:
                return back[head, kind * TQ : (kind + 1) * TQ].astype(f32)
            return dq16[...].astype(f32) if kind == 0 else last(kind)

        for t in range(3 * H // 2 + 1):
            first = block(2 * t)
            second = block(2 * t + 1) if 2 * t + 1 < 3 * H else jnp.zeros_like(first)
            upper, lower = from_blocks(first, second)
            late[0:TQ, t * 128 : (t + 1) * 128] = upper.astype(bf16)
            late[TQ : 2 * TQ, t * 128 : (t + 1) * 128] = lower.astype(bf16)

    parts[i] = times_transposed(late[:, 0:QKV], w[...])

    @pl.when(i == pl.num_programs(0) - 1)
    def _():
        da1 = jnp.concatenate([parts[k] for k in range(parts.shape[0])], axis=1)[:, :D]
        _, normed, inverse = layer_norm(x[...].astype(f32), gains[0:1], 0.0)
        dx = grad_resid[...] + norm_back(da1, normed, inverse, gains[0:1])
        grad_in[...] = dx.astype(bf16)
        sums[...] = jnp.zeros_like(sums)
        sums[0:1, 0:D] = column_sum(da1 * normed)
        sums[1:2, 0:D] = column_sum(da1)
        sums[2:3, 0:D] = column_sum(late[:, 0:D].astype(f32))
        sums[3:4, 0:D] = column_sum(late[:, 2 * D : QKV].astype(f32))
        sums[4:12, 0:D] = before[:, 0:D]


def back_enter(x, back, dq16, grad_resid, before, gains, w_qkv):
    f32, bf16 = jnp.float32, jnp.bfloat16
    rows = 2 * TQ
    steps = -(-D // BACK_ENTER_BLOCK)
    return pl.pallas_call(
        back_enter_kernel,
        grid=(steps,),
        out_shape=[
            jax.ShapeDtypeStruct((rows, LATE_WIDTH), bf16),
            jax.ShapeDtypeStruct((rows, D), bf16),
            jax.ShapeDtypeStruct((16, SMALL), f32),
        ],
        in_specs=[
            fixed(x.shape),
            fixed(back.shape),
            fixed(dq16.shape),
            fixed(grad_resid.shape),
            fixed(before.shape),
            fixed(gains.shape),
            pl.BlockSpec((BACK_ENTER_BLOCK, QKV), lambda i: (i, 0)),
        ],
        out_specs=[fixed((rows, LATE_WIDTH)), fixed((rows, D)), fixed((16, SMALL))],
        scratch_shapes=[pltpu.VMEM((steps, rows, BACK_ENTER_BLOCK), f32)],
        compiler_params=pltpu.CompilerParams(vmem_limit_bytes=VMEM_BYTES),
        cost_estimate=cost(5),
        name="back_enter",
    )(x, back, dq16, grad_resid, before, gains, w_qkv)


AT_OUT, AT_UP, AT_DOWN, DOWN_STEP = 3328, 4480, 8832, 1152


def products_kernel(
    l0, l1, l2, l3, e0, e1, e2, late, small, out, lefts, early, mixed, got, loc, late_s, late_r, small_s, small_r
):
    bf16 = jnp.bfloat16
    rows = 2 * TQ
    j = lax.axis_index("shard")
    xj = lax.rem(j + 2, 4)
    cj = j + 1 - 2 * lax.rem(j, 2)
    places = [{"shard": xj}, {"shard": cj}, {"shard": lax.rem(cj + 2, 4)}]
    greet(places)

    def slot(ref, k):
        return ref.at[pl.ds(k * rows, rows)]

    across = remote(late, slot(mixed, 1), late_s.at[0], late_r.at[0], places[0])
    across.start()
    beside = remote(late, slot(mixed, 2), late_s.at[1], late_r.at[1], places[1])
    beside.start()
    early_relay = remote(e1, slot(early, 3), late_s.at[3], late_r.at[3], places[1])
    early_relay.start()
    smalls = [remote(small, got.at[k], small_s.at[k], small_r.at[k], places[k]) for k in range(3)]
    for copy in smalls:
        copy.start()
    loads = [pltpu.make_async_copy(late, slot(mixed, 0), loc.at[0])]
    loads.append(pltpu.make_async_copy(l0.at[j], slot(lefts, 0), loc.at[1]))
    for k, ref in enumerate((l1, l2, l3)):
        loads.append(pltpu.make_async_copy(ref, slot(lefts, k + 1), loc.at[2 + k]))
    for k, ref in enumerate((e0, e1, e2)):
        loads.append(pltpu.make_async_copy(ref, slot(early, k), loc.at[5 + k]))
    for copy in loads:
        copy.start()
    for copy in loads:
        copy.wait()
    early_relay.wait()

    def stripe(left_at, right, right_at, at, columns, width):
        @pl.loop(0, columns // width)
        def _(i):
            take_at = pl.ds(pl.multiple_of(right_at + i * width, 128), width)
            put_at = pl.ds(pl.multiple_of(at + i * width, 128), width)
            product = outer_sum(lefts[:, left_at : left_at + 272], right[:, take_at])
            out[0:272, put_at] = product.astype(bf16)

    stripe(LEFT_AT[2], early, EARLY_AT[0], AT_UP, FF, 2176)
    across.wait()
    relay = remote(slot(mixed, 1), slot(mixed, 3), late_s.at[2], late_r.at[2], places[1])
    relay.start()
    out[0:272, AT_OUT:AT_UP] = outer_sum(
        lefts[:, LEFT_AT[1] : LEFT_AT[1] + 272], early[:, EARLY_AT[1] : EARLY_AT[2]]
    ).astype(bf16)
    for s in range(4):
        at = AT_DOWN + s * DOWN_STEP
        first = LEFT_AT[3] + s * 272
        out[0:272, at : at + DOWN_STEP] = outer_sum(
            lefts[:, first : first + 272], early[:, EARLY_AT[2] : EARLY_WIDTH]
        ).astype(bf16)
    beside.wait()
    relay.wait()
    stripe(LEFT_AT[0], mixed, 0, 0, LATE_WIDTH, 1664)
    for copy in smalls:
        copy.wait()
    filled = AT_DOWN + 4 * DOWN_STEP
    out[0:272, filled:] = jnp.zeros((272, NR * PIECE - filled), bf16)
    out[272:RED_ROWS] = jnp.zeros((RED_ROWS - 272, NR * PIECE), bf16)
    out[272:RED_ROWS, 0:SMALL] = (small[...] + got[0] + got[1] + got[2]).astype(bf16)


def products(lefts, early, late, small):
    dma = pltpu.SemaphoreType.DMA
    f32, bf16 = jnp.float32, jnp.bfloat16
    anywhere = pl.BlockSpec(memory_space=pl.ANY)
    return pl.pallas_call(
        products_kernel,
        out_shape=jax.ShapeDtypeStruct((RED_ROWS, NR * PIECE), bf16),
        in_specs=[anywhere] * 8 + vmem_specs(1),
        out_specs=pl.BlockSpec(memory_space=pltpu.VMEM),
        scratch_shapes=[
            pltpu.VMEM((8 * TQ, LEFT_WIDTH), bf16),
            pltpu.VMEM((8 * TQ, EARLY_WIDTH), bf16),
            pltpu.VMEM((8 * TQ, LATE_WIDTH), bf16),
            pltpu.VMEM((3, 16, SMALL), f32),
            dma((8,)),
            dma((4,)), dma((4,)), dma((3,)), dma((3,)),
        ],
        compiler_params=pltpu.CompilerParams(
            collective_id=5, has_side_effects=True, vmem_limit_bytes=VMEM_BYTES
        ),
        name="products",
    )(*lefts, *early, late, small)


def widen_kernel(g, qkv, out, up, down):
    f32 = jnp.float32
    qkv[...] = g[:, 0:QKV].astype(f32)
    out[...] = g[:, AT_OUT : AT_OUT + D].astype(f32)
    up[...] = g[:, AT_UP : AT_UP + FF].astype(f32)
    for s in range(4):
        at = AT_DOWN + s * DOWN_STEP
        down[s] = g[:, at : at + D].astype(f32)


def widen(g):
    f32 = jnp.float32
    return pl.pallas_call(
        widen_kernel,
        grid=(6,),
        out_shape=[
            jax.ShapeDtypeStruct((272, QKV), f32),
            jax.ShapeDtypeStruct((272, D), f32),
            jax.ShapeDtypeStruct((272, FF), f32),
            jax.ShapeDtypeStruct((4, 272, D), f32),
        ],
        in_specs=[pl.BlockSpec((48, NR * PIECE), lambda i: (i, 0))],
        out_specs=[
            pl.BlockSpec((48, QKV), lambda i: (i, 0)),
            pl.BlockSpec((48, D), lambda i: (i, 0)),
            pl.BlockSpec((48, FF), lambda i: (i, 0)),
            pl.BlockSpec((4, 48, D), lambda i: (0, i, 0)),
        ],
        compiler_params=pltpu.CompilerParams(vmem_limit_bytes=VMEM_BYTES),
        name="widen",
    )(g)


def layer_forward(x, bounds, gains, biases, up_shift, weights):
    message, q16, act1 = enter(x, gains, biases, weights[0])
    whole = swap(message, 3).reshape(NR, 5, TQ, 2 * HD)
    o, o16, lse, lse16 = attention_forward(bounds, whole, q16)
    result, resid, pre, lefts = leave(x, swap(o, 4), o16, act1, gains, biases, up_shift, weights)
    return result, (whole, q16, lse, lse16, resid, pre), lefts


def layer_backward(dy, x, kept, bounds, gains, weights, early_tie=None, late_tie=None):
    whole, q16, lse, lse16, resid, pre = kept
    early, grad_resid, do, do16, sums = back_leave(dy, resid, pre, gains, weights)
    dx, dq16 = attention_backward(bounds, whole, q16, lse, lse16, swap(do, 4), do16)
    dx, early_tie = lax.optimization_barrier((dx, early_tie))
    back = swap(dx.reshape(NR, 5 * TQ, 2 * HD), 3)
    late, grad_in, small = back_enter(x, back, dq16, grad_resid, sums, gains, weights[0])
    grad_in, late_tie = lax.optimization_barrier((grad_in, late_tie))
    return grad_in, early, late, small, early_tie, late_tie


X_ROUTE = [(j, j ^ 2) for j in range(4)]
C_ROUTE = [(j, j ^ 1) for j in range(4)]


CX_ROUTE = [(j, j ^ 3) for j in range(4)]


def everyone(value):
    return value, lax.ppermute(value, "shard", X_ROUTE), lax.ppermute(value, "shard", C_ROUTE)


def own_columns(cut):
    j = lax.axis_index("shard")

    def of(shard):
        return lax.dynamic_index_in_dim(cut, shard, 0, keepdims=False)

    across, beside = lax.rem(j + 2, 4), j + 1 - 2 * lax.rem(j, 2)
    return (
        cut,
        lax.ppermute(of(across), "shard", X_ROUTE),
        lax.ppermute(of(beside), "shard", C_ROUTE),
        lax.ppermute(of(lax.rem(beside + 2, 4)), "shard", CX_ROUTE),
    )


def shards(tokens, cotangent, doc_ids, gains, biases, up_bias, w_qkv, w_out, w_up, w_down):
    is_first = lax.axis_index("section") == 0
    ids = doc_ids[:, 0]
    counts = jnp.stack([jnp.sum((ids == n).astype(jnp.int32), axis=1) for n in (0, 2)])
    counts = jnp.pad(counts, ((0, 6), (0, 126)))
    *weights, counts = gather_weights((w_qkv[0], w_out[0], w_up[0], w_down[0]), counts)
    counts = jnp.sum(counts[:, :2, :2], axis=0)
    bounds = jnp.concatenate([counts[0], SEQ - counts[1]])
    gains, biases = gains[0], biases[0]
    own_in = tokens.reshape(2 * TQ, D)
    own_cot = cotangent.reshape(2 * TQ, D)
    result, _, _ = layer_forward(own_in, bounds, gains, biases, up_bias, weights)
    inbox = lax.ppermute(result, "section", [(0, 1)])
    inputs = jnp.where(is_first, own_in, inbox)
    layer_out, kept, lefts = layer_forward(inputs, bounds, gains, biases, up_bias, weights)
    lefts = own_columns(lefts)
    grad_in, _, _, _, sooner, later = layer_backward(
        own_cot, inputs, kept, bounds, gains, weights, lefts[1:3], lefts[3]
    )
    lefts = (lefts[0], *sooner, later)
    inbox = lax.ppermute(grad_in, "section", [(1, 0)])
    dy = jnp.where(is_first, inbox, own_cot)
    grad_in, early, late, small, _, _ = layer_backward(dy, inputs, kept, bounds, gains, weights)
    summed = total_over_replicas(products(lefts, everyone(early), late, small))
    qkv, out, up, down = widen(summed)
    small = summed[272:RED_ROWS, :D].astype(jnp.float32)
    return (
        layer_out.reshape(1, 2, 1, TQ, D),
        grad_in.reshape(1, 2, 1, TQ, D),
        jnp.stack([small[0], small[4]])[None],
        jnp.stack([small[k] for k in (1, 2, 3, 6, 5, 7)])[None],
        small[8:12].reshape(1, FF),
        qkv[None],
        out[None],
        up[None],
        down.reshape(1, 1088, D),
    )


def solution(mesh):
    placed = (
        P(None, "shard", "replica", None),
        P(None, "shard", "replica", None),
        P(None, "shard", "replica"),
        P("section", None, None),
        P("section", None, None),
        P("section", None),
        P("section", "shard", None),
        P("section", "shard", None),
        P("section", "shard", None),
        P("section", "shard", None),
    )
    return jax.shard_map(
        shards,
        mesh=mesh,
        in_specs=placed,
        out_specs=(
            P("section", None, "shard", "replica", None),
            P("section", None, "shard", "replica", None),
            P("section", None, None),
            P("section", None, None),
            P("section", None),
            P("section", "shard", None),
            P("section", "shard", None),
            P("section", "shard", None),
            P("section", "shard", None),
        ),
        check_vma=False,
    )
```

```python
import functools

import jax
import jax.numpy as jnp
from jax import lax
from jax.experimental import pallas as pl
from jax.experimental.pallas import tpu as pltpu
from jax.sharding import PartitionSpec as P

MESH = pl.DeviceIdType.MESH
H = 17
HD = 64
TQ = 64
SEQ = 1024
NR = 16
D = 1088
FF = 4352
SCALE = HD ** (-0.5)
epsilon = 1e-05
masked_score = -1e30
BQ = 256
PIECE = 896
VMEM_BYTES = 58 * 1024 * 1024
RED_ROWS = 288
HALF = 144


def layer_norm(values, gain_row, shift_row):
    centre = values - jnp.mean(values, axis=-1, keepdims=True)
    inverse = lax.rsqrt(jnp.mean(centre * centre, axis=-1, keepdims=True) + epsilon)
    normed = centre * inverse
    return (normed * gain_row + shift_row, normed, inverse)


def norm_back(grad_normed_out, normed, inverse, gain_row):
    scaled = grad_normed_out * gain_row
    middle = jnp.mean(scaled, axis=-1, keepdims=True)
    slope = jnp.mean(scaled * normed, axis=-1, keepdims=True)
    return inverse * (scaled - middle - normed * slope)


def times(left, right):
    return jnp.dot(left, right, preferred_element_type=jnp.float32)


def times_transposed(left, right):
    return lax.dot_general(
        left, right, (((1,), (1,)), ((), ())), preferred_element_type=jnp.float32
    )


def outer_sum(left, right):
    return lax.dot_general(
        left, right, (((0,), (0,)), ((), ())), preferred_element_type=jnp.float32
    )


def y_peer(me, d):
    return (me // 4) * 4 + lax.rem(lax.rem(me, 4) + d, 4)


def z_peer(me, d):
    return lax.rem(me + 4 * d, NR)


def any_peer(me, d):
    return lax.rem(me // 4 + d // 4, 4) * 4 + lax.rem(lax.rem(me, 4) + d % 4, 4)


def remote(src, dst, send, recv, where):
    return pltpu.make_async_remote_copy(
        src_ref=src,
        dst_ref=dst,
        send_sem=send,
        recv_sem=recv,
        device_id=where,
        device_id_type=MESH,
    )


def cost(microseconds):
    return pl.CostEstimate(flops=0, bytes_accessed=int(microseconds * 3.5e6), transcendentals=0)


def greet(places):
    barrier = pltpu.get_barrier_semaphore()
    for where in places:
        pl.semaphore_signal(barrier, inc=1, device_id=where, device_id_type=MESH)
    pl.semaphore_wait(barrier, len(places))


def swap_kernel(x, o, send, recv, local):
    me = lax.axis_index("replica")
    greet([{"replica": any_peer(me, d)} for d in range(1, NR)])
    copies = []
    for d in range(1, NR):
        to = any_peer(me, d)
        copy = remote(x.at[to], o.at[me], send.at[d], recv.at[d], {"replica": to})
        copy.start()
        copies.append(copy)
    own = pltpu.make_async_copy(x.at[me], o.at[me], local)
    own.start()
    own.wait()
    for copy in copies:
        copy.wait()


def swap(x, collective_id):
    return pl.pallas_call(
        swap_kernel,
        out_shape=jax.ShapeDtypeStruct(x.shape, x.dtype),
        in_specs=[pl.BlockSpec(memory_space=pl.ANY)],
        out_specs=pl.BlockSpec(memory_space=pl.ANY),
        scratch_shapes=[
            pltpu.SemaphoreType.DMA((NR,)),
            pltpu.SemaphoreType.DMA((NR,)),
            pltpu.SemaphoreType.DMA,
        ],
        compiler_params=pltpu.CompilerParams(
            collective_id=collective_id, has_side_effects=True, vmem_limit_bytes=VMEM_BYTES
        ),
        cost_estimate=cost(16 if x.shape[1] > TQ else 9),
        name="swap",
    )(x)


W_SHAPES = ((272, 3264), (272, 1088), (272, 4352), (1088, 1088))
W_CUTS = (1408, 512, 1920, 512)
W_ENDS = (2816, 896, 3712, 896)


def weights_kernel(*refs):
    ins, docs, outs, all_docs, held = refs[:4], refs[4], refs[5:9], refs[9], refs[10:14]
    (own_s, own_r, local, back, xp_s, xp_r, xd_s, xd_r, xe_s, xe_r, f_s, f_r) = refs[14:26]
    (a1_s, a1_r, b1_s, b1_r, a2_s, a2_r, b2_s, b2_r, a3_s, a3_r, b3_s, b3_r, doc1_s, doc1_r, doc2_s, doc2_r) = refs[26:]
    j = lax.axis_index("shard")
    me = lax.axis_index("replica")
    z, y = me // 4, lax.rem(me, 4)
    xj = lax.rem(j + 2, 4)
    cj = j + 1 - 2 * lax.rem(j, 2)
    x_place, c_place = {"shard": xj}, {"shard": cj}
    y_places = [{"replica": y_peer(me, d)} for d in (1, 2, 3)]
    z_places = [{"replica": z_peer(me, d)} for d in (1, 2, 3)]
    greet([x_place, c_place] + y_places + z_places)

    def rows(start, count):
        return pl.ds(pl.multiple_of(start, 16), count)

    waits = []
    x_pieces, x_directs = [], []
    for a, (r, n) in enumerate(W_SHAPES):
        u = r // 17
        most = pl.ds(0, W_ENDS[a])
        piece = remote(ins[a].at[rows(me * u, u), most], outs[a].at[rows(j * r + me * u, u), most], xp_s.at[a], xp_r.at[a], x_place)
        piece.start()
        x_pieces.append(piece)
    for a, (r, n) in enumerate(W_SHAPES):
        u = r // 17
        most, rest = pl.ds(0, W_ENDS[a]), pl.ds(W_ENDS[a], n - W_ENDS[a])
        direct = remote(ins[a].at[rows(16 * u, u), most], outs[a].at[rows(j * r + 16 * u, u), most], xd_s.at[a], xd_r.at[a], x_place)
        direct.start()
        x_directs.append(direct)
        direct = remote(ins[a].at[:, rest], outs[a].at[rows(j * r, r), rest], xe_s.at[a], xe_r.at[a], x_place)
        direct.start()
        x_directs.append(direct)
    for a, (r, n) in enumerate(W_SHAPES):
        copy = remote(ins[a], outs[a].at[rows(j * r, r)], own_s.at[a], own_r.at[a], c_place)
        copy.start()
        waits.append(copy)
    all_docs[pl.ds(me, 1)] = docs[...][None]
    ours = all_docs.at[me]
    doc_firsts = [remote(ours, ours, doc1_s.at[i], doc1_r.at[i], y_places[i]) for i in range(3)]
    for copy in doc_firsts:
        copy.start()
    loads = [pltpu.make_async_copy(ins[a], held[a], local.at[a]) for a in range(4)]
    for copy in loads:
        copy.start()
    for a, (r, n) in enumerate(W_SHAPES):
        loads[a].wait()
        copy = pltpu.make_async_copy(held[a], outs[a].at[rows(j * r, r)], back.at[a])
        copy.start()
        waits.append(copy)
    for copy in doc_firsts:
        copy.wait()
    ours = all_docs.at[pl.ds(z * 4, 4)]
    for i in range(3):
        copy = remote(ours, ours, doc2_s.at[i], doc2_r.at[i], z_places[i])
        copy.start()
        waits.append(copy)
    firsts = []
    for a, (r, n) in enumerate(W_SHAPES):
        u, cut = r // 17, W_CUTS[a]
        x_pieces[a].wait()
        here = rows(xj * r + me * u, u)
        part_a = outs[a].at[here, pl.ds(0, cut)]
        part_b = outs[a].at[here, pl.ds(cut, W_ENDS[a] - cut)]
        group = []
        for i in range(3):
            group.append(remote(part_a, part_a, a1_s.at[a, i], a1_r.at[a, i], y_places[i]))
            group.append(remote(part_b, part_b, b1_s.at[a, i], b1_r.at[a, i], z_places[i]))
        for copy in group:
            copy.start()
        firsts.append(group)
    def row_part(a, first, half):
        r, u = W_SHAPES[a][0], W_SHAPES[a][0] // 17
        start = xj * r + lax.rem(first + 4, 4) * (4 * u) + half * (2 * u)
        return outs[a].at[rows(start, 2 * u), pl.ds(0, W_CUTS[a])]

    def column_part(a, first, k):
        r, u = W_SHAPES[a][0], W_SHAPES[a][0] // 17
        start = xj * r + (4 * k + lax.rem(first + 4, 4)) * u
        return outs[a].at[rows(start, u), pl.ds(W_CUTS[a], W_ENDS[a] - W_CUTS[a])]

    heres = []
    for a in range(4):
        for copy in firsts[a]:
            copy.wait()
        rights, lefts = [], []
        for k in range(2):
            ref = row_part(a, z, k)
            rights.append(remote(ref, ref, a2_s.at[a, k], a2_r.at[a, k], z_places[0]))
            ref = row_part(a, z, 1 - k)
            lefts.append(remote(ref, ref, a2_s.at[a, 2 + k], a2_r.at[a, 2 + k], z_places[2]))
        for k in range(4):
            ref = column_part(a, y, k)
            rights.append(remote(ref, ref, b2_s.at[a, k], b2_r.at[a, k], y_places[0]))
            ref = column_part(a, y, 3 - k)
            lefts.append(remote(ref, ref, b2_s.at[a, 4 + k], b2_r.at[a, 4 + k], y_places[2]))
        for copy in rights + lefts:
            copy.start()
        heres.append((rights, lefts))
    for a, (r, n) in enumerate(W_SHAPES):
        rights, lefts = heres[a]
        passed = []
        rights[0].wait()
        ref = row_part(a, z - 1, 0)
        passed.append(remote(ref, ref, a3_s.at[a, 0], a3_r.at[a, 0], z_places[0]))
        lefts[0].wait()
        ref = row_part(a, z + 1, 1)
        passed.append(remote(ref, ref, a3_s.at[a, 1], a3_r.at[a, 1], z_places[2]))
        for k in range(2):
            rights[2 + k].wait()
            ref = column_part(a, y - 1, k)
            passed.append(remote(ref, ref, b3_s.at[a, k], b3_r.at[a, k], y_places[0]))
            lefts[2 + k].wait()
            ref = column_part(a, y + 1, 3 - k)
            passed.append(remote(ref, ref, b3_s.at[a, 2 + k], b3_r.at[a, 2 + k], y_places[2]))
        for copy in passed:
            copy.start()
        for copy in rights[1:2] + rights[4:] + lefts[1:2] + lefts[4:] + passed:
            copy.wait()
        x_directs[2 * a].wait()
        x_directs[2 * a + 1].wait()
        whole = outs[a].at[rows(xj * r, r)]
        copy = remote(whole, whole, f_s.at[a], f_r.at[a], c_place)
        copy.start()
        waits.append(copy)
    for copy in waits:
        copy.wait()


def gather_weights(weights, docs):
    dma = pltpu.SemaphoreType.DMA
    outs = [jax.ShapeDtypeStruct((4 * r, n), jnp.bfloat16) for r, n in W_SHAPES]
    return pl.pallas_call(
        weights_kernel,
        out_shape=outs + [jax.ShapeDtypeStruct((NR, 8, 128), jnp.int32)],
        in_specs=[pl.BlockSpec(memory_space=pl.ANY)] * 4 + vmem_specs(1),
        out_specs=[pl.BlockSpec(memory_space=pl.ANY)] * 4 + vmem_specs(1),
        scratch_shapes=[pltpu.VMEM(shape, jnp.bfloat16) for shape in W_SHAPES]
        + [dma((4,))] * 12
        + [dma((4, 3))] * 4
        + [dma((4, 4))] * 2
        + [dma((4, 8))] * 2
        + [dma((4, 2))] * 2
        + [dma((4, 4))] * 2
        + [dma((3,))] * 4,
        compiler_params=pltpu.CompilerParams(
            collective_id=1, has_side_effects=True, vmem_limit_bytes=VMEM_BYTES
        ),
        name="gather_weights",
    )(*weights, docs)


def lane_mask(shape, micro):
    lane = lax.broadcasted_iota(jnp.int32, shape, len(shape) - 1)
    return (lane >= HD) if micro else (lane < HD)


def allowed_block(n0, n2, first_query, queries, keys):
    i = lax.broadcasted_iota(jnp.int32, (queries, keys), 0) + first_query
    j = lax.broadcasted_iota(jnp.int32, (queries, keys), 1)
    row = lax.broadcasted_iota(jnp.int32, (queries, 1), 0) + first_query
    start = jnp.where(row >= n2, n2, jnp.where(row >= n0, n0, 0))
    return (j <= i) & (j >= start)


def scores_of(q, k, micro, allowed):
    zero = jnp.zeros((), jnp.bfloat16)
    q = jnp.where(lane_mask(q.shape, micro), q, zero)
    s = lax.dot_general(q, k, (((1,), (1,)), ((), ())), preferred_element_type=jnp.float32)
    return jnp.where(allowed, s * SCALE, masked_score)


def take(x, entry, start, count):
    return x[pl.ds(start, count), entry].reshape(count * TQ, 2 * HD)


def forward_kernel(bounds, x, q16, o, o16, lse, lse16):
    zero = jnp.zeros((), jnp.bfloat16)
    me = lax.axis_index("replica")

    def attend(q, k, v, micro, first_query):
        allowed = allowed_block(bounds[micro], bounds[2 + micro], first_query, q.shape[0], k.shape[0])
        s = scores_of(q, k, micro, allowed)
        largest = jnp.max(s, axis=-1, keepdims=True)
        e = jnp.exp(s - largest)
        summed = jnp.sum(e, axis=-1, keepdims=True)
        p = (e * (1.0 / summed)).astype(jnp.bfloat16)
        v = jnp.where(lane_mask(v.shape, micro), v, zero)
        return times(p, v), largest + jnp.log(summed)

    per = BQ // TQ
    for b in range(SEQ // BQ):
        count = (b + 1) * per
        q = take(x, 0, b * per, per)
        k = take(x, 1, 0, count)
        v = take(x, 2, 0, count)
        o0, l0 = attend(q, k, v, 0, b * BQ)
        o1, l1 = attend(q, k, v, 1, b * BQ)
        o[pl.ds(b * per, per)] = (o0 + o1).astype(jnp.bfloat16).reshape(per, TQ, 2 * HD)
        lse[pl.ds(b * BQ, BQ)] = jnp.where(lane_mask((BQ, 2 * HD), 0), l0, l1)
    q = q16[...]
    k = take(x, 3, 0, NR)
    v = take(x, 4, 0, NR)
    o0, l0 = attend(q, k, v, 0, me * TQ)
    o1, l1 = attend(q, k, v, 1, me * TQ)
    o16[...] = (o0 + o1).astype(jnp.bfloat16)
    lse16[...] = jnp.where(lane_mask((TQ, 2 * HD), 0), l0, l1)


def vmem_specs(count):
    return [pl.BlockSpec(memory_space=pltpu.VMEM)] * count


def attention_forward(bounds, x, q16):
    f32, bf16 = jnp.float32, jnp.bfloat16
    return pl.pallas_call(
        forward_kernel,
        out_shape=[
            jax.ShapeDtypeStruct((NR, TQ, 2 * HD), bf16),
            jax.ShapeDtypeStruct((TQ, 2 * HD), bf16),
            jax.ShapeDtypeStruct((SEQ, 2 * HD), f32),
            jax.ShapeDtypeStruct((TQ, 2 * HD), f32),
        ],
        in_specs=[pl.BlockSpec(memory_space=pltpu.SMEM)] + vmem_specs(2),
        out_specs=vmem_specs(4),
        compiler_params=pltpu.CompilerParams(vmem_limit_bytes=VMEM_BYTES),
        cost_estimate=cost(5),
        name="attention_forward",
    )(bounds, x, q16)


def backward_kernel(bounds, x, q16, lse, lse16, do, do16, dx, dq16, dk, dv):
    zero = jnp.zeros((), jnp.bfloat16)
    me = lax.axis_index("replica")
    bf16 = jnp.bfloat16

    def pull(q, k, v, grad, logs, micro, first_query):
        allowed = allowed_block(bounds[micro], bounds[2 + micro], first_query, q.shape[0], k.shape[0])
        s = scores_of(q, k, micro, allowed)
        soft = jnp.exp(s - logs[:, micro * HD : micro * HD + 1])
        grad = jnp.where(lane_mask(grad.shape, micro), grad, zero)
        dp = times_transposed(grad, v)
        along = jnp.sum(soft * dp, axis=-1, keepdims=True)
        ds = (soft * (dp - along)).astype(bf16)
        q = jnp.where(lane_mask(q.shape, micro), q, zero)
        k = jnp.where(lane_mask(k.shape, micro), k, zero)
        return times(ds, k), outer_sum(ds, q), outer_sum(soft.astype(bf16), grad)

    per = BQ // TQ
    for b in reversed(range(SEQ // BQ)):
        count = (b + 1) * per
        q = take(x, 0, b * per, per)
        k = take(x, 1, 0, count)
        v = take(x, 2, 0, count)
        grad = do[pl.ds(b * per, per)].reshape(BQ, 2 * HD)
        logs = lse[pl.ds(b * BQ, BQ)]
        q0, k0, v0 = pull(q, k, v, grad, logs, 0, b * BQ)
        q1, k1, v1 = pull(q, k, v, grad, logs, 1, b * BQ)
        dx[pl.ds(b * per, per), 0] = ((q0 + q1) * SCALE).astype(bf16).reshape(per, TQ, 2 * HD)
        keys = pl.ds(0, (b + 1) * BQ)
        if b == SEQ // BQ - 1:
            dk[keys] = k0 + k1
            dv[keys] = v0 + v1
        else:
            dk[keys] += k0 + k1
            dv[keys] += v0 + v1
    dx[:, 1] = (dk[...] * SCALE).astype(bf16).reshape(NR, TQ, 2 * HD)
    dx[:, 2] = dv[...].astype(bf16).reshape(NR, TQ, 2 * HD)
    q = q16[...]
    k = take(x, 3, 0, NR)
    v = take(x, 4, 0, NR)
    q0, k0, v0 = pull(q, k, v, do16[...], lse16[...], 0, me * TQ)
    q1, k1, v1 = pull(q, k, v, do16[...], lse16[...], 1, me * TQ)
    dq16[...] = ((q0 + q1) * SCALE).astype(bf16)
    dx[:, 3] = ((k0 + k1) * SCALE).astype(bf16).reshape(NR, TQ, 2 * HD)
    dx[:, 4] = (v0 + v1).astype(bf16).reshape(NR, TQ, 2 * HD)


def attention_backward(bounds, x, q16, lse, lse16, do, do16):
    f32, bf16 = jnp.float32, jnp.bfloat16
    return pl.pallas_call(
        backward_kernel,
        out_shape=[
            jax.ShapeDtypeStruct((NR, 5, TQ, 2 * HD), bf16),
            jax.ShapeDtypeStruct((TQ, 2 * HD), bf16),
        ],
        in_specs=[pl.BlockSpec(memory_space=pltpu.SMEM)] + vmem_specs(6),
        out_specs=vmem_specs(2),
        scratch_shapes=[pltpu.VMEM((SEQ, 2 * HD), f32), pltpu.VMEM((SEQ, 2 * HD), f32)],
        compiler_params=pltpu.CompilerParams(vmem_limit_bytes=VMEM_BYTES),
        cost_estimate=cost(8),
        name="attention_backward",
    )(bounds, x, q16, lse, lse16, do, do16)


QKV = 3 * D
ENTER_BLOCK, LEAVE_BLOCK, BACK_ENTER_BLOCK = 1664, 2176, 640
LEFT_AT, LEFT_WIDTH = (0, 384, 768, 1152), 2304
EARLY_AT, EARLY_WIDTH = (0, 4352, 5504), 6656
LATE_WIDTH = 3328
SMALL = 1152


def low_lanes(shape):
    return lane_mask(shape, 0)


def to_blocks(upper, lower, odd):
    half = low_lanes(upper.shape)
    if odd:
        return jnp.where(half, pltpu.roll(upper, HD, 1), lower)
    return jnp.where(half, upper, pltpu.roll(lower, HD, 1))


def from_blocks(first, second):
    half = low_lanes(first.shape)
    upper = jnp.where(half, first, pltpu.roll(second, HD, 1))
    return upper, jnp.where(half, pltpu.roll(first, HD, 1), second)


def lines(start, count):
    return pl.ds(start, count)


def enter_kernel(x, gains, biases, w, message, q16, act, mixed):
    i = pl.program_id(0)

    @pl.when(i == 0)
    def _():
        normed, _, _ = layer_norm(x[...].astype(jnp.float32), gains[0:1], biases[0:1])
        act[...] = normed.astype(jnp.bfloat16)

    mixed[i] = times(act[...], w[...])

    @pl.when(i == pl.num_programs(0) - 1)
    def _():
        for b in range(3 * H):
            kind, head = divmod(b, H)
            i, t = divmod(b // 2, ENTER_BLOCK // 128)
            part = pl.ds(t * 128, 128)
            block = to_blocks(mixed[i, 0:TQ, part], mixed[i, TQ : 2 * TQ, part], b % 2)
            if kind != 1:
                row = 1 if kind == 0 else 2
                shift = biases[row : row + 1, head * HD : (head + 1) * HD]
                block = block + jnp.concatenate([shift, shift], axis=1)
            block = block.astype(jnp.bfloat16)
            if head < H - 1:
                message[head, kind * TQ : (kind + 1) * TQ] = block
            elif kind == 0:
                q16[...] = block
            else:
                for p in range(NR):
                    message[p, (kind + 2) * TQ : (kind + 3) * TQ] = block


def fixed(shape):
    return pl.BlockSpec(shape, lambda i: (0,) * len(shape))


def enter(x, gains, biases, w_qkv):
    bf16 = jnp.bfloat16
    steps = -(-QKV // ENTER_BLOCK)
    shapes = [(NR, 5 * TQ, 2 * HD), (TQ, 2 * HD), (2 * TQ, D)]
    return pl.pallas_call(
        enter_kernel,
        grid=(steps,),
        out_shape=[jax.ShapeDtypeStruct(shape, bf16) for shape in shapes],
        in_specs=[
            fixed(x.shape),
            fixed(gains.shape),
            fixed(biases.shape),
            pl.BlockSpec((D, ENTER_BLOCK), lambda i: (0, i)),
        ],
        out_specs=[fixed(shape) for shape in shapes],
        scratch_shapes=[pltpu.VMEM((steps, 2 * TQ, ENTER_BLOCK), jnp.float32)],
        compiler_params=pltpu.CompilerParams(vmem_limit_bytes=VMEM_BYTES),
        cost_estimate=cost(5),
        name="enter",
    )(x, gains, biases, w_qkv)


CURVE = 0.044715
ROOT = 0.7978845608028654


def leave_kernel(
    x, o, o16, act1, gains, biases, up_shift, w_out, w_up, w_down, result, resid, pre, lefts, act2, total
):
    i = pl.program_id(0)
    bf16 = jnp.bfloat16

    @pl.when(i == 0)
    def _():
        tiles = []
        for t in range(H // 2 + 1):
            first = o[2 * t] if 2 * t < H - 1 else o16[...]
            second = o[2 * t + 1] if 2 * t + 1 < H - 1 else o16[...]
            upper, lower = from_blocks(first.astype(jnp.float32), second.astype(jnp.float32))
            tiles.append(jnp.concatenate([upper, lower], axis=0))
        attended = jnp.concatenate(tiles, axis=1)[:, :D].astype(bf16)
        r = x[...].astype(jnp.float32) + times(attended, w_out[...]) + biases[3:4]
        resid[...] = r
        normed, _, _ = layer_norm(r, gains[1:2], biases[4:5])
        act2[...] = normed.astype(bf16)
        for s in range(4):
            part = slice(s * 272, (s + 1) * 272)
            for at, value in zip(LEFT_AT, (act1, attended, act2)):
                lefts[s, :, at : at + 272] = value[:, part]
        total[...] = r + biases[5:6]

    u = times(act2[...], w_up[...]) + up_shift[...]
    pre[...] = u
    g = (0.5 * u * (1.0 + jnp.tanh(ROOT * (u + CURVE * u * u * u)))).astype(bf16)
    for s in range(2):
        lefts[2 * i + s, :, LEFT_AT[3] : LEFT_AT[3] + D] = g[:, s * D : (s + 1) * D]
    total[...] += times(g, w_down[...])

    @pl.when(i == pl.num_programs(0) - 1)
    def _():
        result[...] = total[...].astype(bf16)


def leave(x, o, o16, act1, gains, biases, up_shift, weights):
    _, w_out, w_up, w_down = weights
    f32, bf16 = jnp.float32, jnp.bfloat16
    rows = 2 * TQ
    return pl.pallas_call(
        leave_kernel,
        grid=(FF // LEAVE_BLOCK,),
        out_shape=[
            jax.ShapeDtypeStruct((rows, D), bf16),
            jax.ShapeDtypeStruct((rows, D), f32),
            jax.ShapeDtypeStruct((rows, FF), f32),
            jax.ShapeDtypeStruct((4, rows, LEFT_WIDTH), bf16),
        ],
        in_specs=[
            fixed(x.shape),
            fixed(o.shape),
            fixed(o16.shape),
            fixed(act1.shape),
            fixed(gains.shape),
            fixed(biases.shape),
            pl.BlockSpec((1, LEAVE_BLOCK), lambda i: (0, i)),
            fixed(w_out.shape),
            pl.BlockSpec((D, LEAVE_BLOCK), lambda i: (0, i)),
            pl.BlockSpec((LEAVE_BLOCK, D), lambda i: (i, 0)),
        ],
        out_specs=[
            fixed((rows, D)),
            fixed((rows, D)),
            pl.BlockSpec((rows, LEAVE_BLOCK), lambda i: (0, i)),
            fixed((4, rows, LEFT_WIDTH)),
        ],
        scratch_shapes=[pltpu.VMEM((rows, D), bf16), pltpu.VMEM((rows, D), f32)],
        compiler_params=pltpu.CompilerParams(vmem_limit_bytes=VMEM_BYTES),
        cost_estimate=cost(12),
        name="leave",
    )(x, o, o16, act1, gains, biases, up_shift, w_out, w_up, w_down)


def column_sum(value):
    return jnp.sum(value, axis=0, keepdims=True)


def back_leave_kernel(
    dy, resid, pre, gains, w_out, w_up, w_down, early, grad_resid, do, do16, sums, total
):
    i = pl.program_id(0)
    f32, bf16 = jnp.float32, jnp.bfloat16

    @pl.when(i == 0)
    def _():
        total[...] = jnp.zeros_like(total)

    u = pre[...]
    grad_hidden = times_transposed(dy[...], w_down[...])
    t = jnp.tanh(ROOT * (u + CURVE * u * u * u))
    slope = 0.5 * (1.0 + t) + 0.5 * u * (1.0 - t * t) * (ROOT * (1.0 + 3.0 * CURVE * u * u))
    du = (grad_hidden * slope).astype(bf16)
    early[:, pl.ds(pl.multiple_of(i * LEAVE_BLOCK, 128), LEAVE_BLOCK)] = du
    du_sum = column_sum(du.astype(f32))
    for s in range(2):
        sums[pl.ds(4 + 2 * i + s, 1), 0:D] = du_sum[:, s * D : (s + 1) * D]
    total[...] += times_transposed(du, w_up[...])

    @pl.when(i == pl.num_programs(0) - 1)
    def _():
        da2 = total[...]
        _, normed, inverse = layer_norm(resid[...], gains[1:2], 0.0)
        dr = dy[...].astype(f32) + norm_back(da2, normed, inverse, gains[1:2])
        grad_resid[...] = dr
        db = dr.astype(bf16)
        for at in EARLY_AT[1:]:
            early[:, at + 1024 : at + 1152] = jnp.zeros((2 * TQ, 128), bf16)
        early[:, EARLY_AT[1] : EARLY_AT[1] + D] = db
        early[:, EARLY_AT[2] : EARLY_AT[2] + D] = dy[...]
        sums[0:1, 0:D] = column_sum(da2 * normed)
        sums[1:2, 0:D] = column_sum(da2)
        sums[2:3, 0:D] = column_sum(db.astype(f32))
        sums[3:4, 0:D] = column_sum(dy[...].astype(f32))
        heads = times_transposed(db, w_out[...])
        heads = jnp.concatenate([heads, jnp.zeros((2 * TQ, HD), f32)], axis=1)
        for b in range(H):
            tile = heads[:, (b // 2) * 128 : (b // 2 + 1) * 128]
            block = to_blocks(tile[0:TQ], tile[TQ : 2 * TQ], b % 2).astype(bf16)
            if b < H - 1:
                do[b] = block
            else:
                do16[...] = block


def back_leave(dy, resid, pre, gains, weights):
    _, w_out, w_up, w_down = weights
    f32, bf16 = jnp.float32, jnp.bfloat16
    rows = 2 * TQ
    shapes = [(rows, EARLY_WIDTH), (rows, D), (NR, TQ, 2 * HD), (TQ, 2 * HD), (8, SMALL)]
    types = [bf16, f32, bf16, bf16, f32]
    return pl.pallas_call(
        back_leave_kernel,
        grid=(FF // LEAVE_BLOCK,),
        out_shape=[jax.ShapeDtypeStruct(shape, t) for shape, t in zip(shapes, types)],
        in_specs=[
            fixed((rows, D)),
            fixed((rows, D)),
            pl.BlockSpec((rows, LEAVE_BLOCK), lambda i: (0, i)),
            fixed(gains.shape),
            fixed(w_out.shape),
            pl.BlockSpec((D, LEAVE_BLOCK), lambda i: (0, i)),
            pl.BlockSpec((LEAVE_BLOCK, D), lambda i: (i, 0)),
        ],
        out_specs=[fixed(shape) for shape in shapes],
        scratch_shapes=[pltpu.VMEM((rows, D), f32)],
        compiler_params=pltpu.CompilerParams(vmem_limit_bytes=VMEM_BYTES),
        cost_estimate=cost(14),
        name="back_leave",
    )(dy, resid, pre, gains, w_out, w_up, w_down)


def back_enter_kernel(x, back, dq16, grad_resid, before, gains, w, late, grad_in, sums, parts):
    i = pl.program_id(0)
    f32, bf16 = jnp.float32, jnp.bfloat16

    @pl.when(i == 0)
    def _():
        def last(kind):
            total = back[0, (kind + 2) * TQ : (kind + 3) * TQ].astype(f32)
            for p in range(1, NR):
                total = total + back[p, (kind + 2) * TQ : (kind + 3) * TQ].astype(f32)
            return total

        def block(b):
            kind, head = divmod(b, H)
            if head < H - 1:
                return back[head, kind * TQ : (kind + 1) * TQ].astype(f32)
            return dq16[...].astype(f32) if kind == 0 else last(kind)

        for t in range(3 * H // 2 + 1):
            first = block(2 * t)
            second = block(2 * t + 1) if 2 * t + 1 < 3 * H else jnp.zeros_like(first)
            upper, lower = from_blocks(first, second)
            late[0:TQ, t * 128 : (t + 1) * 128] = upper.astype(bf16)
            late[TQ : 2 * TQ, t * 128 : (t + 1) * 128] = lower.astype(bf16)

    parts[i] = times_transposed(late[:, 0:QKV], w[...])

    @pl.when(i == pl.num_programs(0) - 1)
    def _():
        da1 = jnp.concatenate([parts[k] for k in range(parts.shape[0])], axis=1)[:, :D]
        _, normed, inverse = layer_norm(x[...].astype(f32), gains[0:1], 0.0)
        dx = grad_resid[...] + norm_back(da1, normed, inverse, gains[0:1])
        grad_in[...] = dx.astype(bf16)
        sums[...] = jnp.zeros_like(sums)
        sums[0:1, 0:D] = column_sum(da1 * normed)
        sums[1:2, 0:D] = column_sum(da1)
        sums[2:3, 0:D] = column_sum(late[:, 0:D].astype(f32))
        sums[3:4, 0:D] = column_sum(late[:, 2 * D : QKV].astype(f32))
        sums[4:12, 0:D] = before[:, 0:D]


def back_enter(x, back, dq16, grad_resid, before, gains, w_qkv):
    f32, bf16 = jnp.float32, jnp.bfloat16
    rows = 2 * TQ
    steps = -(-D // BACK_ENTER_BLOCK)
    return pl.pallas_call(
        back_enter_kernel,
        grid=(steps,),
        out_shape=[
            jax.ShapeDtypeStruct((rows, LATE_WIDTH), bf16),
            jax.ShapeDtypeStruct((rows, D), bf16),
            jax.ShapeDtypeStruct((16, SMALL), f32),
        ],
        in_specs=[
            fixed(x.shape),
            fixed(back.shape),
            fixed(dq16.shape),
            fixed(grad_resid.shape),
            fixed(before.shape),
            fixed(gains.shape),
            pl.BlockSpec((BACK_ENTER_BLOCK, QKV), lambda i: (i, 0)),
        ],
        out_specs=[fixed((rows, LATE_WIDTH)), fixed((rows, D)), fixed((16, SMALL))],
        scratch_shapes=[pltpu.VMEM((steps, rows, BACK_ENTER_BLOCK), f32)],
        compiler_params=pltpu.CompilerParams(vmem_limit_bytes=VMEM_BYTES),
        cost_estimate=cost(5),
        name="back_enter",
    )(x, back, dq16, grad_resid, before, gains, w_qkv)


AT_OUT, AT_UP, AT_DOWN, DOWN_STEP = 3328, 4480, 8832, 1152


def weight_sums_kernel(
    l0, l1, l2, l3, e0, e1, e2, late, small, out,
    lefts, early, mixed, got, g, tr, ins, ad, part, mid, fin,
    loc, late_s, late_r, small_s, small_r,
    p_s, p_r, q_s, q_r, m_s, m_r, n_s, n_r, e_s, e_r, w_s, w_r, last,
):
    f32, bf16 = jnp.float32, jnp.bfloat16
    rows = 2 * TQ
    j = lax.axis_index("shard")
    me = lax.axis_index("replica")
    z, y = me // 4, lax.rem(me, 4)
    xj = lax.rem(j + 2, 4)
    cj = j + 1 - 2 * lax.rem(j, 2)
    places = [{"shard": xj}, {"shard": cj}, {"shard": lax.rem(cj + 2, 4)}]
    y_places = [{"replica": y_peer(me, d)} for d in (1, 2, 3)]
    z_places = [{"replica": z_peer(me, d)} for d in (1, 2, 3)]
    greet(places + y_places + z_places)

    def slot(ref, k):
        return ref.at[pl.ds(k * rows, rows)]

    across = remote(late, slot(mixed, 1), late_s.at[0], late_r.at[0], places[0])
    across.start()
    beside = remote(late, slot(mixed, 2), late_s.at[1], late_r.at[1], places[1])
    beside.start()
    early_relay = remote(e1, slot(early, 3), late_s.at[3], late_r.at[3], places[1])
    early_relay.start()
    smalls = [remote(small, got.at[k], small_s.at[k], small_r.at[k], places[k]) for k in range(3)]
    for copy in smalls:
        copy.start()
    loads = [pltpu.make_async_copy(late, slot(mixed, 0), loc.at[0])]
    loads.append(pltpu.make_async_copy(l0.at[j], slot(lefts, 0), loc.at[1]))
    for k, ref in enumerate((l1, l2, l3)):
        loads.append(pltpu.make_async_copy(ref, slot(lefts, k + 1), loc.at[2 + k]))
    for k, ref in enumerate((e0, e1, e2)):
        loads.append(pltpu.make_async_copy(ref, slot(early, k), loc.at[5 + k]))
    for copy in loads:
        copy.start()
    for copy in loads:
        copy.wait()
    early_relay.wait()

    def stripe(left_at, right, right_at, at, columns, width):
        @pl.loop(0, columns // width)
        def _(i):
            take_at = pl.ds(pl.multiple_of(right_at + i * width, 128), width)
            put_at = pl.ds(pl.multiple_of(at + i * width, 128), width)
            product = outer_sum(lefts[:, left_at : left_at + 272], right[:, take_at])
            g[0:272, put_at] = product.astype(bf16)

    stripe(LEFT_AT[2], early, EARLY_AT[0], AT_UP, FF, 2176)
    g[0:272, AT_OUT:AT_UP] = outer_sum(
        lefts[:, LEFT_AT[1] : LEFT_AT[1] + 272], early[:, EARLY_AT[1] : EARLY_AT[2]]
    ).astype(bf16)
    for s in range(4):
        at = AT_DOWN + s * DOWN_STEP
        first = LEFT_AT[3] + s * 272
        g[0:272, at : at + DOWN_STEP] = outer_sum(
            lefts[:, first : first + 272], early[:, EARLY_AT[2] : EARLY_WIDTH]
        ).astype(bf16)
    filled = AT_DOWN + 4 * DOWN_STEP
    g[0:272, filled:] = jnp.zeros((272, NR * PIECE - filled), bf16)
    g[272:RED_ROWS] = jnp.zeros((RED_ROWS - 272, NR * PIECE), bf16)

    firsts, seconds = (y_places, z_places), (z_places, y_places)
    here, there = (y, z), (z, y)

    def at(side, first, second):
        piece = 4 * second + lax.rem(first + 4, 4)
        return (pl.ds(side * HALF, HALF), pl.ds(pl.multiple_of(piece * PIECE, 128), PIECE))

    def piece_of(ref, side, first, second):
        return ref.at[at(side, first, second)]

    def value_of(side, first, second):
        return g[at(side, first, second)].astype(f32)

    opened, direct, added = {}, {}, {}

    def open_piece(s, k):
        t, right, left = here[s], firsts[s][0], firsts[s][2]
        copy = remote(piece_of(g, s, t + 2, k), tr.at[s, k], p_s.at[s, k], p_r.at[s, k], right if k < 2 else left)
        copy.start()
        opened[s, k] = copy

    def direct_piece(s, k):
        t, right, left = here[s], firsts[s][0], firsts[s][2]
        if k < 2:
            copy = remote(piece_of(g, s, t - 1, k), ins.at[s, 1, k], p_s.at[s, 4 + k], p_r.at[s, 4 + k], left)
        else:
            copy = remote(piece_of(g, s, t + 1, k), ins.at[s, 0, k], p_s.at[s, 4 + k], p_r.at[s, 4 + k], right)
        copy.start()
        direct[s, k] = copy

    def add_piece(s, k):
        t, right, left = here[s], firsts[s][0], firsts[s][2]
        opened[s, k].wait()
        mine = value_of(s, t + 1 if k < 2 else t - 1, k)
        ad[s, k] = (tr[s, k].astype(f32) + mine).astype(bf16)
        to, side = (right, 0) if k < 2 else (left, 1)
        copy = remote(ad.at[s, k], ins.at[s, side, k], q_s.at[s, k], q_r.at[s, k], to)
        copy.start()
        added[s, k] = copy

    for k in (1, 2, 3):
        for s in range(2):
            open_piece(s, k)
    for k in (1, 2, 3):
        for s in range(2):
            direct_piece(s, k)
    for k in (1, 2):
        for s in range(2):
            add_piece(s, k)
    across.wait()
    relay = remote(slot(mixed, 1), slot(mixed, 3), late_s.at[2], late_r.at[2], places[1])
    relay.start()
    beside.wait()
    for s in range(2):
        add_piece(s, 3)
    relay.wait()
    stripe(LEFT_AT[0], mixed, 0, 0, LATE_WIDTH, 1664)
    for copy in smalls:
        copy.wait()
    g[272:RED_ROWS, 0:SMALL] = (small[...] + got[0] + got[1] + got[2]).astype(bf16)
    for s in range(2):
        open_piece(s, 0)
        direct_piece(s, 0)
    for s in range(2):
        add_piece(s, 0)

    middles = []
    for s in range(2):
        for k in range(4):
            direct[s, k].wait()
            added[s, k].wait()
            part[s, k] = (value_of(s, here[s], k) + ins[s, 0, k].astype(f32) + ins[s, 1, k].astype(f32)).astype(bf16)
        group = []
        for i in range(3):
            to = lax.rem(there[s] + 1 + i, 4)
            group.append(remote(part.at[s, to], mid.at[s, i], m_s.at[s, i], m_r.at[s, i], seconds[s][i]))
        for copy in group:
            copy.start()
        middles.append(group)
    backs = []
    for s in range(2):
        for copy in middles[s]:
            copy.wait()
        total = part[s, there[s]].astype(f32)
        for i in range(3):
            total = total + mid[s, i].astype(f32)
        fin[s] = total.astype(bf16)
        where = piece_of(out, s, here[s], there[s])
        group = [remote(fin.at[s], where, n_s.at[s, i], n_r.at[s, i], seconds[s][i]) for i in range(3)]
        group.append(pltpu.make_async_copy(fin.at[s], where, last.at[s]))
        for copy in group:
            copy.start()
        backs.append(group)
    to_rights, to_lefts = [], []
    for s in range(2):
        t, right, left = here[s], firsts[s][0], firsts[s][2]
        for copy in backs[s]:
            copy.wait()
        to_right, to_left = [], []
        for k in range(4):
            ref = piece_of(out, s, t, k)
            to_right.append(remote(ref, ref, e_s.at[s, k], e_r.at[s, k], right))
            ref = piece_of(out, s, t, 3 - k)
            to_left.append(remote(ref, ref, e_s.at[s, 4 + k], e_r.at[s, 4 + k], left))
        for k in range(4):
            to_right[k].start()
            to_left[k].start()
        to_rights.append(to_right)
        to_lefts.append(to_left)
    passed = []
    for k in range(2):
        for s in range(2):
            t, right, left = here[s], firsts[s][0], firsts[s][2]
            to_rights[s][k].wait()
            ref = piece_of(out, s, t - 1, k)
            copy = remote(ref, ref, w_s.at[s, k], w_r.at[s, k], right)
            copy.start()
            passed.append(copy)
            to_lefts[s][k].wait()
            ref = piece_of(out, s, t + 1, 3 - k)
            copy = remote(ref, ref, w_s.at[s, 2 + k], w_r.at[s, 2 + k], left)
            copy.start()
            passed.append(copy)
    for s in range(2):
        for copy in to_rights[s][2:] + to_lefts[s][2:]:
            copy.wait()
    for copy in passed:
        copy.wait()


def weight_sums(lefts, early, late, small):
    dma = pltpu.SemaphoreType.DMA
    f32, bf16 = jnp.float32, jnp.bfloat16
    anywhere = pl.BlockSpec(memory_space=pl.ANY)
    piece = (HALF, PIECE)
    return pl.pallas_call(
        weight_sums_kernel,
        out_shape=jax.ShapeDtypeStruct((RED_ROWS, NR * PIECE), bf16),
        in_specs=[anywhere] * 8 + vmem_specs(1),
        out_specs=anywhere,
        scratch_shapes=[
            pltpu.VMEM((8 * TQ, LEFT_WIDTH), bf16),
            pltpu.VMEM((8 * TQ, EARLY_WIDTH), bf16),
            pltpu.VMEM((8 * TQ, LATE_WIDTH), bf16),
            pltpu.VMEM((3, 16, SMALL), f32),
            pltpu.VMEM((RED_ROWS, NR * PIECE), bf16),
            pltpu.VMEM((2, 4) + piece, bf16),
            pltpu.VMEM((2, 2, 4) + piece, bf16),
            pltpu.VMEM((2, 4) + piece, bf16),
            pltpu.VMEM((2, 4) + piece, bf16),
            pltpu.VMEM((2, 3) + piece, bf16),
            pltpu.VMEM((2,) + piece, bf16),
            dma((8,)),
            dma((4,)), dma((4,)), dma((3,)), dma((3,)),
        ]
        + [dma((2, 8))] * 2
        + [dma((2, 4))] * 2
        + [dma((2, 3))] * 4
        + [dma((2, 8))] * 2
        + [dma((2, 4))] * 2
        + [dma((2,))],
        compiler_params=pltpu.CompilerParams(
            collective_id=2, has_side_effects=True, vmem_limit_bytes=VMEM_BYTES
        ),
        name="weight_sums",
    )(*lefts, *early, late, small)


def widen_kernel(g, qkv, out, up, down):
    f32 = jnp.float32
    qkv[...] = g[:, 0:QKV].astype(f32)
    out[...] = g[:, AT_OUT : AT_OUT + D].astype(f32)
    up[...] = g[:, AT_UP : AT_UP + FF].astype(f32)
    for s in range(4):
        at = AT_DOWN + s * DOWN_STEP
        down[s] = g[:, at : at + D].astype(f32)


def widen(g):
    f32 = jnp.float32
    return pl.pallas_call(
        widen_kernel,
        grid=(6,),
        out_shape=[
            jax.ShapeDtypeStruct((272, QKV), f32),
            jax.ShapeDtypeStruct((272, D), f32),
            jax.ShapeDtypeStruct((272, FF), f32),
            jax.ShapeDtypeStruct((4, 272, D), f32),
        ],
        in_specs=[pl.BlockSpec((48, NR * PIECE), lambda i: (i, 0))],
        out_specs=[
            pl.BlockSpec((48, QKV), lambda i: (i, 0)),
            pl.BlockSpec((48, D), lambda i: (i, 0)),
            pl.BlockSpec((48, FF), lambda i: (i, 0)),
            pl.BlockSpec((4, 48, D), lambda i: (0, i, 0)),
        ],
        compiler_params=pltpu.CompilerParams(vmem_limit_bytes=VMEM_BYTES),
        name="widen",
    )(g)


def layer_forward(x, bounds, gains, biases, up_shift, weights):
    message, q16, act1 = enter(x, gains, biases, weights[0])
    whole = swap(message, 3).reshape(NR, 5, TQ, 2 * HD)
    o, o16, lse, lse16 = attention_forward(bounds, whole, q16)
    result, resid, pre, lefts = leave(x, swap(o, 4), o16, act1, gains, biases, up_shift, weights)
    return result, (whole, q16, lse, lse16, resid, pre), lefts


def layer_backward(dy, x, kept, bounds, gains, weights, early_tie=None, late_tie=None):
    whole, q16, lse, lse16, resid, pre = kept
    early, grad_resid, do, do16, sums = back_leave(dy, resid, pre, gains, weights)
    dx, dq16 = attention_backward(bounds, whole, q16, lse, lse16, swap(do, 4), do16)
    dx, early_tie = lax.optimization_barrier((dx, early_tie))
    back = swap(dx.reshape(NR, 5 * TQ, 2 * HD), 3)
    late, grad_in, small = back_enter(x, back, dq16, grad_resid, sums, gains, weights[0])
    grad_in, late_tie = lax.optimization_barrier((grad_in, late_tie))
    return grad_in, early, late, small, early_tie, late_tie


X_ROUTE = [(j, j ^ 2) for j in range(4)]
C_ROUTE = [(j, j ^ 1) for j in range(4)]


CX_ROUTE = [(j, j ^ 3) for j in range(4)]


def everyone(value):
    return value, lax.ppermute(value, "shard", X_ROUTE), lax.ppermute(value, "shard", C_ROUTE)


def own_columns(cut):
    j = lax.axis_index("shard")

    def of(shard):
        return lax.dynamic_index_in_dim(cut, shard, 0, keepdims=False)

    across, beside = lax.rem(j + 2, 4), j + 1 - 2 * lax.rem(j, 2)
    return (
        cut,
        lax.ppermute(of(across), "shard", X_ROUTE),
        lax.ppermute(of(beside), "shard", C_ROUTE),
        lax.ppermute(of(lax.rem(beside + 2, 4)), "shard", CX_ROUTE),
    )


def shards(tokens, cotangent, doc_ids, gains, biases, up_bias, w_qkv, w_out, w_up, w_down):
    is_first = lax.axis_index("section") == 0
    ids = doc_ids[:, 0]
    counts = jnp.stack([jnp.sum((ids == n).astype(jnp.int32), axis=1) for n in (0, 2)])
    counts = jnp.pad(counts, ((0, 6), (0, 126)))
    *weights, counts = gather_weights((w_qkv[0], w_out[0], w_up[0], w_down[0]), counts)
    counts = jnp.sum(counts[:, :2, :2], axis=0)
    bounds = jnp.concatenate([counts[0], SEQ - counts[1]])
    gains, biases = gains[0], biases[0]
    own_in = tokens.reshape(2 * TQ, D)
    own_cot = cotangent.reshape(2 * TQ, D)
    result, _, _ = layer_forward(own_in, bounds, gains, biases, up_bias, weights)
    inbox = lax.ppermute(result, "section", [(0, 1)])
    inputs = jnp.where(is_first, own_in, inbox)
    layer_out, kept, lefts = layer_forward(inputs, bounds, gains, biases, up_bias, weights)
    lefts = own_columns(lefts)
    grad_in, _, _, _, sooner, later = layer_backward(
        own_cot, inputs, kept, bounds, gains, weights, lefts[1:3], lefts[3]
    )
    lefts = (lefts[0], *sooner, later)
    inbox = lax.ppermute(grad_in, "section", [(1, 0)])
    dy = jnp.where(is_first, inbox, own_cot)
    grad_in, early, late, small, _, _ = layer_backward(dy, inputs, kept, bounds, gains, weights)
    summed = weight_sums(lefts, everyone(early), late, small)
    qkv, out, up, down = widen(summed)
    small = summed[272:RED_ROWS, :D].astype(jnp.float32)
    return (
        layer_out.reshape(1, 2, 1, TQ, D),
        grad_in.reshape(1, 2, 1, TQ, D),
        jnp.stack([small[0], small[4]])[None],
        jnp.stack([small[k] for k in (1, 2, 3, 6, 5, 7)])[None],
        small[8:12].reshape(1, FF),
        qkv[None],
        out[None],
        up[None],
        down.reshape(1, 1088, D),
    )


def solution(mesh):
    placed = (
        P(None, "shard", "replica", None),
        P(None, "shard", "replica", None),
        P(None, "shard", "replica"),
        P("section", None, None),
        P("section", None, None),
        P("section", None),
        P("section", "shard", None),
        P("section", "shard", None),
        P("section", "shard", None),
        P("section", "shard", None),
    )
    return jax.shard_map(
        shards,
        mesh=mesh,
        in_specs=placed,
        out_specs=(
            P("section", None, "shard", "replica", None),
            P("section", None, "shard", "replica", None),
            P("section", None, None),
            P("section", None, None),
            P("section", None),
            P("section", "shard", None),
            P("section", "shard", None),
            P("section", "shard", None),
            P("section", "shard", None),
        ),
        check_vma=False,
    )
```

```python
import functools

import jax
import jax.numpy as jnp
from jax import lax
from jax.experimental import pallas as pl
from jax.experimental.pallas import tpu as pltpu
from jax.sharding import PartitionSpec as P

MESH = pl.DeviceIdType.MESH
H = 17
HD = 64
TQ = 64
SEQ = 1024
NR = 16
D = 1088
FF = 4352
SCALE = HD ** (-0.5)
epsilon = 1e-05
masked_score = -1e30
BQ = 256
PIECE = 896
VMEM_BYTES = 58 * 1024 * 1024
RED_ROWS = 256
HALF = 128


def layer_norm(values, gain_row, shift_row):
    centre = values - jnp.mean(values, axis=-1, keepdims=True)
    inverse = lax.rsqrt(jnp.mean(centre * centre, axis=-1, keepdims=True) + epsilon)
    normed = centre * inverse
    return (normed * gain_row + shift_row, normed, inverse)


def norm_back(grad_normed_out, normed, inverse, gain_row):
    scaled = grad_normed_out * gain_row
    middle = jnp.mean(scaled, axis=-1, keepdims=True)
    slope = jnp.mean(scaled * normed, axis=-1, keepdims=True)
    return inverse * (scaled - middle - normed * slope)


def times(left, right):
    return jnp.dot(left, right, preferred_element_type=jnp.float32)


def times_transposed(left, right):
    return lax.dot_general(
        left, right, (((1,), (1,)), ((), ())), preferred_element_type=jnp.float32
    )


def outer_sum(left, right):
    return lax.dot_general(
        left, right, (((0,), (0,)), ((), ())), preferred_element_type=jnp.float32
    )


def y_peer(me, d):
    return (me // 4) * 4 + lax.rem(lax.rem(me, 4) + d, 4)


def z_peer(me, d):
    return lax.rem(me + 4 * d, NR)


def any_peer(me, d):
    return lax.rem(me // 4 + d // 4, 4) * 4 + lax.rem(lax.rem(me, 4) + d % 4, 4)


def remote(src, dst, send, recv, where):
    return pltpu.make_async_remote_copy(
        src_ref=src,
        dst_ref=dst,
        send_sem=send,
        recv_sem=recv,
        device_id=where,
        device_id_type=MESH,
    )


def cost(microseconds):
    return pl.CostEstimate(flops=0, bytes_accessed=int(microseconds * 3.5e6), transcendentals=0)


def greet(places):
    barrier = pltpu.get_barrier_semaphore()
    for where in places:
        pl.semaphore_signal(barrier, inc=1, device_id=where, device_id_type=MESH)
    pl.semaphore_wait(barrier, len(places))


def swap_kernel(x, o, send, recv, local):
    me = lax.axis_index("replica")
    greet([{"replica": any_peer(me, d)} for d in range(1, NR)])
    copies = []
    for d in range(1, NR):
        to = any_peer(me, d)
        copy = remote(x.at[to], o.at[me], send.at[d], recv.at[d], {"replica": to})
        copy.start()
        copies.append(copy)
    own = pltpu.make_async_copy(x.at[me], o.at[me], local)
    own.start()
    own.wait()
    for copy in copies:
        copy.wait()


def swap(x, collective_id):
    return pl.pallas_call(
        swap_kernel,
        out_shape=jax.ShapeDtypeStruct(x.shape, x.dtype),
        in_specs=[pl.BlockSpec(memory_space=pl.ANY)],
        out_specs=pl.BlockSpec(memory_space=pl.ANY),
        scratch_shapes=[
            pltpu.SemaphoreType.DMA((NR,)),
            pltpu.SemaphoreType.DMA((NR,)),
            pltpu.SemaphoreType.DMA,
        ],
        compiler_params=pltpu.CompilerParams(
            collective_id=collective_id, has_side_effects=True, vmem_limit_bytes=VMEM_BYTES
        ),
        cost_estimate=cost(16 if x.shape[1] > TQ else 9),
        name="swap",
    )(x)


W_SHAPES = ((272, 3264), (272, 1088), (272, 4352), (1088, 1088))
W_CUTS = (1408, 512, 1920, 512)
W_ENDS = (2816, 896, 3712, 896)


def weights_kernel(*refs):
    ins, docs, outs, all_docs, held = refs[:4], refs[4], refs[5:9], refs[9], refs[10:14]
    (own_s, own_r, local, back, xp_s, xp_r, xd_s, xd_r, xe_s, xe_r, f_s, f_r) = refs[14:26]
    (a1_s, a1_r, b1_s, b1_r, a2_s, a2_r, b2_s, b2_r, a3_s, a3_r, b3_s, b3_r, doc1_s, doc1_r, doc2_s, doc2_r) = refs[26:]
    j = lax.axis_index("shard")
    me = lax.axis_index("replica")
    z, y = me // 4, lax.rem(me, 4)
    xj = lax.rem(j + 2, 4)
    cj = j + 1 - 2 * lax.rem(j, 2)
    x_place, c_place = {"shard": xj}, {"shard": cj}
    y_places = [{"replica": y_peer(me, d)} for d in (1, 2, 3)]
    z_places = [{"replica": z_peer(me, d)} for d in (1, 2, 3)]
    greet([x_place, c_place] + y_places + z_places)

    def rows(start, count):
        return pl.ds(pl.multiple_of(start, 16), count)

    waits = []
    x_pieces, x_directs = [], []
    for a, (r, n) in enumerate(W_SHAPES):
        u = r // 17
        most = pl.ds(0, W_ENDS[a])
        piece = remote(ins[a].at[rows(me * u, u), most], outs[a].at[rows(j * r + me * u, u), most], xp_s.at[a], xp_r.at[a], x_place)
        piece.start()
        x_pieces.append(piece)
    for a, (r, n) in enumerate(W_SHAPES):
        u = r // 17
        most, rest = pl.ds(0, W_ENDS[a]), pl.ds(W_ENDS[a], n - W_ENDS[a])
        direct = remote(ins[a].at[rows(16 * u, u), most], outs[a].at[rows(j * r + 16 * u, u), most], xd_s.at[a], xd_r.at[a], x_place)
        direct.start()
        x_directs.append(direct)
        direct = remote(ins[a].at[:, rest], outs[a].at[rows(j * r, r), rest], xe_s.at[a], xe_r.at[a], x_place)
        direct.start()
        x_directs.append(direct)
    for a, (r, n) in enumerate(W_SHAPES):
        copy = remote(ins[a], outs[a].at[rows(j * r, r)], own_s.at[a], own_r.at[a], c_place)
        copy.start()
        waits.append(copy)
    all_docs[pl.ds(me, 1)] = docs[...][None]
    ours = all_docs.at[me]
    doc_firsts = [remote(ours, ours, doc1_s.at[i], doc1_r.at[i], y_places[i]) for i in range(3)]
    for copy in doc_firsts:
        copy.start()
    loads = [pltpu.make_async_copy(ins[a], held[a], local.at[a]) for a in range(4)]
    for copy in loads:
        copy.start()
    for a, (r, n) in enumerate(W_SHAPES):
        loads[a].wait()
        copy = pltpu.make_async_copy(held[a], outs[a].at[rows(j * r, r)], back.at[a])
        copy.start()
        waits.append(copy)
    for copy in doc_firsts:
        copy.wait()
    ours = all_docs.at[pl.ds(z * 4, 4)]
    for i in range(3):
        copy = remote(ours, ours, doc2_s.at[i], doc2_r.at[i], z_places[i])
        copy.start()
        waits.append(copy)
    firsts = []
    for a, (r, n) in enumerate(W_SHAPES):
        u, cut = r // 17, W_CUTS[a]
        x_pieces[a].wait()
        here = rows(xj * r + me * u, u)
        part_a = outs[a].at[here, pl.ds(0, cut)]
        part_b = outs[a].at[here, pl.ds(cut, W_ENDS[a] - cut)]
        group = []
        for i in range(3):
            group.append(remote(part_a, part_a, a1_s.at[a, i], a1_r.at[a, i], y_places[i]))
            group.append(remote(part_b, part_b, b1_s.at[a, i], b1_r.at[a, i], z_places[i]))
        for copy in group:
            copy.start()
        firsts.append(group)
    def row_part(a, first, half):
        r, u = W_SHAPES[a][0], W_SHAPES[a][0] // 17
        start = xj * r + lax.rem(first + 4, 4) * (4 * u) + half * (2 * u)
        return outs[a].at[rows(start, 2 * u), pl.ds(0, W_CUTS[a])]

    def column_part(a, first, k):
        r, u = W_SHAPES[a][0], W_SHAPES[a][0] // 17
        start = xj * r + (4 * k + lax.rem(first + 4, 4)) * u
        return outs[a].at[rows(start, u), pl.ds(W_CUTS[a], W_ENDS[a] - W_CUTS[a])]

    heres = []
    for a in range(4):
        for copy in firsts[a]:
            copy.wait()
        rights, lefts = [], []
        for k in range(2):
            ref = row_part(a, z, k)
            rights.append(remote(ref, ref, a2_s.at[a, k], a2_r.at[a, k], z_places[0]))
            ref = row_part(a, z, 1 - k)
            lefts.append(remote(ref, ref, a2_s.at[a, 2 + k], a2_r.at[a, 2 + k], z_places[2]))
        for k in range(4):
            ref = column_part(a, y, k)
            rights.append(remote(ref, ref, b2_s.at[a, k], b2_r.at[a, k], y_places[0]))
            ref = column_part(a, y, 3 - k)
            lefts.append(remote(ref, ref, b2_s.at[a, 4 + k], b2_r.at[a, 4 + k], y_places[2]))
        for copy in rights + lefts:
            copy.start()
        heres.append((rights, lefts))
    for a, (r, n) in enumerate(W_SHAPES):
        rights, lefts = heres[a]
        passed = []
        rights[0].wait()
        ref = row_part(a, z - 1, 0)
        passed.append(remote(ref, ref, a3_s.at[a, 0], a3_r.at[a, 0], z_places[0]))
        lefts[0].wait()
        ref = row_part(a, z + 1, 1)
        passed.append(remote(ref, ref, a3_s.at[a, 1], a3_r.at[a, 1], z_places[2]))
        for k in range(2):
            rights[2 + k].wait()
            ref = column_part(a, y - 1, k)
            passed.append(remote(ref, ref, b3_s.at[a, k], b3_r.at[a, k], y_places[0]))
            lefts[2 + k].wait()
            ref = column_part(a, y + 1, 3 - k)
            passed.append(remote(ref, ref, b3_s.at[a, 2 + k], b3_r.at[a, 2 + k], y_places[2]))
        for copy in passed:
            copy.start()
        for copy in rights[1:2] + rights[4:] + lefts[1:2] + lefts[4:] + passed:
            copy.wait()
        x_directs[2 * a].wait()
        x_directs[2 * a + 1].wait()
        whole = outs[a].at[rows(xj * r, r)]
        copy = remote(whole, whole, f_s.at[a], f_r.at[a], c_place)
        copy.start()
        waits.append(copy)
    for copy in waits:
        copy.wait()


def gather_weights(weights, docs):
    dma = pltpu.SemaphoreType.DMA
    outs = [jax.ShapeDtypeStruct((4 * r, n), jnp.bfloat16) for r, n in W_SHAPES]
    return pl.pallas_call(
        weights_kernel,
        out_shape=outs + [jax.ShapeDtypeStruct((NR, 8, 128), jnp.int32)],
        in_specs=[pl.BlockSpec(memory_space=pl.ANY)] * 4 + vmem_specs(1),
        out_specs=[pl.BlockSpec(memory_space=pl.ANY)] * 4 + vmem_specs(1),
        scratch_shapes=[pltpu.VMEM(shape, jnp.bfloat16) for shape in W_SHAPES]
        + [dma((4,))] * 12
        + [dma((4, 3))] * 4
        + [dma((4, 4))] * 2
        + [dma((4, 8))] * 2
        + [dma((4, 2))] * 2
        + [dma((4, 4))] * 2
        + [dma((3,))] * 4,
        compiler_params=pltpu.CompilerParams(
            collective_id=1, has_side_effects=True, vmem_limit_bytes=VMEM_BYTES
        ),
        name="gather_weights",
    )(*weights, docs)


def lane_mask(shape, micro):
    lane = lax.broadcasted_iota(jnp.int32, shape, len(shape) - 1)
    return (lane >= HD) if micro else (lane < HD)


def allowed_block(n0, n2, first_query, queries, keys):
    i = lax.broadcasted_iota(jnp.int32, (queries, keys), 0) + first_query
    j = lax.broadcasted_iota(jnp.int32, (queries, keys), 1)
    row = lax.broadcasted_iota(jnp.int32, (queries, 1), 0) + first_query
    start = jnp.where(row >= n2, n2, jnp.where(row >= n0, n0, 0))
    return (j <= i) & (j >= start)


def scores_of(q, k, micro, allowed):
    zero = jnp.zeros((), jnp.bfloat16)
    q = jnp.where(lane_mask(q.shape, micro), q, zero)
    s = lax.dot_general(q, k, (((1,), (1,)), ((), ())), preferred_element_type=jnp.float32)
    return jnp.where(allowed, s * SCALE, masked_score)


def take(x, entry, start, count):
    return x[pl.ds(start, count), entry].reshape(count * TQ, 2 * HD)


def forward_kernel(bounds, x, q16, o, o16, lse, lse16):
    zero = jnp.zeros((), jnp.bfloat16)
    me = lax.axis_index("replica")

    def attend(q, k, v, micro, first_query):
        allowed = allowed_block(bounds[micro], bounds[2 + micro], first_query, q.shape[0], k.shape[0])
        s = scores_of(q, k, micro, allowed)
        largest = jnp.max(s, axis=-1, keepdims=True)
        e = jnp.exp(s - largest)
        summed = jnp.sum(e, axis=-1, keepdims=True)
        p = (e * (1.0 / summed)).astype(jnp.bfloat16)
        v = jnp.where(lane_mask(v.shape, micro), v, zero)
        return times(p, v), largest + jnp.log(summed)

    per = BQ // TQ
    for b in range(SEQ // BQ):
        count = (b + 1) * per
        q = take(x, 0, b * per, per)
        k = take(x, 1, 0, count)
        v = take(x, 2, 0, count)
        o0, l0 = attend(q, k, v, 0, b * BQ)
        o1, l1 = attend(q, k, v, 1, b * BQ)
        o[pl.ds(b * per, per)] = (o0 + o1).astype(jnp.bfloat16).reshape(per, TQ, 2 * HD)
        lse[pl.ds(b * BQ, BQ)] = jnp.where(lane_mask((BQ, 2 * HD), 0), l0, l1)
    q = q16[...]
    k = take(x, 3, 0, NR)
    v = take(x, 4, 0, NR)
    o0, l0 = attend(q, k, v, 0, me * TQ)
    o1, l1 = attend(q, k, v, 1, me * TQ)
    o16[...] = (o0 + o1).astype(jnp.bfloat16)
    lse16[...] = jnp.where(lane_mask((TQ, 2 * HD), 0), l0, l1)


def vmem_specs(count):
    return [pl.BlockSpec(memory_space=pltpu.VMEM)] * count


def attention_forward(bounds, x, q16):
    f32, bf16 = jnp.float32, jnp.bfloat16
    return pl.pallas_call(
        forward_kernel,
        out_shape=[
            jax.ShapeDtypeStruct((NR, TQ, 2 * HD), bf16),
            jax.ShapeDtypeStruct((TQ, 2 * HD), bf16),
            jax.ShapeDtypeStruct((SEQ, 2 * HD), f32),
            jax.ShapeDtypeStruct((TQ, 2 * HD), f32),
        ],
        in_specs=[pl.BlockSpec(memory_space=pltpu.SMEM)] + vmem_specs(2),
        out_specs=vmem_specs(4),
        compiler_params=pltpu.CompilerParams(vmem_limit_bytes=VMEM_BYTES),
        cost_estimate=cost(5),
        name="attention_forward",
    )(bounds, x, q16)


def backward_kernel(bounds, x, q16, lse, lse16, do, do16, dx, dq16, dk, dv):
    zero = jnp.zeros((), jnp.bfloat16)
    me = lax.axis_index("replica")
    bf16 = jnp.bfloat16

    def pull(q, k, v, grad, logs, micro, first_query):
        allowed = allowed_block(bounds[micro], bounds[2 + micro], first_query, q.shape[0], k.shape[0])
        s = scores_of(q, k, micro, allowed)
        soft = jnp.exp(s - logs[:, micro * HD : micro * HD + 1])
        grad = jnp.where(lane_mask(grad.shape, micro), grad, zero)
        dp = times_transposed(grad, v)
        along = jnp.sum(soft * dp, axis=-1, keepdims=True)
        ds = (soft * (dp - along)).astype(bf16)
        q = jnp.where(lane_mask(q.shape, micro), q, zero)
        k = jnp.where(lane_mask(k.shape, micro), k, zero)
        return times(ds, k), outer_sum(ds, q), outer_sum(soft.astype(bf16), grad)

    per = BQ // TQ
    for b in reversed(range(SEQ // BQ)):
        count = (b + 1) * per
        q = take(x, 0, b * per, per)
        k = take(x, 1, 0, count)
        v = take(x, 2, 0, count)
        grad = do[pl.ds(b * per, per)].reshape(BQ, 2 * HD)
        logs = lse[pl.ds(b * BQ, BQ)]
        q0, k0, v0 = pull(q, k, v, grad, logs, 0, b * BQ)
        q1, k1, v1 = pull(q, k, v, grad, logs, 1, b * BQ)
        dx[pl.ds(b * per, per), 0] = ((q0 + q1) * SCALE).astype(bf16).reshape(per, TQ, 2 * HD)
        keys = pl.ds(0, (b + 1) * BQ)
        if b == SEQ // BQ - 1:
            dk[keys] = k0 + k1
            dv[keys] = v0 + v1
        else:
            dk[keys] += k0 + k1
            dv[keys] += v0 + v1
    dx[:, 1] = (dk[...] * SCALE).astype(bf16).reshape(NR, TQ, 2 * HD)
    dx[:, 2] = dv[...].astype(bf16).reshape(NR, TQ, 2 * HD)
    q = q16[...]
    k = take(x, 3, 0, NR)
    v = take(x, 4, 0, NR)
    q0, k0, v0 = pull(q, k, v, do16[...], lse16[...], 0, me * TQ)
    q1, k1, v1 = pull(q, k, v, do16[...], lse16[...], 1, me * TQ)
    dq16[...] = ((q0 + q1) * SCALE).astype(bf16)
    dx[:, 3] = ((k0 + k1) * SCALE).astype(bf16).reshape(NR, TQ, 2 * HD)
    dx[:, 4] = (v0 + v1).astype(bf16).reshape(NR, TQ, 2 * HD)


def attention_backward(bounds, x, q16, lse, lse16, do, do16):
    f32, bf16 = jnp.float32, jnp.bfloat16
    return pl.pallas_call(
        backward_kernel,
        out_shape=[
            jax.ShapeDtypeStruct((NR, 5, TQ, 2 * HD), bf16),
            jax.ShapeDtypeStruct((TQ, 2 * HD), bf16),
        ],
        in_specs=[pl.BlockSpec(memory_space=pltpu.SMEM)] + vmem_specs(6),
        out_specs=vmem_specs(2),
        scratch_shapes=[pltpu.VMEM((SEQ, 2 * HD), f32), pltpu.VMEM((SEQ, 2 * HD), f32)],
        compiler_params=pltpu.CompilerParams(vmem_limit_bytes=VMEM_BYTES),
        cost_estimate=cost(8),
        name="attention_backward",
    )(bounds, x, q16, lse, lse16, do, do16)


QKV = 3 * D
ENTER_BLOCK, LEAVE_BLOCK, BACK_ENTER_BLOCK = 1664, 2176, 640
LEFT_AT, LEFT_WIDTH = (0, 384, 768, 1152), 2304
EARLY_AT, EARLY_WIDTH = (0, 4352, 5504), 6656
LATE_WIDTH = 3328
SMALL = 1152


def low_lanes(shape):
    return lane_mask(shape, 0)


def to_blocks(upper, lower, odd):
    half = low_lanes(upper.shape)
    if odd:
        return jnp.where(half, pltpu.roll(upper, HD, 1), lower)
    return jnp.where(half, upper, pltpu.roll(lower, HD, 1))


def from_blocks(first, second):
    half = low_lanes(first.shape)
    upper = jnp.where(half, first, pltpu.roll(second, HD, 1))
    return upper, jnp.where(half, pltpu.roll(first, HD, 1), second)


def lines(start, count):
    return pl.ds(start, count)


def enter_kernel(x, gains, biases, w, message, q16, act, mixed):
    i = pl.program_id(0)

    @pl.when(i == 0)
    def _():
        normed, _, _ = layer_norm(x[...].astype(jnp.float32), gains[0:1], biases[0:1])
        act[...] = normed.astype(jnp.bfloat16)

    mixed[i] = times(act[...], w[...])

    @pl.when(i == pl.num_programs(0) - 1)
    def _():
        for b in range(3 * H):
            kind, head = divmod(b, H)
            i, t = divmod(b // 2, ENTER_BLOCK // 128)
            part = pl.ds(t * 128, 128)
            block = to_blocks(mixed[i, 0:TQ, part], mixed[i, TQ : 2 * TQ, part], b % 2)
            if kind != 1:
                row = 1 if kind == 0 else 2
                shift = biases[row : row + 1, head * HD : (head + 1) * HD]
                block = block + jnp.concatenate([shift, shift], axis=1)
            block = block.astype(jnp.bfloat16)
            if head < H - 1:
                message[head, kind * TQ : (kind + 1) * TQ] = block
            elif kind == 0:
                q16[...] = block
            else:
                for p in range(NR):
                    message[p, (kind + 2) * TQ : (kind + 3) * TQ] = block


def fixed(shape):
    return pl.BlockSpec(shape, lambda i: (0,) * len(shape))


def enter(x, gains, biases, w_qkv):
    bf16 = jnp.bfloat16
    steps = -(-QKV // ENTER_BLOCK)
    shapes = [(NR, 5 * TQ, 2 * HD), (TQ, 2 * HD), (2 * TQ, D)]
    return pl.pallas_call(
        enter_kernel,
        grid=(steps,),
        out_shape=[jax.ShapeDtypeStruct(shape, bf16) for shape in shapes],
        in_specs=[
            fixed(x.shape),
            fixed(gains.shape),
            fixed(biases.shape),
            pl.BlockSpec((D, ENTER_BLOCK), lambda i: (0, i)),
        ],
        out_specs=[fixed(shape) for shape in shapes],
        scratch_shapes=[pltpu.VMEM((steps, 2 * TQ, ENTER_BLOCK), jnp.float32)],
        compiler_params=pltpu.CompilerParams(vmem_limit_bytes=VMEM_BYTES),
        cost_estimate=cost(5),
        name="enter",
    )(x, gains, biases, w_qkv)


CURVE = 0.044715
ROOT = 0.7978845608028654


def weight_loads(w_out, w_up, w_down, v_out, v_up, v_down, sems):
    load_up, load_down = [], []
    for i in range(2):
        part = pl.ds(i * LEAVE_BLOCK, LEAVE_BLOCK)
        load_up.append(pltpu.make_async_copy(w_up.at[:, part], v_up.at[i], sems.at[1 + i]))
        load_down.append(pltpu.make_async_copy(w_down.at[part], v_down.at[i], sems.at[3 + i]))
    return pltpu.make_async_copy(w_out, v_out, sems.at[0]), load_up, load_down


def weight_buffers():
    bf16 = jnp.bfloat16
    return [
        pltpu.VMEM((D, D), bf16),
        pltpu.VMEM((2, D, LEAVE_BLOCK), bf16),
        pltpu.VMEM((2, LEAVE_BLOCK, D), bf16),
        pltpu.SemaphoreType.DMA((5,)),
    ]


def leave_kernel(
    x, o, o16, act1, gains, biases, up_shift, w_out, w_up, w_down,
    result, resid, pre, lefts, act2, total, v_out, v_up, v_down, sems,
):
    bf16 = jnp.bfloat16
    load_out, load_up, load_down = weight_loads(w_out, w_up, w_down, v_out, v_up, v_down, sems)
    load_out.start()
    for i in range(2):
        load_up[i].start()
        load_down[i].start()

    def attention_out():
        tiles = []
        for t in range(H // 2 + 1):
            first = o[2 * t] if 2 * t < H - 1 else o16[...]
            second = o[2 * t + 1] if 2 * t + 1 < H - 1 else o16[...]
            upper, lower = from_blocks(first.astype(jnp.float32), second.astype(jnp.float32))
            tiles.append(jnp.concatenate([upper, lower], axis=0))
        attended = jnp.concatenate(tiles, axis=1)[:, :D].astype(bf16)
        load_out.wait()
        r = x[...].astype(jnp.float32) + times(attended, v_out[...]) + biases[3:4]
        resid[...] = r
        normed, _, _ = layer_norm(r, gains[1:2], biases[4:5])
        act2[...] = normed.astype(bf16)
        for s in range(4):
            part = slice(s * 272, (s + 1) * 272)
            for at, value in zip(LEFT_AT, (act1, attended, act2)):
                lefts[s, :, at : at + 272] = value[:, part]
        total[...] = r + biases[5:6]

    attention_out()
    for i in range(2):
        part = slice(i * LEAVE_BLOCK, (i + 1) * LEAVE_BLOCK)
        load_up[i].wait()
        u = times(act2[...], v_up[i]) + up_shift[:, part]
        pre[:, part] = u
        g = (0.5 * u * (1.0 + jnp.tanh(ROOT * (u + CURVE * u * u * u)))).astype(bf16)
        for s in range(2):
            lefts[2 * i + s, :, LEFT_AT[3] : LEFT_AT[3] + D] = g[:, s * D : (s + 1) * D]
        load_down[i].wait()
        total[...] += times(g, v_down[i])
    result[...] = total[...].astype(bf16)


def leave(x, o, o16, act1, gains, biases, up_shift, weights):
    _, w_out, w_up, w_down = weights
    f32, bf16 = jnp.float32, jnp.bfloat16
    rows = 2 * TQ
    return pl.pallas_call(
        leave_kernel,
        out_shape=[
            jax.ShapeDtypeStruct((rows, D), bf16),
            jax.ShapeDtypeStruct((rows, D), f32),
            jax.ShapeDtypeStruct((rows, FF), f32),
            jax.ShapeDtypeStruct((4, rows, LEFT_WIDTH), bf16),
        ],
        in_specs=vmem_specs(7) + [pl.BlockSpec(memory_space=pl.ANY)] * 3,
        out_specs=vmem_specs(4),
        scratch_shapes=[pltpu.VMEM((rows, D), bf16), pltpu.VMEM((rows, D), f32)] + weight_buffers(),
        compiler_params=pltpu.CompilerParams(vmem_limit_bytes=VMEM_BYTES),
        cost_estimate=cost(12),
        name="leave",
    )(x, o, o16, act1, gains, biases, up_shift, w_out, w_up, w_down)


def column_sum(value):
    return jnp.sum(value, axis=0, keepdims=True)


def back_leave_kernel(
    dy, resid, pre, gains, w_out, w_up, w_down,
    early, grad_resid, do, do16, sums, total, v_out, v_up, v_down, sems,
):
    f32, bf16 = jnp.float32, jnp.bfloat16
    load_out, load_up, load_down = weight_loads(w_out, w_up, w_down, v_out, v_up, v_down, sems)
    for i in range(2):
        load_down[i].start()
        load_up[i].start()
    load_out.start()
    total[...] = jnp.zeros_like(total)
    for i in range(2):
        part = slice(i * LEAVE_BLOCK, (i + 1) * LEAVE_BLOCK)
        u = pre[:, part]
        load_down[i].wait()
        grad_hidden = times_transposed(dy[...], v_down[i])
        t = jnp.tanh(ROOT * (u + CURVE * u * u * u))
        slope = 0.5 * (1.0 + t) + 0.5 * u * (1.0 - t * t) * (ROOT * (1.0 + 3.0 * CURVE * u * u))
        du = (grad_hidden * slope).astype(bf16)
        early[:, part] = du
        du_sum = column_sum(du.astype(f32))
        for s in range(2):
            sums[4 + 2 * i + s : 5 + 2 * i + s, 0:D] = du_sum[:, s * D : (s + 1) * D]
        load_up[i].wait()
        total[...] += times_transposed(du, v_up[i])
    load_out.wait()

    def norm_and_heads():
        da2 = total[...]
        _, normed, inverse = layer_norm(resid[...], gains[1:2], 0.0)
        dr = dy[...].astype(f32) + norm_back(da2, normed, inverse, gains[1:2])
        grad_resid[...] = dr
        db = dr.astype(bf16)
        for at in EARLY_AT[1:]:
            early[:, at + 1024 : at + 1152] = jnp.zeros((2 * TQ, 128), bf16)
        early[:, EARLY_AT[1] : EARLY_AT[1] + D] = db
        early[:, EARLY_AT[2] : EARLY_AT[2] + D] = dy[...]
        sums[0:1, 0:D] = column_sum(da2 * normed)
        sums[1:2, 0:D] = column_sum(da2)
        sums[2:3, 0:D] = column_sum(db.astype(f32))
        sums[3:4, 0:D] = column_sum(dy[...].astype(f32))
        heads = times_transposed(db, v_out[...])
        heads = jnp.concatenate([heads, jnp.zeros((2 * TQ, HD), f32)], axis=1)
        for b in range(H):
            tile = heads[:, (b // 2) * 128 : (b // 2 + 1) * 128]
            block = to_blocks(tile[0:TQ], tile[TQ : 2 * TQ], b % 2).astype(bf16)
            if b < H - 1:
                do[b] = block
            else:
                do16[...] = block

    norm_and_heads()


def back_leave(dy, resid, pre, gains, weights):
    _, w_out, w_up, w_down = weights
    f32, bf16 = jnp.float32, jnp.bfloat16
    rows = 2 * TQ
    shapes = [(rows, EARLY_WIDTH), (rows, D), (NR, TQ, 2 * HD), (TQ, 2 * HD), (8, SMALL)]
    types = [bf16, f32, bf16, bf16, f32]
    return pl.pallas_call(
        back_leave_kernel,
        out_shape=[jax.ShapeDtypeStruct(shape, t) for shape, t in zip(shapes, types)],
        in_specs=vmem_specs(4) + [pl.BlockSpec(memory_space=pl.ANY)] * 3,
        out_specs=vmem_specs(5),
        scratch_shapes=[pltpu.VMEM((rows, D), f32)] + weight_buffers(),
        compiler_params=pltpu.CompilerParams(vmem_limit_bytes=VMEM_BYTES),
        cost_estimate=cost(14),
        name="back_leave",
    )(dy, resid, pre, gains, w_out, w_up, w_down)


def back_enter_kernel(x, back, dq16, grad_resid, before, gains, w, late, grad_in, sums, parts):
    i = pl.program_id(0)
    f32, bf16 = jnp.float32, jnp.bfloat16

    @pl.when(i == 0)
    def _():
        def last(kind):
            total = back[0, (kind + 2) * TQ : (kind + 3) * TQ].astype(f32)
            for p in range(1, NR):
                total = total + back[p, (kind + 2) * TQ : (kind + 3) * TQ].astype(f32)
            return total

        def block(b):
            kind, head = divmod(b, H)
            if head < H - 1:
                return back[head, kind * TQ : (kind + 1) * TQ].astype(f32)
            return dq16[...].astype(f32) if kind == 0 else last(kind)

        for t in range(3 * H // 2 + 1):
            first = block(2 * t)
            second = block(2 * t + 1) if 2 * t + 1 < 3 * H else jnp.zeros_like(first)
            upper, lower = from_blocks(first, second)
            late[0:TQ, t * 128 : (t + 1) * 128] = upper.astype(bf16)
            late[TQ : 2 * TQ, t * 128 : (t + 1) * 128] = lower.astype(bf16)

    parts[i] = times_transposed(late[:, 0:QKV], w[...])

    @pl.when(i == pl.num_programs(0) - 1)
    def _():
        da1 = jnp.concatenate([parts[k] for k in range(parts.shape[0])], axis=1)[:, :D]
        _, normed, inverse = layer_norm(x[...].astype(f32), gains[0:1], 0.0)
        dx = grad_resid[...] + norm_back(da1, normed, inverse, gains[0:1])
        grad_in[...] = dx.astype(bf16)
        sums[...] = jnp.zeros_like(sums)
        sums[0:1, 0:D] = column_sum(da1 * normed)
        sums[1:2, 0:D] = column_sum(da1)
        sums[2:3, 0:D] = column_sum(late[:, 0:D].astype(f32))
        sums[3:4, 0:D] = column_sum(late[:, 2 * D : QKV].astype(f32))
        sums[4:12, 0:D] = before[:, 0:D]


def back_enter(x, back, dq16, grad_resid, before, gains, w_qkv):
    f32, bf16 = jnp.float32, jnp.bfloat16
    rows = 2 * TQ
    steps = -(-D // BACK_ENTER_BLOCK)
    return pl.pallas_call(
        back_enter_kernel,
        grid=(steps,),
        out_shape=[
            jax.ShapeDtypeStruct((rows, LATE_WIDTH), bf16),
            jax.ShapeDtypeStruct((rows, D), bf16),
            jax.ShapeDtypeStruct((16, SMALL), f32),
        ],
        in_specs=[
            fixed(x.shape),
            fixed(back.shape),
            fixed(dq16.shape),
            fixed(grad_resid.shape),
            fixed(before.shape),
            fixed(gains.shape),
            pl.BlockSpec((BACK_ENTER_BLOCK, QKV), lambda i: (i, 0)),
        ],
        out_specs=[fixed((rows, LATE_WIDTH)), fixed((rows, D)), fixed((16, SMALL))],
        scratch_shapes=[pltpu.VMEM((steps, rows, BACK_ENTER_BLOCK), f32)],
        compiler_params=pltpu.CompilerParams(vmem_limit_bytes=VMEM_BYTES),
        cost_estimate=cost(5),
        name="back_enter",
    )(x, back, dq16, grad_resid, before, gains, w_qkv)


AT_OUT, AT_UP, AT_DOWN, DOWN_STEP = 3584, 4736, 9088, 1152
LATE_FREE, LATE_CHUNK = 3328, 256
EARLY_FREE, EARLY_CHUNK = 13696, 640


def weight_sums_kernel(
    l0, l1, l2, l3, e0, e1, e2, late, small, out,
    lefts, early, mixed, got, strip, g, tr, ins, ad, part, mid, fin,
    loc, late_s, late_r, small_s, small_r,
    p_s, p_r, q_s, q_r, m_s, m_r, n_s, n_r, e_s, e_r, w_s, w_r, last,
):
    f32, bf16 = jnp.float32, jnp.bfloat16
    rows = 2 * TQ
    j = lax.axis_index("shard")
    me = lax.axis_index("replica")
    z, y = me // 4, lax.rem(me, 4)
    xj = lax.rem(j + 2, 4)
    cj = j + 1 - 2 * lax.rem(j, 2)
    places = [{"shard": xj}, {"shard": cj}, {"shard": lax.rem(cj + 2, 4)}]
    y_places = [{"replica": y_peer(me, d)} for d in (1, 2, 3)]
    z_places = [{"replica": z_peer(me, d)} for d in (1, 2, 3)]
    greet(places + y_places + z_places)

    def slot(ref, k):
        return ref.at[pl.ds(k * rows, rows)]

    across = remote(late, slot(mixed, 1), late_s.at[0], late_r.at[0], places[0])
    across.start()
    beside = remote(late, slot(mixed, 2), late_s.at[1], late_r.at[1], places[1])
    beside.start()
    early_relay = remote(e1, slot(early, 3), late_s.at[3], late_r.at[3], places[1])
    early_relay.start()
    smalls = [remote(small, got.at[k], small_s.at[k], small_r.at[k], places[k]) for k in range(3)]
    for copy in smalls:
        copy.start()
    loads = [pltpu.make_async_copy(late, slot(mixed, 0), loc.at[0])]
    loads.append(pltpu.make_async_copy(l0.at[j], slot(lefts, 0), loc.at[1]))
    for k, ref in enumerate((l1, l2, l3)):
        loads.append(pltpu.make_async_copy(ref, slot(lefts, k + 1), loc.at[2 + k]))
    for k, ref in enumerate((e0, e1, e2)):
        loads.append(pltpu.make_async_copy(ref, slot(early, k), loc.at[5 + k]))
    for copy in loads:
        copy.start()
    for copy in loads:
        copy.wait()
    early_relay.wait()

    def keep(product, put_at):
        g[:, put_at] = product[0:RED_ROWS]
        strip[:, put_at] = product[RED_ROWS:272]

    def stripe(left_at, right, right_at, at, columns, width):
        @pl.loop(0, columns // width)
        def _(i):
            take_at = pl.ds(pl.multiple_of(right_at + i * width, 128), width)
            put_at = pl.ds(pl.multiple_of(at + i * width, 128), width)
            product = outer_sum(lefts[:, left_at : left_at + 272], right[:, take_at])
            keep(product.astype(bf16), put_at)

    stripe(LEFT_AT[2], early, EARLY_AT[0], AT_UP, FF, 2176)
    product = outer_sum(lefts[:, LEFT_AT[1] : LEFT_AT[1] + 272], early[:, EARLY_AT[1] : EARLY_AT[2]])
    keep(product.astype(bf16), slice(AT_OUT, AT_UP))
    for s in range(4):
        at = AT_DOWN + s * DOWN_STEP
        first = LEFT_AT[3] + s * 272
        product = outer_sum(lefts[:, first : first + 272], early[:, EARLY_AT[2] : EARLY_WIDTH])
        keep(product.astype(bf16), slice(at, at + DOWN_STEP))
    g[:, EARLY_FREE:] = jnp.zeros((RED_ROWS, EARLY_CHUNK), bf16)
    for c in range(16):
        first = AT_OUT + c * EARLY_CHUNK
        width = min(EARLY_CHUNK, EARLY_FREE - first)
        g[16 * c : 16 * c + 16, EARLY_FREE : EARLY_FREE + width] = strip[:, first : first + width]

    firsts, seconds = (y_places, z_places), (z_places, y_places)
    here, there = (y, z), (z, y)

    def at(side, first, second):
        piece = 4 * second + lax.rem(first + 4, 4)
        return (pl.ds(side * HALF, HALF), pl.ds(pl.multiple_of(piece * PIECE, 128), PIECE))

    def piece_of(ref, side, first, second):
        return ref.at[at(side, first, second)]

    def value_of(side, first, second):
        return g[at(side, first, second)].astype(f32)

    opened, direct, added = {}, {}, {}

    def open_piece(s, k):
        t, right, left = here[s], firsts[s][0], firsts[s][2]
        copy = remote(piece_of(g, s, t + 2, k), tr.at[s, k], p_s.at[s, k], p_r.at[s, k], right if k < 2 else left)
        copy.start()
        opened[s, k] = copy

    def direct_piece(s, k):
        t, right, left = here[s], firsts[s][0], firsts[s][2]
        if k < 2:
            copy = remote(piece_of(g, s, t - 1, k), ins.at[s, 1, k], p_s.at[s, 4 + k], p_r.at[s, 4 + k], left)
        else:
            copy = remote(piece_of(g, s, t + 1, k), ins.at[s, 0, k], p_s.at[s, 4 + k], p_r.at[s, 4 + k], right)
        copy.start()
        direct[s, k] = copy

    def add_piece(s, k):
        t, right, left = here[s], firsts[s][0], firsts[s][2]
        opened[s, k].wait()
        mine = value_of(s, t + 1 if k < 2 else t - 1, k)
        ad[s, k] = (tr[s, k].astype(f32) + mine).astype(bf16)
        to, side = (right, 0) if k < 2 else (left, 1)
        copy = remote(ad.at[s, k], ins.at[s, side, k], q_s.at[s, k], q_r.at[s, k], to)
        copy.start()
        added[s, k] = copy

    for k in (1, 2, 3):
        for s in range(2):
            open_piece(s, k)
    for k in (1, 2, 3):
        for s in range(2):
            direct_piece(s, k)
    for k in (1, 2):
        for s in range(2):
            add_piece(s, k)
    across.wait()
    relay = remote(slot(mixed, 1), slot(mixed, 3), late_s.at[2], late_r.at[2], places[1])
    relay.start()
    beside.wait()
    for s in range(2):
        add_piece(s, 3)
    relay.wait()
    stripe(LEFT_AT[0], mixed, 0, 0, LATE_WIDTH, 1664)
    for copy in smalls:
        copy.wait()
    for c in range(13):
        g[16 * c : 16 * c + 16, LATE_FREE:AT_OUT] = strip[:, c * LATE_CHUNK : (c + 1) * LATE_CHUNK]
    sums = (small[...] + got[0] + got[1] + got[2]).astype(bf16)
    for c in range(3):
        row = 208 + 16 * c
        g[row : row + 16, LATE_FREE:AT_OUT] = sums[:, c * LATE_CHUNK : (c + 1) * LATE_CHUNK]
    for c in range(5):
        first = 3 * LATE_CHUNK + c * 64
        g[16 * c : 16 * c + 16, QKV:LATE_FREE] = sums[:, first : first + 64]
    for s in range(2):
        open_piece(s, 0)
        direct_piece(s, 0)
    for s in range(2):
        add_piece(s, 0)

    middles = []
    for s in range(2):
        for k in range(4):
            direct[s, k].wait()
            added[s, k].wait()
            part[s, k] = (value_of(s, here[s], k) + ins[s, 0, k].astype(f32) + ins[s, 1, k].astype(f32)).astype(bf16)
        group = []
        for i in range(3):
            to = lax.rem(there[s] + 1 + i, 4)
            group.append(remote(part.at[s, to], mid.at[s, i], m_s.at[s, i], m_r.at[s, i], seconds[s][i]))
        for copy in group:
            copy.start()
        middles.append(group)
    backs = []
    for s in range(2):
        for copy in middles[s]:
            copy.wait()
        total = part[s, there[s]].astype(f32)
        for i in range(3):
            total = total + mid[s, i].astype(f32)
        fin[s] = total.astype(bf16)
        where = piece_of(out, s, here[s], there[s])
        group = [remote(fin.at[s], where, n_s.at[s, i], n_r.at[s, i], seconds[s][i]) for i in range(3)]
        group.append(pltpu.make_async_copy(fin.at[s], where, last.at[s]))
        for copy in group:
            copy.start()
        backs.append(group)
    to_rights, to_lefts = [], []
    for s in range(2):
        t, right, left = here[s], firsts[s][0], firsts[s][2]
        for copy in backs[s]:
            copy.wait()
        to_right, to_left = [], []
        for k in range(4):
            ref = piece_of(out, s, t, k)
            to_right.append(remote(ref, ref, e_s.at[s, k], e_r.at[s, k], right))
            ref = piece_of(out, s, t, 3 - k)
            to_left.append(remote(ref, ref, e_s.at[s, 4 + k], e_r.at[s, 4 + k], left))
        for k in range(4):
            to_right[k].start()
            to_left[k].start()
        to_rights.append(to_right)
        to_lefts.append(to_left)
    passed = []
    for k in range(2):
        for s in range(2):
            t, right, left = here[s], firsts[s][0], firsts[s][2]
            to_rights[s][k].wait()
            ref = piece_of(out, s, t - 1, k)
            copy = remote(ref, ref, w_s.at[s, k], w_r.at[s, k], right)
            copy.start()
            passed.append(copy)
            to_lefts[s][k].wait()
            ref = piece_of(out, s, t + 1, 3 - k)
            copy = remote(ref, ref, w_s.at[s, 2 + k], w_r.at[s, 2 + k], left)
            copy.start()
            passed.append(copy)
    for s in range(2):
        for copy in to_rights[s][2:] + to_lefts[s][2:]:
            copy.wait()
    for copy in passed:
        copy.wait()


def weight_sums(lefts, early, late, small):
    dma = pltpu.SemaphoreType.DMA
    f32, bf16 = jnp.float32, jnp.bfloat16
    anywhere = pl.BlockSpec(memory_space=pl.ANY)
    piece = (HALF, PIECE)
    return pl.pallas_call(
        weight_sums_kernel,
        out_shape=jax.ShapeDtypeStruct((RED_ROWS, NR * PIECE), bf16),
        in_specs=[anywhere] * 8 + vmem_specs(1),
        out_specs=anywhere,
        scratch_shapes=[
            pltpu.VMEM((8 * TQ, LEFT_WIDTH), bf16),
            pltpu.VMEM((8 * TQ, EARLY_WIDTH), bf16),
            pltpu.VMEM((8 * TQ, LATE_WIDTH), bf16),
            pltpu.VMEM((3, 16, SMALL), f32),
            pltpu.VMEM((16, NR * PIECE), bf16),
            pltpu.VMEM((RED_ROWS, NR * PIECE), bf16),
            pltpu.VMEM((2, 4) + piece, bf16),
            pltpu.VMEM((2, 2, 4) + piece, bf16),
            pltpu.VMEM((2, 4) + piece, bf16),
            pltpu.VMEM((2, 4) + piece, bf16),
            pltpu.VMEM((2, 3) + piece, bf16),
            pltpu.VMEM((2,) + piece, bf16),
            dma((8,)),
            dma((4,)), dma((4,)), dma((3,)), dma((3,)),
        ]
        + [dma((2, 8))] * 2
        + [dma((2, 4))] * 2
        + [dma((2, 3))] * 4
        + [dma((2, 8))] * 2
        + [dma((2, 4))] * 2
        + [dma((2,))],
        compiler_params=pltpu.CompilerParams(
            collective_id=2, has_side_effects=True, vmem_limit_bytes=VMEM_BYTES
        ),
        name="weight_sums",
    )(*lefts, *early, late, small)


def widen_kernel(g, qkv, out, up, down, small, late_free, early_free):
    i = pl.program_id(0)
    f32 = jnp.float32

    @pl.when(i < 4)
    def _():
        qkv[...] = g[:, 0:QKV].astype(f32)
        out[...] = g[:, AT_OUT : AT_OUT + D].astype(f32)
        up[...] = g[:, AT_UP : AT_UP + FF].astype(f32)
        for s in range(4):
            at = AT_DOWN + s * DOWN_STEP
            down[s] = g[:, at : at + D].astype(f32)
        rows = pl.ds(pl.multiple_of(i * 64, 64), 64)
        late_free[rows] = g[:, LATE_FREE - 128 : AT_OUT]
        early_free[rows] = g[:, EARLY_FREE:]

    @pl.when(i == 4)
    def _():
        late = [late_free[16 * c : 16 * c + 16, 128:].astype(f32) for c in range(16)]
        qkv[0:16] = jnp.concatenate(late[:13], axis=1)[:, :QKV]
        early = [early_free[16 * c : 16 * c + 16, :].astype(f32) for c in range(16)]
        rest = jnp.concatenate(early, axis=1)
        out[0:16] = rest[:, 0:D]
        first = AT_UP - AT_OUT
        up[0:16] = rest[:, first : first + FF]
        for s in range(4):
            at = AT_DOWN - AT_OUT + s * DOWN_STEP
            down[s, 0:16] = rest[:, at : at + D]
        small[:, 0:768] = jnp.concatenate(late[13:], axis=1)
        for c in range(5):
            small[:, 768 + 64 * c : 832 + 64 * c] = late_free[16 * c : 16 * c + 16, 64:128].astype(f32)
        small[:, 1088:SMALL] = jnp.zeros((16, SMALL - 1088), f32)


def widen(g):
    f32, bf16 = jnp.float32, jnp.bfloat16
    return pl.pallas_call(
        widen_kernel,
        grid=(5,),
        out_shape=[
            jax.ShapeDtypeStruct((272, QKV), f32),
            jax.ShapeDtypeStruct((272, D), f32),
            jax.ShapeDtypeStruct((272, FF), f32),
            jax.ShapeDtypeStruct((4, 272, D), f32),
            jax.ShapeDtypeStruct((16, SMALL), f32),
        ],
        in_specs=[pl.BlockSpec((64, NR * PIECE), lambda i: (jnp.minimum(i, 3), 0))],
        out_specs=[
            pl.BlockSpec((64, QKV), lambda i: (i, 0)),
            pl.BlockSpec((64, D), lambda i: (i, 0)),
            pl.BlockSpec((64, FF), lambda i: (i, 0)),
            pl.BlockSpec((4, 64, D), lambda i: (0, i, 0)),
            fixed((16, SMALL)),
        ],
        scratch_shapes=[
            pltpu.VMEM((RED_ROWS, 384), bf16),
            pltpu.VMEM((RED_ROWS, EARLY_CHUNK), bf16),
        ],
        compiler_params=pltpu.CompilerParams(vmem_limit_bytes=VMEM_BYTES),
        name="widen",
    )(g)


def layer_forward(x, bounds, gains, biases, up_shift, weights):
    message, q16, act1 = enter(x, gains, biases, weights[0])
    whole = swap(message, 3).reshape(NR, 5, TQ, 2 * HD)
    o, o16, lse, lse16 = attention_forward(bounds, whole, q16)
    result, resid, pre, lefts = leave(x, swap(o, 4), o16, act1, gains, biases, up_shift, weights)
    return result, (whole, q16, lse, lse16, resid, pre), lefts


def layer_backward(dy, x, kept, bounds, gains, weights, tie=None):
    whole, q16, lse, lse16, resid, pre = kept
    early, grad_resid, do, do16, sums = back_leave(dy, resid, pre, gains, weights)
    dx, dq16 = attention_backward(bounds, whole, q16, lse, lse16, swap(do, 4), do16)
    dx, tie = lax.optimization_barrier((dx, tie))
    back = swap(dx.reshape(NR, 5 * TQ, 2 * HD), 3)
    late, grad_in, small = back_enter(x, back, dq16, grad_resid, sums, gains, weights[0])
    return grad_in, early, late, small, tie


X_ROUTE = [(j, j ^ 2) for j in range(4)]
C_ROUTE = [(j, j ^ 1) for j in range(4)]


CX_ROUTE = [(j, j ^ 3) for j in range(4)]


def everyone(value):
    return value, lax.ppermute(value, "shard", X_ROUTE), lax.ppermute(value, "shard", C_ROUTE)


def own_columns(cut):
    j = lax.axis_index("shard")

    def of(shard):
        return lax.dynamic_index_in_dim(cut, shard, 0, keepdims=False)

    across, beside = lax.rem(j + 2, 4), j + 1 - 2 * lax.rem(j, 2)
    return (
        cut,
        lax.ppermute(of(across), "shard", X_ROUTE),
        lax.ppermute(of(beside), "shard", C_ROUTE),
        lax.ppermute(of(lax.rem(beside + 2, 4)), "shard", CX_ROUTE),
    )


def shards(tokens, cotangent, doc_ids, gains, biases, up_bias, w_qkv, w_out, w_up, w_down):
    is_first = lax.axis_index("section") == 0
    ids = doc_ids[:, 0]
    counts = jnp.stack([jnp.sum((ids == n).astype(jnp.int32), axis=1) for n in (0, 2)])
    counts = jnp.pad(counts, ((0, 6), (0, 126)))
    *weights, counts = gather_weights((w_qkv[0], w_out[0], w_up[0], w_down[0]), counts)
    counts = jnp.sum(counts[:, :2, :2], axis=0)
    bounds = jnp.concatenate([counts[0], SEQ - counts[1]])
    gains, biases = gains[0], biases[0]
    own_in = tokens.reshape(2 * TQ, D)
    own_cot = cotangent.reshape(2 * TQ, D)
    result, _, _ = layer_forward(own_in, bounds, gains, biases, up_bias, weights)
    inbox = lax.ppermute(result, "section", [(0, 1)])
    inputs = jnp.where(is_first, own_in, inbox)
    layer_out, kept, lefts = layer_forward(inputs, bounds, gains, biases, up_bias, weights)
    lefts = own_columns(lefts)
    grad_in, _, _, _, others = layer_backward(own_cot, inputs, kept, bounds, gains, weights, lefts[1:])
    lefts = (lefts[0], *others)
    inbox = lax.ppermute(grad_in, "section", [(1, 0)])
    dy = jnp.where(is_first, inbox, own_cot)
    grad_in, early, late, small, _ = layer_backward(dy, inputs, kept, bounds, gains, weights)
    summed = weight_sums(lefts, everyone(early), late, small)
    qkv, out, up, down, small = widen(summed)
    small = small[:, :D]
    return (
        layer_out.reshape(1, 2, 1, TQ, D),
        grad_in.reshape(1, 2, 1, TQ, D),
        jnp.stack([small[0], small[4]])[None],
        jnp.stack([small[k] for k in (1, 2, 3, 6, 5, 7)])[None],
        small[8:12].reshape(1, FF),
        qkv[None],
        out[None],
        up[None],
        down.reshape(1, 1088, D),
    )


def solution(mesh):
    placed = (
        P(None, "shard", "replica", None),
        P(None, "shard", "replica", None),
        P(None, "shard", "replica"),
        P("section", None, None),
        P("section", None, None),
        P("section", None),
        P("section", "shard", None),
        P("section", "shard", None),
        P("section", "shard", None),
        P("section", "shard", None),
    )
    return jax.shard_map(
        shards,
        mesh=mesh,
        in_specs=placed,
        out_specs=(
            P("section", None, "shard", "replica", None),
            P("section", None, "shard", "replica", None),
            P("section", None, None),
            P("section", None, None),
            P("section", None),
            P("section", "shard", None),
            P("section", "shard", None),
            P("section", "shard", None),
            P("section", "shard", None),
        ),
        check_vma=False,
    )
```

```python
import functools

import jax
import jax.numpy as jnp
from jax import lax
from jax.experimental import pallas as pl
from jax.experimental.pallas import tpu as pltpu
from jax.sharding import PartitionSpec as P

MESH = pl.DeviceIdType.MESH
H = 17
HD = 64
TQ = 64
SEQ = 1024
NR = 16
D = 1088
FF = 4352
SCALE = HD ** (-0.5)
epsilon = 1e-05
masked_score = -1e30
BQ = 256
PIECE = 896
VMEM_BYTES = 58 * 1024 * 1024
RED_ROWS = 256
HALF = 128


def layer_norm(values, gain_row, shift_row):
    centre = values - jnp.mean(values, axis=-1, keepdims=True)
    inverse = lax.rsqrt(jnp.mean(centre * centre, axis=-1, keepdims=True) + epsilon)
    normed = centre * inverse
    return (normed * gain_row + shift_row, normed, inverse)


def norm_back(grad_normed_out, normed, inverse, gain_row):
    scaled = grad_normed_out * gain_row
    middle = jnp.mean(scaled, axis=-1, keepdims=True)
    slope = jnp.mean(scaled * normed, axis=-1, keepdims=True)
    return inverse * (scaled - middle - normed * slope)


def times(left, right):
    return jnp.dot(left, right, preferred_element_type=jnp.float32)


def times_transposed(left, right):
    return lax.dot_general(
        left, right, (((1,), (1,)), ((), ())), preferred_element_type=jnp.float32
    )


def outer_sum(left, right):
    return lax.dot_general(
        left, right, (((0,), (0,)), ((), ())), preferred_element_type=jnp.float32
    )


def y_peer(me, d):
    return (me // 4) * 4 + lax.rem(lax.rem(me, 4) + d, 4)


def z_peer(me, d):
    return lax.rem(me + 4 * d, NR)


def any_peer(me, d):
    return lax.rem(me // 4 + d // 4, 4) * 4 + lax.rem(lax.rem(me, 4) + d % 4, 4)


def remote(src, dst, send, recv, where):
    return pltpu.make_async_remote_copy(
        src_ref=src,
        dst_ref=dst,
        send_sem=send,
        recv_sem=recv,
        device_id=where,
        device_id_type=MESH,
    )


def cost(microseconds):
    return pl.CostEstimate(flops=0, bytes_accessed=int(microseconds * 3.5e6), transcendentals=0)


def greet(places):
    barrier = pltpu.get_barrier_semaphore()
    for where in places:
        pl.semaphore_signal(barrier, inc=1, device_id=where, device_id_type=MESH)
    pl.semaphore_wait(barrier, len(places))


SWAP_ORDER = (10, 2, 8, 5, 15, 7, 13, 6, 9, 14, 11, 1, 4, 3, 12)


def swap_kernel(x, o, send, recv, local):
    me = lax.axis_index("replica")
    greet([{"replica": any_peer(me, d)} for d in range(1, NR)])
    copies = []
    for d in SWAP_ORDER:
        to = any_peer(me, d)
        copy = remote(x.at[to], o.at[me], send.at[d], recv.at[d], {"replica": to})
        copy.start()
        copies.append(copy)
    own = pltpu.make_async_copy(x.at[me], o.at[me], local)
    own.start()
    own.wait()
    for copy in copies:
        copy.wait()


def swap(x, collective_id):
    return pl.pallas_call(
        swap_kernel,
        out_shape=jax.ShapeDtypeStruct(x.shape, x.dtype),
        in_specs=[pl.BlockSpec(memory_space=pl.ANY)],
        out_specs=pl.BlockSpec(memory_space=pl.ANY),
        scratch_shapes=[
            pltpu.SemaphoreType.DMA((NR,)),
            pltpu.SemaphoreType.DMA((NR,)),
            pltpu.SemaphoreType.DMA,
        ],
        compiler_params=pltpu.CompilerParams(
            collective_id=collective_id, has_side_effects=True, vmem_limit_bytes=VMEM_BYTES
        ),
        cost_estimate=cost(16 if x.shape[1] > TQ else 9),
        name="swap",
    )(x)


W_SHAPES = ((272, 3264), (272, 1088), (272, 4352), (1088, 1088))
W_CUTS = (1408, 512, 1920, 512)
W_ENDS = (2816, 896, 3712, 896)


def weights_kernel(*refs):
    ins, docs, outs, all_docs, held = refs[:4], refs[4], refs[5:9], refs[9], refs[10:14]
    (own_s, own_r, local, back, xp_s, xp_r, xd_s, xd_r, xe_s, xe_r, f_s, f_r) = refs[14:26]
    (a1_s, a1_r, b1_s, b1_r, a2_s, a2_r, b2_s, b2_r, a3_s, a3_r, b3_s, b3_r, doc1_s, doc1_r, doc2_s, doc2_r) = refs[26:]
    j = lax.axis_index("shard")
    me = lax.axis_index("replica")
    z, y = me // 4, lax.rem(me, 4)
    xj = lax.rem(j + 2, 4)
    cj = j + 1 - 2 * lax.rem(j, 2)
    x_place, c_place = {"shard": xj}, {"shard": cj}
    y_places = [{"replica": y_peer(me, d)} for d in (1, 2, 3)]
    z_places = [{"replica": z_peer(me, d)} for d in (1, 2, 3)]
    greet([x_place, c_place] + y_places + z_places)

    def rows(start, count):
        return pl.ds(pl.multiple_of(start, 16), count)

    waits = []
    x_pieces, x_directs = [], []
    for a, (r, n) in enumerate(W_SHAPES):
        u = r // 17
        most = pl.ds(0, W_ENDS[a])
        piece = remote(ins[a].at[rows(me * u, u), most], outs[a].at[rows(j * r + me * u, u), most], xp_s.at[a], xp_r.at[a], x_place)
        piece.start()
        x_pieces.append(piece)
    for a, (r, n) in enumerate(W_SHAPES):
        u = r // 17
        most, rest = pl.ds(0, W_ENDS[a]), pl.ds(W_ENDS[a], n - W_ENDS[a])
        direct = remote(ins[a].at[rows(16 * u, u), most], outs[a].at[rows(j * r + 16 * u, u), most], xd_s.at[a], xd_r.at[a], x_place)
        direct.start()
        x_directs.append(direct)
        direct = remote(ins[a].at[:, rest], outs[a].at[rows(j * r, r), rest], xe_s.at[a], xe_r.at[a], x_place)
        direct.start()
        x_directs.append(direct)
    for a, (r, n) in enumerate(W_SHAPES):
        copy = remote(ins[a], outs[a].at[rows(j * r, r)], own_s.at[a], own_r.at[a], c_place)
        copy.start()
        waits.append(copy)
    all_docs[pl.ds(me, 1)] = docs[...][None]
    ours = all_docs.at[me]
    doc_firsts = [remote(ours, ours, doc1_s.at[i], doc1_r.at[i], y_places[i]) for i in range(3)]
    for copy in doc_firsts:
        copy.start()
    loads = [pltpu.make_async_copy(ins[a], held[a], local.at[a]) for a in range(4)]
    for copy in loads:
        copy.start()
    for a, (r, n) in enumerate(W_SHAPES):
        loads[a].wait()
        copy = pltpu.make_async_copy(held[a], outs[a].at[rows(j * r, r)], back.at[a])
        copy.start()
        waits.append(copy)
    for copy in doc_firsts:
        copy.wait()
    ours = all_docs.at[pl.ds(z * 4, 4)]
    for i in range(3):
        copy = remote(ours, ours, doc2_s.at[i], doc2_r.at[i], z_places[i])
        copy.start()
        waits.append(copy)
    firsts = []
    for a, (r, n) in enumerate(W_SHAPES):
        u, cut = r // 17, W_CUTS[a]
        x_pieces[a].wait()
        here = rows(xj * r + me * u, u)
        part_a = outs[a].at[here, pl.ds(0, cut)]
        part_b = outs[a].at[here, pl.ds(cut, W_ENDS[a] - cut)]
        group = []
        for i in range(3):
            group.append(remote(part_a, part_a, a1_s.at[a, i], a1_r.at[a, i], y_places[i]))
            group.append(remote(part_b, part_b, b1_s.at[a, i], b1_r.at[a, i], z_places[i]))
        for copy in group:
            copy.start()
        firsts.append(group)
    def row_part(a, first, half):
        r, u = W_SHAPES[a][0], W_SHAPES[a][0] // 17
        start = xj * r + lax.rem(first + 4, 4) * (4 * u) + half * (2 * u)
        return outs[a].at[rows(start, 2 * u), pl.ds(0, W_CUTS[a])]

    def column_part(a, first, k):
        r, u = W_SHAPES[a][0], W_SHAPES[a][0] // 17
        start = xj * r + (4 * k + lax.rem(first + 4, 4)) * u
        return outs[a].at[rows(start, u), pl.ds(W_CUTS[a], W_ENDS[a] - W_CUTS[a])]

    heres = []
    for a in range(4):
        for copy in firsts[a]:
            copy.wait()
        rights, lefts = [], []
        for k in range(2):
            ref = row_part(a, z, k)
            rights.append(remote(ref, ref, a2_s.at[a, k], a2_r.at[a, k], z_places[0]))
            ref = row_part(a, z, 1 - k)
            lefts.append(remote(ref, ref, a2_s.at[a, 2 + k], a2_r.at[a, 2 + k], z_places[2]))
        for k in range(4):
            ref = column_part(a, y, k)
            rights.append(remote(ref, ref, b2_s.at[a, k], b2_r.at[a, k], y_places[0]))
            ref = column_part(a, y, 3 - k)
            lefts.append(remote(ref, ref, b2_s.at[a, 4 + k], b2_r.at[a, 4 + k], y_places[2]))
        for copy in rights + lefts:
            copy.start()
        heres.append((rights, lefts))
    for a, (r, n) in enumerate(W_SHAPES):
        rights, lefts = heres[a]
        passed = []
        rights[0].wait()
        ref = row_part(a, z - 1, 0)
        passed.append(remote(ref, ref, a3_s.at[a, 0], a3_r.at[a, 0], z_places[0]))
        lefts[0].wait()
        ref = row_part(a, z + 1, 1)
        passed.append(remote(ref, ref, a3_s.at[a, 1], a3_r.at[a, 1], z_places[2]))
        for k in range(2):
            rights[2 + k].wait()
            ref = column_part(a, y - 1, k)
            passed.append(remote(ref, ref, b3_s.at[a, k], b3_r.at[a, k], y_places[0]))
            lefts[2 + k].wait()
            ref = column_part(a, y + 1, 3 - k)
            passed.append(remote(ref, ref, b3_s.at[a, 2 + k], b3_r.at[a, 2 + k], y_places[2]))
        for copy in passed:
            copy.start()
        for copy in rights[1:2] + rights[4:] + lefts[1:2] + lefts[4:] + passed:
            copy.wait()
        x_directs[2 * a].wait()
        x_directs[2 * a + 1].wait()
        whole = outs[a].at[rows(xj * r, r)]
        copy = remote(whole, whole, f_s.at[a], f_r.at[a], c_place)
        copy.start()
        waits.append(copy)
    for copy in waits:
        copy.wait()


def gather_weights(weights, docs):
    dma = pltpu.SemaphoreType.DMA
    outs = [jax.ShapeDtypeStruct((4 * r, n), jnp.bfloat16) for r, n in W_SHAPES]
    return pl.pallas_call(
        weights_kernel,
        out_shape=outs + [jax.ShapeDtypeStruct((NR, 8, 128), jnp.int32)],
        in_specs=[pl.BlockSpec(memory_space=pl.ANY)] * 4 + vmem_specs(1),
        out_specs=[pl.BlockSpec(memory_space=pl.ANY)] * 4 + vmem_specs(1),
        scratch_shapes=[pltpu.VMEM(shape, jnp.bfloat16) for shape in W_SHAPES]
        + [dma((4,))] * 12
        + [dma((4, 3))] * 4
        + [dma((4, 4))] * 2
        + [dma((4, 8))] * 2
        + [dma((4, 2))] * 2
        + [dma((4, 4))] * 2
        + [dma((3,))] * 4,
        compiler_params=pltpu.CompilerParams(
            collective_id=1, has_side_effects=True, vmem_limit_bytes=VMEM_BYTES
        ),
        name="gather_weights",
    )(*weights, docs)


def lane_mask(shape, micro):
    lane = lax.broadcasted_iota(jnp.int32, shape, len(shape) - 1)
    return (lane >= HD) if micro else (lane < HD)


def allowed_block(n0, n2, first_query, queries, keys):
    i = lax.broadcasted_iota(jnp.int32, (queries, keys), 0) + first_query
    j = lax.broadcasted_iota(jnp.int32, (queries, keys), 1)
    row = lax.broadcasted_iota(jnp.int32, (queries, 1), 0) + first_query
    start = jnp.where(row >= n2, n2, jnp.where(row >= n0, n0, 0))
    return (j <= i) & (j >= start)


def scores_of(q, k, micro, allowed):
    zero = jnp.zeros((), jnp.bfloat16)
    q = jnp.where(lane_mask(q.shape, micro), q, zero)
    s = lax.dot_general(q, k, (((1,), (1,)), ((), ())), preferred_element_type=jnp.float32)
    return jnp.where(allowed, s * SCALE, masked_score)


def take(x, entry, start, count):
    return x[pl.ds(start, count), entry].reshape(count * TQ, 2 * HD)


def forward_kernel(bounds, x, q16, o, o16, lse, lse16):
    zero = jnp.zeros((), jnp.bfloat16)
    me = lax.axis_index("replica")

    def attend(q, k, v, micro, first_query):
        allowed = allowed_block(bounds[micro], bounds[2 + micro], first_query, q.shape[0], k.shape[0])
        s = scores_of(q, k, micro, allowed)
        largest = jnp.max(s, axis=-1, keepdims=True)
        e = jnp.exp(s - largest)
        summed = jnp.sum(e, axis=-1, keepdims=True)
        p = (e * (1.0 / summed)).astype(jnp.bfloat16)
        v = jnp.where(lane_mask(v.shape, micro), v, zero)
        return times(p, v), largest + jnp.log(summed)

    per = BQ // TQ
    for b in range(SEQ // BQ):
        count = (b + 1) * per
        q = take(x, 0, b * per, per)
        k = take(x, 1, 0, count)
        v = take(x, 2, 0, count)
        o0, l0 = attend(q, k, v, 0, b * BQ)
        o1, l1 = attend(q, k, v, 1, b * BQ)
        o[pl.ds(b * per, per)] = (o0 + o1).astype(jnp.bfloat16).reshape(per, TQ, 2 * HD)
        lse[pl.ds(b * BQ, BQ)] = jnp.where(lane_mask((BQ, 2 * HD), 0), l0, l1)
    q = q16[...]
    k = take(x, 3, 0, NR)
    v = take(x, 4, 0, NR)
    o0, l0 = attend(q, k, v, 0, me * TQ)
    o1, l1 = attend(q, k, v, 1, me * TQ)
    o16[...] = (o0 + o1).astype(jnp.bfloat16)
    lse16[...] = jnp.where(lane_mask((TQ, 2 * HD), 0), l0, l1)


def vmem_specs(count):
    return [pl.BlockSpec(memory_space=pltpu.VMEM)] * count


def attention_forward(bounds, x, q16):
    f32, bf16 = jnp.float32, jnp.bfloat16
    return pl.pallas_call(
        forward_kernel,
        out_shape=[
            jax.ShapeDtypeStruct((NR, TQ, 2 * HD), bf16),
            jax.ShapeDtypeStruct((TQ, 2 * HD), bf16),
            jax.ShapeDtypeStruct((SEQ, 2 * HD), f32),
            jax.ShapeDtypeStruct((TQ, 2 * HD), f32),
        ],
        in_specs=[pl.BlockSpec(memory_space=pltpu.SMEM)] + vmem_specs(2),
        out_specs=vmem_specs(4),
        compiler_params=pltpu.CompilerParams(vmem_limit_bytes=VMEM_BYTES),
        cost_estimate=cost(5),
        name="attention_forward",
    )(bounds, x, q16)


def backward_kernel(bounds, x, q16, lse, lse16, do, do16, dx, dq16, dk, dv):
    zero = jnp.zeros((), jnp.bfloat16)
    me = lax.axis_index("replica")
    bf16 = jnp.bfloat16

    def pull(q, k, v, grad, logs, micro, first_query):
        allowed = allowed_block(bounds[micro], bounds[2 + micro], first_query, q.shape[0], k.shape[0])
        s = scores_of(q, k, micro, allowed)
        soft = jnp.exp(s - logs[:, micro * HD : micro * HD + 1])
        grad = jnp.where(lane_mask(grad.shape, micro), grad, zero)
        dp = times_transposed(grad, v)
        along = jnp.sum(soft * dp, axis=-1, keepdims=True)
        ds = (soft * (dp - along)).astype(bf16)
        q = jnp.where(lane_mask(q.shape, micro), q, zero)
        k = jnp.where(lane_mask(k.shape, micro), k, zero)
        return times(ds, k), outer_sum(ds, q), outer_sum(soft.astype(bf16), grad)

    per = BQ // TQ
    for b in reversed(range(SEQ // BQ)):
        count = (b + 1) * per
        q = take(x, 0, b * per, per)
        k = take(x, 1, 0, count)
        v = take(x, 2, 0, count)
        grad = do[pl.ds(b * per, per)].reshape(BQ, 2 * HD)
        logs = lse[pl.ds(b * BQ, BQ)]
        q0, k0, v0 = pull(q, k, v, grad, logs, 0, b * BQ)
        q1, k1, v1 = pull(q, k, v, grad, logs, 1, b * BQ)
        dx[pl.ds(b * per, per), 0] = ((q0 + q1) * SCALE).astype(bf16).reshape(per, TQ, 2 * HD)
        keys = pl.ds(0, (b + 1) * BQ)
        if b == SEQ // BQ - 1:
            dk[keys] = k0 + k1
            dv[keys] = v0 + v1
        else:
            dk[keys] += k0 + k1
            dv[keys] += v0 + v1
    dx[:, 1] = (dk[...] * SCALE).astype(bf16).reshape(NR, TQ, 2 * HD)
    dx[:, 2] = dv[...].astype(bf16).reshape(NR, TQ, 2 * HD)
    q = q16[...]
    k = take(x, 3, 0, NR)
    v = take(x, 4, 0, NR)
    q0, k0, v0 = pull(q, k, v, do16[...], lse16[...], 0, me * TQ)
    q1, k1, v1 = pull(q, k, v, do16[...], lse16[...], 1, me * TQ)
    dq16[...] = ((q0 + q1) * SCALE).astype(bf16)
    dx[:, 3] = ((k0 + k1) * SCALE).astype(bf16).reshape(NR, TQ, 2 * HD)
    dx[:, 4] = (v0 + v1).astype(bf16).reshape(NR, TQ, 2 * HD)


def attention_backward(bounds, x, q16, lse, lse16, do, do16):
    f32, bf16 = jnp.float32, jnp.bfloat16
    return pl.pallas_call(
        backward_kernel,
        out_shape=[
            jax.ShapeDtypeStruct((NR, 5, TQ, 2 * HD), bf16),
            jax.ShapeDtypeStruct((TQ, 2 * HD), bf16),
        ],
        in_specs=[pl.BlockSpec(memory_space=pltpu.SMEM)] + vmem_specs(6),
        out_specs=vmem_specs(2),
        scratch_shapes=[pltpu.VMEM((SEQ, 2 * HD), f32), pltpu.VMEM((SEQ, 2 * HD), f32)],
        compiler_params=pltpu.CompilerParams(vmem_limit_bytes=VMEM_BYTES),
        cost_estimate=cost(8),
        name="attention_backward",
    )(bounds, x, q16, lse, lse16, do, do16)


QKV = 3 * D
ENTER_BLOCK, LEAVE_BLOCK, BACK_ENTER_BLOCK = 1664, 2176, 640
LEFT_AT, LEFT_WIDTH = (0, 384, 768, 1152), 2304
EARLY_AT, EARLY_WIDTH = (0, 4352, 5504), 6656
LATE_WIDTH = 3328
SMALL = 1152


def low_lanes(shape):
    return lane_mask(shape, 0)


def to_blocks(upper, lower, odd):
    half = low_lanes(upper.shape)
    if odd:
        return jnp.where(half, pltpu.roll(upper, HD, 1), lower)
    return jnp.where(half, upper, pltpu.roll(lower, HD, 1))


def from_blocks(first, second):
    half = low_lanes(first.shape)
    upper = jnp.where(half, first, pltpu.roll(second, HD, 1))
    return upper, jnp.where(half, pltpu.roll(first, HD, 1), second)


def lines(start, count):
    return pl.ds(start, count)


def enter_kernel(x, gains, biases, w, message, q16, act, mixed):
    i = pl.program_id(0)

    @pl.when(i == 0)
    def _():
        normed, _, _ = layer_norm(x[...].astype(jnp.float32), gains[0:1], biases[0:1])
        act[...] = normed.astype(jnp.bfloat16)

    mixed[i] = times(act[...], w[...])

    @pl.when(i == pl.num_programs(0) - 1)
    def _():
        for b in range(3 * H):
            kind, head = divmod(b, H)
            i, t = divmod(b // 2, ENTER_BLOCK // 128)
            part = pl.ds(t * 128, 128)
            block = to_blocks(mixed[i, 0:TQ, part], mixed[i, TQ : 2 * TQ, part], b % 2)
            if kind != 1:
                row = 1 if kind == 0 else 2
                shift = biases[row : row + 1, head * HD : (head + 1) * HD]
                block = block + jnp.concatenate([shift, shift], axis=1)
            block = block.astype(jnp.bfloat16)
            if head < H - 1:
                message[head, kind * TQ : (kind + 1) * TQ] = block
            elif kind == 0:
                q16[...] = block
            else:
                for p in range(NR):
                    message[p, (kind + 2) * TQ : (kind + 3) * TQ] = block


def fixed(shape):
    return pl.BlockSpec(shape, lambda i: (0,) * len(shape))


def enter(x, gains, biases, w_qkv):
    bf16 = jnp.bfloat16
    steps = -(-QKV // ENTER_BLOCK)
    shapes = [(NR, 5 * TQ, 2 * HD), (TQ, 2 * HD), (2 * TQ, D)]
    return pl.pallas_call(
        enter_kernel,
        grid=(steps,),
        out_shape=[jax.ShapeDtypeStruct(shape, bf16) for shape in shapes],
        in_specs=[
            fixed(x.shape),
            fixed(gains.shape),
            fixed(biases.shape),
            pl.BlockSpec((D, ENTER_BLOCK), lambda i: (0, i)),
        ],
        out_specs=[fixed(shape) for shape in shapes],
        scratch_shapes=[pltpu.VMEM((steps, 2 * TQ, ENTER_BLOCK), jnp.float32)],
        compiler_params=pltpu.CompilerParams(vmem_limit_bytes=VMEM_BYTES),
        cost_estimate=cost(5),
        name="enter",
    )(x, gains, biases, w_qkv)


CURVE = 0.044715
ROOT = 0.7978845608028654


def weight_loads(w_out, w_up, w_down, v_out, v_up, v_down, sems):
    load_up, load_down = [], []
    for i in range(2):
        part = pl.ds(i * LEAVE_BLOCK, LEAVE_BLOCK)
        load_up.append(pltpu.make_async_copy(w_up.at[:, part], v_up.at[i], sems.at[1 + i]))
        load_down.append(pltpu.make_async_copy(w_down.at[part], v_down.at[i], sems.at[3 + i]))
    return pltpu.make_async_copy(w_out, v_out, sems.at[0]), load_up, load_down


def weight_buffers():
    bf16 = jnp.bfloat16
    return [
        pltpu.VMEM((D, D), bf16),
        pltpu.VMEM((2, D, LEAVE_BLOCK), bf16),
        pltpu.VMEM((2, LEAVE_BLOCK, D), bf16),
        pltpu.SemaphoreType.DMA((5,)),
    ]


def leave_kernel(
    x, o, o16, act1, gains, biases, up_shift, w_out, w_up, w_down,
    result, resid, pre, lefts, act2, total, v_out, v_up, v_down, sems,
):
    bf16 = jnp.bfloat16
    load_out, load_up, load_down = weight_loads(w_out, w_up, w_down, v_out, v_up, v_down, sems)
    load_out.start()
    for i in range(2):
        load_up[i].start()
        load_down[i].start()

    def attention_out():
        tiles = []
        for t in range(H // 2 + 1):
            first = o[2 * t] if 2 * t < H - 1 else o16[...]
            second = o[2 * t + 1] if 2 * t + 1 < H - 1 else o16[...]
            upper, lower = from_blocks(first.astype(jnp.float32), second.astype(jnp.float32))
            tiles.append(jnp.concatenate([upper, lower], axis=0))
        attended = jnp.concatenate(tiles, axis=1)[:, :D].astype(bf16)
        load_out.wait()
        r = x[...].astype(jnp.float32) + times(attended, v_out[...]) + biases[3:4]
        resid[...] = r
        normed, _, _ = layer_norm(r, gains[1:2], biases[4:5])
        act2[...] = normed.astype(bf16)
        for s in range(4):
            part = slice(s * 272, (s + 1) * 272)
            for at, value in zip(LEFT_AT, (act1, attended, act2)):
                lefts[s, :, at : at + 272] = value[:, part]
        total[...] = r + biases[5:6]

    attention_out()
    for i in range(2):
        part = slice(i * LEAVE_BLOCK, (i + 1) * LEAVE_BLOCK)
        load_up[i].wait()
        u = times(act2[...], v_up[i]) + up_shift[:, part]
        pre[:, part] = u
        g = (0.5 * u * (1.0 + jnp.tanh(ROOT * (u + CURVE * u * u * u)))).astype(bf16)
        for s in range(2):
            lefts[2 * i + s, :, LEFT_AT[3] : LEFT_AT[3] + D] = g[:, s * D : (s + 1) * D]
        load_down[i].wait()
        total[...] += times(g, v_down[i])
    result[...] = total[...].astype(bf16)


def leave(x, o, o16, act1, gains, biases, up_shift, weights):
    _, w_out, w_up, w_down = weights
    f32, bf16 = jnp.float32, jnp.bfloat16
    rows = 2 * TQ
    return pl.pallas_call(
        leave_kernel,
        out_shape=[
            jax.ShapeDtypeStruct((rows, D), bf16),
            jax.ShapeDtypeStruct((rows, D), f32),
            jax.ShapeDtypeStruct((rows, FF), f32),
            jax.ShapeDtypeStruct((4, rows, LEFT_WIDTH), bf16),
        ],
        in_specs=vmem_specs(7) + [pl.BlockSpec(memory_space=pl.ANY)] * 3,
        out_specs=vmem_specs(4),
        scratch_shapes=[pltpu.VMEM((rows, D), bf16), pltpu.VMEM((rows, D), f32)] + weight_buffers(),
        compiler_params=pltpu.CompilerParams(vmem_limit_bytes=VMEM_BYTES),
        cost_estimate=cost(12),
        name="leave",
    )(x, o, o16, act1, gains, biases, up_shift, w_out, w_up, w_down)


def column_sum(value):
    return jnp.sum(value, axis=0, keepdims=True)


def back_leave_kernel(
    dy, resid, pre, gains, w_out, w_up, w_down,
    early, grad_resid, do, do16, sums, total, v_out, v_up, v_down, sems,
):
    f32, bf16 = jnp.float32, jnp.bfloat16
    load_out, load_up, load_down = weight_loads(w_out, w_up, w_down, v_out, v_up, v_down, sems)
    for i in range(2):
        load_down[i].start()
        load_up[i].start()
    load_out.start()
    total[...] = jnp.zeros_like(total)
    for i in range(2):
        part = slice(i * LEAVE_BLOCK, (i + 1) * LEAVE_BLOCK)
        u = pre[:, part]
        load_down[i].wait()
        grad_hidden = times_transposed(dy[...], v_down[i])
        t = jnp.tanh(ROOT * (u + CURVE * u * u * u))
        slope = 0.5 * (1.0 + t) + 0.5 * u * (1.0 - t * t) * (ROOT * (1.0 + 3.0 * CURVE * u * u))
        du = (grad_hidden * slope).astype(bf16)
        early[:, part] = du
        du_sum = column_sum(du.astype(f32))
        for s in range(2):
            sums[4 + 2 * i + s : 5 + 2 * i + s, 0:D] = du_sum[:, s * D : (s + 1) * D]
        load_up[i].wait()
        total[...] += times_transposed(du, v_up[i])
    load_out.wait()

    def norm_and_heads():
        da2 = total[...]
        _, normed, inverse = layer_norm(resid[...], gains[1:2], 0.0)
        dr = dy[...].astype(f32) + norm_back(da2, normed, inverse, gains[1:2])
        grad_resid[...] = dr
        db = dr.astype(bf16)
        for at in EARLY_AT[1:]:
            early[:, at + 1024 : at + 1152] = jnp.zeros((2 * TQ, 128), bf16)
        early[:, EARLY_AT[1] : EARLY_AT[1] + D] = db
        early[:, EARLY_AT[2] : EARLY_AT[2] + D] = dy[...]
        sums[0:1, 0:D] = column_sum(da2 * normed)
        sums[1:2, 0:D] = column_sum(da2)
        sums[2:3, 0:D] = column_sum(db.astype(f32))
        sums[3:4, 0:D] = column_sum(dy[...].astype(f32))
        heads = times_transposed(db, v_out[...])
        heads = jnp.concatenate([heads, jnp.zeros((2 * TQ, HD), f32)], axis=1)
        for b in range(H):
            tile = heads[:, (b // 2) * 128 : (b // 2 + 1) * 128]
            block = to_blocks(tile[0:TQ], tile[TQ : 2 * TQ], b % 2).astype(bf16)
            if b < H - 1:
                do[b] = block
            else:
                do16[...] = block

    norm_and_heads()


def back_leave(dy, resid, pre, gains, weights):
    _, w_out, w_up, w_down = weights
    f32, bf16 = jnp.float32, jnp.bfloat16
    rows = 2 * TQ
    shapes = [(rows, EARLY_WIDTH), (rows, D), (NR, TQ, 2 * HD), (TQ, 2 * HD), (8, SMALL)]
    types = [bf16, f32, bf16, bf16, f32]
    return pl.pallas_call(
        back_leave_kernel,
        out_shape=[jax.ShapeDtypeStruct(shape, t) for shape, t in zip(shapes, types)],
        in_specs=vmem_specs(4) + [pl.BlockSpec(memory_space=pl.ANY)] * 3,
        out_specs=vmem_specs(5),
        scratch_shapes=[pltpu.VMEM((rows, D), f32)] + weight_buffers(),
        compiler_params=pltpu.CompilerParams(vmem_limit_bytes=VMEM_BYTES),
        cost_estimate=cost(14),
        name="back_leave",
    )(dy, resid, pre, gains, w_out, w_up, w_down)


def back_enter_kernel(x, back, dq16, grad_resid, before, gains, w, late, grad_in, sums, held, sems):
    f32, bf16 = jnp.float32, jnp.bfloat16
    pieces = [pl.ds(0, BACK_ENTER_BLOCK), pl.ds(BACK_ENTER_BLOCK, D - BACK_ENTER_BLOCK)]
    loads = [pltpu.make_async_copy(w.at[p], held.at[p], sems.at[i]) for i, p in enumerate(pieces)]
    for load in loads:
        load.start()

    def unpack():
        def last(kind):
            total = back[0, (kind + 2) * TQ : (kind + 3) * TQ].astype(f32)
            for p in range(1, NR):
                total = total + back[p, (kind + 2) * TQ : (kind + 3) * TQ].astype(f32)
            return total

        def block(b):
            kind, head = divmod(b, H)
            if head < H - 1:
                return back[head, kind * TQ : (kind + 1) * TQ].astype(f32)
            return dq16[...].astype(f32) if kind == 0 else last(kind)

        for t in range(3 * H // 2 + 1):
            first = block(2 * t)
            second = block(2 * t + 1) if 2 * t + 1 < 3 * H else jnp.zeros_like(first)
            upper, lower = from_blocks(first, second)
            late[0:TQ, t * 128 : (t + 1) * 128] = upper.astype(bf16)
            late[TQ : 2 * TQ, t * 128 : (t + 1) * 128] = lower.astype(bf16)

    unpack()
    products = []
    for load, piece in zip(loads, pieces):
        load.wait()
        products.append(times_transposed(late[:, 0:QKV], held[piece]))

    def finish():
        da1 = jnp.concatenate(products, axis=1)
        _, normed, inverse = layer_norm(x[...].astype(f32), gains[0:1], 0.0)
        dx = grad_resid[...] + norm_back(da1, normed, inverse, gains[0:1])
        grad_in[...] = dx.astype(bf16)
        sums[...] = jnp.zeros_like(sums)
        sums[0:1, 0:D] = column_sum(da1 * normed)
        sums[1:2, 0:D] = column_sum(da1)
        sums[2:3, 0:D] = column_sum(late[:, 0:D].astype(f32))
        sums[3:4, 0:D] = column_sum(late[:, 2 * D : QKV].astype(f32))
        sums[4:12, 0:D] = before[:, 0:D]

    finish()


def back_enter(x, back, dq16, grad_resid, before, gains, w_qkv):
    f32, bf16 = jnp.float32, jnp.bfloat16
    rows = 2 * TQ
    return pl.pallas_call(
        back_enter_kernel,
        out_shape=[
            jax.ShapeDtypeStruct((rows, LATE_WIDTH), bf16),
            jax.ShapeDtypeStruct((rows, D), bf16),
            jax.ShapeDtypeStruct((16, SMALL), f32),
        ],
        in_specs=vmem_specs(6) + [pl.BlockSpec(memory_space=pl.ANY)],
        out_specs=vmem_specs(3),
        scratch_shapes=[pltpu.VMEM((D, QKV), bf16), pltpu.SemaphoreType.DMA((2,))],
        compiler_params=pltpu.CompilerParams(vmem_limit_bytes=VMEM_BYTES),
        cost_estimate=cost(5),
        name="back_enter",
    )(x, back, dq16, grad_resid, before, gains, w_qkv)


AT_OUT, AT_UP, AT_DOWN, DOWN_STEP = 3584, 4736, 9088, 1152
LATE_FREE, LATE_CHUNK = 3328, 256
EARLY_FREE, EARLY_CHUNK = 13696, 640


def weight_sums_kernel(
    l0, l1, l2, l3, e0, e1, e2, late, small, out,
    lefts, early, mixed, got, strip, g, tr, ins, ad, part, mid, fin,
    loc, late_s, late_r, small_s, small_r,
    p_s, p_r, q_s, q_r, m_s, m_r, n_s, n_r, e_s, e_r, w_s, w_r, last,
):
    f32, bf16 = jnp.float32, jnp.bfloat16
    rows = 2 * TQ
    j = lax.axis_index("shard")
    me = lax.axis_index("replica")
    z, y = me // 4, lax.rem(me, 4)
    xj = lax.rem(j + 2, 4)
    cj = j + 1 - 2 * lax.rem(j, 2)
    places = [{"shard": xj}, {"shard": cj}, {"shard": lax.rem(cj + 2, 4)}]
    y_places = [{"replica": y_peer(me, d)} for d in (1, 2, 3)]
    z_places = [{"replica": z_peer(me, d)} for d in (1, 2, 3)]
    greet(places + y_places + z_places)

    def slot(ref, k):
        return ref.at[pl.ds(k * rows, rows)]

    across = remote(late, slot(mixed, 1), late_s.at[0], late_r.at[0], places[0])
    across.start()
    beside = remote(late, slot(mixed, 2), late_s.at[1], late_r.at[1], places[1])
    beside.start()
    early_relay = remote(e1, slot(early, 3), late_s.at[3], late_r.at[3], places[1])
    early_relay.start()
    smalls = [remote(small, got.at[k], small_s.at[k], small_r.at[k], places[k]) for k in range(3)]
    for copy in smalls:
        copy.start()
    loads = [pltpu.make_async_copy(late, slot(mixed, 0), loc.at[0])]
    loads.append(pltpu.make_async_copy(l0.at[j], slot(lefts, 0), loc.at[1]))
    for k, ref in enumerate((l1, l2, l3)):
        loads.append(pltpu.make_async_copy(ref, slot(lefts, k + 1), loc.at[2 + k]))
    for k, ref in enumerate((e0, e1, e2)):
        loads.append(pltpu.make_async_copy(ref, slot(early, k), loc.at[5 + k]))
    for copy in loads:
        copy.start()
    for copy in loads:
        copy.wait()
    early_relay.wait()

    def keep(product, put_at):
        g[:, put_at] = product[0:RED_ROWS]
        strip[:, put_at] = product[RED_ROWS:272]

    def stripe(left_at, right, right_at, at, columns, width):
        @pl.loop(0, columns // width)
        def _(i):
            take_at = pl.ds(pl.multiple_of(right_at + i * width, 128), width)
            put_at = pl.ds(pl.multiple_of(at + i * width, 128), width)
            product = outer_sum(lefts[:, left_at : left_at + 272], right[:, take_at])
            keep(product.astype(bf16), put_at)

    stripe(LEFT_AT[2], early, EARLY_AT[0], AT_UP, FF, 2176)
    product = outer_sum(lefts[:, LEFT_AT[1] : LEFT_AT[1] + 272], early[:, EARLY_AT[1] : EARLY_AT[2]])
    keep(product.astype(bf16), slice(AT_OUT, AT_UP))
    for s in range(4):
        at = AT_DOWN + s * DOWN_STEP
        first = LEFT_AT[3] + s * 272
        product = outer_sum(lefts[:, first : first + 272], early[:, EARLY_AT[2] : EARLY_WIDTH])
        keep(product.astype(bf16), slice(at, at + DOWN_STEP))
    g[:, EARLY_FREE:] = jnp.zeros((RED_ROWS, EARLY_CHUNK), bf16)
    for c in range(16):
        first = AT_OUT + c * EARLY_CHUNK
        width = min(EARLY_CHUNK, EARLY_FREE - first)
        g[16 * c : 16 * c + 16, EARLY_FREE : EARLY_FREE + width] = strip[:, first : first + width]

    firsts, seconds = (y_places, z_places), (z_places, y_places)
    here, there = (y, z), (z, y)

    def at(side, first, second):
        piece = 4 * second + lax.rem(first + 4, 4)
        return (pl.ds(side * HALF, HALF), pl.ds(pl.multiple_of(piece * PIECE, 128), PIECE))

    def piece_of(ref, side, first, second):
        return ref.at[at(side, first, second)]

    def value_of(side, first, second):
        return g[at(side, first, second)].astype(f32)

    opened, direct, added = {}, {}, {}

    def open_piece(s, k):
        t, right, left = here[s], firsts[s][0], firsts[s][2]
        copy = remote(piece_of(g, s, t + 2, k), tr.at[s, k], p_s.at[s, k], p_r.at[s, k], right if k < 2 else left)
        copy.start()
        opened[s, k] = copy

    def direct_piece(s, k):
        t, right, left = here[s], firsts[s][0], firsts[s][2]
        if k < 2:
            copy = remote(piece_of(g, s, t - 1, k), ins.at[s, 1, k], p_s.at[s, 4 + k], p_r.at[s, 4 + k], left)
        else:
            copy = remote(piece_of(g, s, t + 1, k), ins.at[s, 0, k], p_s.at[s, 4 + k], p_r.at[s, 4 + k], right)
        copy.start()
        direct[s, k] = copy

    def add_piece(s, k):
        t, right, left = here[s], firsts[s][0], firsts[s][2]
        opened[s, k].wait()
        mine = value_of(s, t + 1 if k < 2 else t - 1, k)
        ad[s, k] = (tr[s, k].astype(f32) + mine).astype(bf16)
        to, side = (right, 0) if k < 2 else (left, 1)
        copy = remote(ad.at[s, k], ins.at[s, side, k], q_s.at[s, k], q_r.at[s, k], to)
        copy.start()
        added[s, k] = copy

    for k in (1, 2, 3):
        for s in range(2):
            open_piece(s, k)
    for k in (1, 2, 3):
        for s in range(2):
            direct_piece(s, k)
    for k in (1, 2):
        for s in range(2):
            add_piece(s, k)
    across.wait()
    relay = remote(slot(mixed, 1), slot(mixed, 3), late_s.at[2], late_r.at[2], places[1])
    relay.start()
    beside.wait()
    for s in range(2):
        add_piece(s, 3)
    relay.wait()
    stripe(LEFT_AT[0], mixed, 0, 0, LATE_WIDTH, 1664)
    for copy in smalls:
        copy.wait()
    for c in range(13):
        g[16 * c : 16 * c + 16, LATE_FREE:AT_OUT] = strip[:, c * LATE_CHUNK : (c + 1) * LATE_CHUNK]
    sums = (small[...] + got[0] + got[1] + got[2]).astype(bf16)
    for c in range(3):
        row = 208 + 16 * c
        g[row : row + 16, LATE_FREE:AT_OUT] = sums[:, c * LATE_CHUNK : (c + 1) * LATE_CHUNK]
    for c in range(5):
        first = 3 * LATE_CHUNK + c * 64
        g[16 * c : 16 * c + 16, QKV:LATE_FREE] = sums[:, first : first + 64]
    for s in range(2):
        open_piece(s, 0)
        direct_piece(s, 0)
    for s in range(2):
        add_piece(s, 0)

    middles = []
    for s in range(2):
        for k in range(4):
            direct[s, k].wait()
            added[s, k].wait()
            part[s, k] = (value_of(s, here[s], k) + ins[s, 0, k].astype(f32) + ins[s, 1, k].astype(f32)).astype(bf16)
        group = []
        for i in range(3):
            to = lax.rem(there[s] + 1 + i, 4)
            group.append(remote(part.at[s, to], mid.at[s, i], m_s.at[s, i], m_r.at[s, i], seconds[s][i]))
        for copy in group:
            copy.start()
        middles.append(group)
    backs = []
    for s in range(2):
        for copy in middles[s]:
            copy.wait()
        total = part[s, there[s]].astype(f32)
        for i in range(3):
            total = total + mid[s, i].astype(f32)
        fin[s] = total.astype(bf16)
        where = piece_of(out, s, here[s], there[s])
        group = [remote(fin.at[s], where, n_s.at[s, i], n_r.at[s, i], seconds[s][i]) for i in range(3)]
        group.append(pltpu.make_async_copy(fin.at[s], where, last.at[s]))
        for copy in group:
            copy.start()
        backs.append(group)
    to_rights, to_lefts = [], []
    for s in range(2):
        t, right, left = here[s], firsts[s][0], firsts[s][2]
        for copy in backs[s]:
            copy.wait()
        to_right, to_left = [], []
        for k in range(4):
            ref = piece_of(out, s, t, k)
            to_right.append(remote(ref, ref, e_s.at[s, k], e_r.at[s, k], right))
            ref = piece_of(out, s, t, 3 - k)
            to_left.append(remote(ref, ref, e_s.at[s, 4 + k], e_r.at[s, 4 + k], left))
        for k in range(4):
            to_right[k].start()
            to_left[k].start()
        to_rights.append(to_right)
        to_lefts.append(to_left)
    passed = []
    for k in range(2):
        for s in range(2):
            t, right, left = here[s], firsts[s][0], firsts[s][2]
            to_rights[s][k].wait()
            ref = piece_of(out, s, t - 1, k)
            copy = remote(ref, ref, w_s.at[s, k], w_r.at[s, k], right)
            copy.start()
            passed.append(copy)
            to_lefts[s][k].wait()
            ref = piece_of(out, s, t + 1, 3 - k)
            copy = remote(ref, ref, w_s.at[s, 2 + k], w_r.at[s, 2 + k], left)
            copy.start()
            passed.append(copy)
    for s in range(2):
        for copy in to_rights[s][2:] + to_lefts[s][2:]:
            copy.wait()
    for copy in passed:
        copy.wait()


def weight_sums(lefts, early, late, small):
    dma = pltpu.SemaphoreType.DMA
    f32, bf16 = jnp.float32, jnp.bfloat16
    anywhere = pl.BlockSpec(memory_space=pl.ANY)
    piece = (HALF, PIECE)
    return pl.pallas_call(
        weight_sums_kernel,
        out_shape=jax.ShapeDtypeStruct((RED_ROWS, NR * PIECE), bf16),
        in_specs=[anywhere] * 8 + vmem_specs(1),
        out_specs=anywhere,
        scratch_shapes=[
            pltpu.VMEM((8 * TQ, LEFT_WIDTH), bf16),
            pltpu.VMEM((8 * TQ, EARLY_WIDTH), bf16),
            pltpu.VMEM((8 * TQ, LATE_WIDTH), bf16),
            pltpu.VMEM((3, 16, SMALL), f32),
            pltpu.VMEM((16, NR * PIECE), bf16),
            pltpu.VMEM((RED_ROWS, NR * PIECE), bf16),
            pltpu.VMEM((2, 4) + piece, bf16),
            pltpu.VMEM((2, 2, 4) + piece, bf16),
            pltpu.VMEM((2, 4) + piece, bf16),
            pltpu.VMEM((2, 4) + piece, bf16),
            pltpu.VMEM((2, 3) + piece, bf16),
            pltpu.VMEM((2,) + piece, bf16),
            dma((8,)),
            dma((4,)), dma((4,)), dma((3,)), dma((3,)),
        ]
        + [dma((2, 8))] * 2
        + [dma((2, 4))] * 2
        + [dma((2, 3))] * 4
        + [dma((2, 8))] * 2
        + [dma((2, 4))] * 2
        + [dma((2,))],
        compiler_params=pltpu.CompilerParams(
            collective_id=2, has_side_effects=True, vmem_limit_bytes=VMEM_BYTES
        ),
        name="weight_sums",
    )(*lefts, *early, late, small)


def widen_kernel(g, qkv, out, up, down, small, late_free, early_free):
    i = pl.program_id(0)
    f32 = jnp.float32

    @pl.when(i < 4)
    def _():
        qkv[...] = g[:, 0:QKV].astype(f32)
        out[...] = g[:, AT_OUT : AT_OUT + D].astype(f32)
        up[...] = g[:, AT_UP : AT_UP + FF].astype(f32)
        for s in range(4):
            at = AT_DOWN + s * DOWN_STEP
            down[s] = g[:, at : at + D].astype(f32)
        rows = pl.ds(pl.multiple_of(i * 64, 64), 64)
        late_free[rows] = g[:, LATE_FREE - 128 : AT_OUT]
        early_free[rows] = g[:, EARLY_FREE:]

    @pl.when(i == 4)
    def _():
        late = [late_free[16 * c : 16 * c + 16, 128:].astype(f32) for c in range(16)]
        qkv[0:16] = jnp.concatenate(late[:13], axis=1)[:, :QKV]
        early = [early_free[16 * c : 16 * c + 16, :].astype(f32) for c in range(16)]
        rest = jnp.concatenate(early, axis=1)
        out[0:16] = rest[:, 0:D]
        first = AT_UP - AT_OUT
        up[0:16] = rest[:, first : first + FF]
        for s in range(4):
            at = AT_DOWN - AT_OUT + s * DOWN_STEP
            down[s, 0:16] = rest[:, at : at + D]
        small[:, 0:768] = jnp.concatenate(late[13:], axis=1)
        for c in range(5):
            small[:, 768 + 64 * c : 832 + 64 * c] = late_free[16 * c : 16 * c + 16, 64:128].astype(f32)
        small[:, 1088:SMALL] = jnp.zeros((16, SMALL - 1088), f32)


def widen(g):
    f32, bf16 = jnp.float32, jnp.bfloat16
    return pl.pallas_call(
        widen_kernel,
        grid=(5,),
        out_shape=[
            jax.ShapeDtypeStruct((272, QKV), f32),
            jax.ShapeDtypeStruct((272, D), f32),
            jax.ShapeDtypeStruct((272, FF), f32),
            jax.ShapeDtypeStruct((4, 272, D), f32),
            jax.ShapeDtypeStruct((16, SMALL), f32),
        ],
        in_specs=[pl.BlockSpec((64, NR * PIECE), lambda i: (jnp.minimum(i, 3), 0))],
        out_specs=[
            pl.BlockSpec((64, QKV), lambda i: (i, 0)),
            pl.BlockSpec((64, D), lambda i: (i, 0)),
            pl.BlockSpec((64, FF), lambda i: (i, 0)),
            pl.BlockSpec((4, 64, D), lambda i: (0, i, 0)),
            fixed((16, SMALL)),
        ],
        scratch_shapes=[
            pltpu.VMEM((RED_ROWS, 384), bf16),
            pltpu.VMEM((RED_ROWS, EARLY_CHUNK), bf16),
        ],
        compiler_params=pltpu.CompilerParams(vmem_limit_bytes=VMEM_BYTES),
        name="widen",
    )(g)


def layer_forward(x, bounds, gains, biases, up_shift, weights):
    message, q16, act1 = enter(x, gains, biases, weights[0])
    whole = swap(message, 3).reshape(NR, 5, TQ, 2 * HD)
    o, o16, lse, lse16 = attention_forward(bounds, whole, q16)
    result, resid, pre, lefts = leave(x, swap(o, 4), o16, act1, gains, biases, up_shift, weights)
    return result, (whole, q16, lse, lse16, resid, pre), lefts


def layer_backward(dy, x, kept, bounds, gains, weights, tie=None):
    whole, q16, lse, lse16, resid, pre = kept
    early, grad_resid, do, do16, sums = back_leave(dy, resid, pre, gains, weights)
    dx, dq16 = attention_backward(bounds, whole, q16, lse, lse16, swap(do, 4), do16)
    dx, tie = lax.optimization_barrier((dx, tie))
    back = swap(dx.reshape(NR, 5 * TQ, 2 * HD), 3)
    late, grad_in, small = back_enter(x, back, dq16, grad_resid, sums, gains, weights[0])
    return grad_in, early, late, small, tie


X_ROUTE = [(j, j ^ 2) for j in range(4)]
C_ROUTE = [(j, j ^ 1) for j in range(4)]


CX_ROUTE = [(j, j ^ 3) for j in range(4)]


def everyone(value):
    return value, lax.ppermute(value, "shard", X_ROUTE), lax.ppermute(value, "shard", C_ROUTE)


def own_columns(cut):
    j = lax.axis_index("shard")

    def of(shard):
        return lax.dynamic_index_in_dim(cut, shard, 0, keepdims=False)

    across, beside = lax.rem(j + 2, 4), j + 1 - 2 * lax.rem(j, 2)
    return (
        cut,
        lax.ppermute(of(across), "shard", X_ROUTE),
        lax.ppermute(of(beside), "shard", C_ROUTE),
        lax.ppermute(of(lax.rem(beside + 2, 4)), "shard", CX_ROUTE),
    )


def shards(tokens, cotangent, doc_ids, gains, biases, up_bias, w_qkv, w_out, w_up, w_down):
    is_first = lax.axis_index("section") == 0
    ids = doc_ids[:, 0]
    counts = jnp.stack([jnp.sum((ids == n).astype(jnp.int32), axis=1) for n in (0, 2)])
    counts = jnp.pad(counts, ((0, 6), (0, 126)))
    *weights, counts = gather_weights((w_qkv[0], w_out[0], w_up[0], w_down[0]), counts)
    counts = jnp.sum(counts[:, :2, :2], axis=0)
    bounds = jnp.concatenate([counts[0], SEQ - counts[1]])
    gains, biases = gains[0], biases[0]
    own_in = tokens.reshape(2 * TQ, D)
    own_cot = cotangent.reshape(2 * TQ, D)
    result, _, _ = layer_forward(own_in, bounds, gains, biases, up_bias, weights)
    inbox = lax.ppermute(result, "section", [(0, 1)])
    inputs = jnp.where(is_first, own_in, inbox)
    layer_out, kept, lefts = layer_forward(inputs, bounds, gains, biases, up_bias, weights)
    lefts = own_columns(lefts)
    grad_in, _, _, _, others = layer_backward(own_cot, inputs, kept, bounds, gains, weights, lefts[1:])
    lefts = (lefts[0], *others)
    inbox = lax.ppermute(grad_in, "section", [(1, 0)])
    dy = jnp.where(is_first, inbox, own_cot)
    grad_in, early, late, small, _ = layer_backward(dy, inputs, kept, bounds, gains, weights)
    summed = weight_sums(lefts, everyone(early), late, small)
    qkv, out, up, down, small = widen(summed)
    small = small[:, :D]
    return (
        layer_out.reshape(1, 2, 1, TQ, D),
        grad_in.reshape(1, 2, 1, TQ, D),
        jnp.stack([small[0], small[4]])[None],
        jnp.stack([small[k] for k in (1, 2, 3, 6, 5, 7)])[None],
        small[8:12].reshape(1, FF),
        qkv[None],
        out[None],
        up[None],
        down.reshape(1, 1088, D),
    )


def solution(mesh):
    placed = (
        P(None, "shard", "replica", None),
        P(None, "shard", "replica", None),
        P(None, "shard", "replica"),
        P("section", None, None),
        P("section", None, None),
        P("section", None),
        P("section", "shard", None),
        P("section", "shard", None),
        P("section", "shard", None),
        P("section", "shard", None),
    )
    return jax.shard_map(
        shards,
        mesh=mesh,
        in_specs=placed,
        out_specs=(
            P("section", None, "shard", "replica", None),
            P("section", None, "shard", "replica", None),
            P("section", None, None),
            P("section", None, None),
            P("section", None),
            P("section", "shard", None),
            P("section", "shard", None),
            P("section", "shard", None),
            P("section", "shard", None),
        ),
        check_vma=False,
    )
```

```python
import functools

import jax
import jax.numpy as jnp
from jax import lax
from jax.experimental import pallas as pl
from jax.experimental.pallas import tpu as pltpu
from jax.sharding import PartitionSpec as P

MESH = pl.DeviceIdType.MESH
H = 17
HD = 64
TQ = 64
SEQ = 1024
NR = 16
D = 1088
FF = 4352
SCALE = HD ** (-0.5)
epsilon = 1e-05
masked_score = -1e30
BQ = 256
PIECE = 896
VMEM_BYTES = 58 * 1024 * 1024
RED_ROWS = 256
HALF = 128


def layer_norm(values, gain_row, shift_row):
    centre = values - jnp.mean(values, axis=-1, keepdims=True)
    inverse = lax.rsqrt(jnp.mean(centre * centre, axis=-1, keepdims=True) + epsilon)
    normed = centre * inverse
    return (normed * gain_row + shift_row, normed, inverse)


def norm_back(grad_normed_out, normed, inverse, gain_row):
    scaled = grad_normed_out * gain_row
    middle = jnp.mean(scaled, axis=-1, keepdims=True)
    slope = jnp.mean(scaled * normed, axis=-1, keepdims=True)
    return inverse * (scaled - middle - normed * slope)


def times(left, right):
    return jnp.dot(left, right, preferred_element_type=jnp.float32)


def times_transposed(left, right):
    return lax.dot_general(
        left, right, (((1,), (1,)), ((), ())), preferred_element_type=jnp.float32
    )


def outer_sum(left, right):
    return lax.dot_general(
        left, right, (((0,), (0,)), ((), ())), preferred_element_type=jnp.float32
    )


def y_peer(me, d):
    return (me // 4) * 4 + lax.rem(lax.rem(me, 4) + d, 4)


def z_peer(me, d):
    return lax.rem(me + 4 * d, NR)


def any_peer(me, d):
    return lax.rem(me // 4 + d // 4, 4) * 4 + lax.rem(lax.rem(me, 4) + d % 4, 4)


def remote(src, dst, send, recv, where):
    return pltpu.make_async_remote_copy(
        src_ref=src,
        dst_ref=dst,
        send_sem=send,
        recv_sem=recv,
        device_id=where,
        device_id_type=MESH,
    )


def cost(microseconds):
    return pl.CostEstimate(flops=0, bytes_accessed=int(microseconds * 3.5e6), transcendentals=0)


def greet(places):
    barrier = pltpu.get_barrier_semaphore()
    for where in places:
        pl.semaphore_signal(barrier, inc=1, device_id=where, device_id_type=MESH)
    pl.semaphore_wait(barrier, len(places))


SWAP_ORDER = (10, 2, 8, 5, 15, 7, 13, 6, 9, 14, 11, 1, 4, 3, 12)


def swap_kernel(x, o, send, recv, local):
    me = lax.axis_index("replica")
    greet([{"replica": any_peer(me, d)} for d in range(1, NR)])
    copies = []
    for d in SWAP_ORDER:
        to = any_peer(me, d)
        copy = remote(x.at[to], o.at[me], send.at[d], recv.at[d], {"replica": to})
        copy.start()
        copies.append(copy)
    own = pltpu.make_async_copy(x.at[me], o.at[me], local)
    own.start()
    own.wait()
    for copy in copies:
        copy.wait()


def swap(x, collective_id):
    return pl.pallas_call(
        swap_kernel,
        out_shape=jax.ShapeDtypeStruct(x.shape, x.dtype),
        in_specs=[pl.BlockSpec(memory_space=pl.ANY)],
        out_specs=pl.BlockSpec(memory_space=pl.ANY),
        scratch_shapes=[
            pltpu.SemaphoreType.DMA((NR,)),
            pltpu.SemaphoreType.DMA((NR,)),
            pltpu.SemaphoreType.DMA,
        ],
        compiler_params=pltpu.CompilerParams(
            collective_id=collective_id, has_side_effects=True, vmem_limit_bytes=VMEM_BYTES
        ),
        cost_estimate=cost(16 if x.shape[1] > TQ else 9),
        name="swap",
    )(x)


W_SHAPES = ((272, 3264), (272, 1088), (272, 4352), (1088, 1088))
W_CUTS = (1408, 512, 1920, 512)
W_ENDS = (2816, 896, 3712, 896)


def weights_kernel(*refs):
    ins, docs, outs, all_docs, held = refs[:4], refs[4], refs[5:9], refs[9], refs[10:14]
    (own_s, own_r, local, back, xp_s, xp_r, xd_s, xd_r, xe_s, xe_r, f_s, f_r) = refs[14:26]
    (a1_s, a1_r, b1_s, b1_r, a2_s, a2_r, b2_s, b2_r, a3_s, a3_r, b3_s, b3_r, doc1_s, doc1_r, doc2_s, doc2_r) = refs[26:]
    j = lax.axis_index("shard")
    me = lax.axis_index("replica")
    z, y = me // 4, lax.rem(me, 4)
    xj = lax.rem(j + 2, 4)
    cj = j + 1 - 2 * lax.rem(j, 2)
    x_place, c_place = {"shard": xj}, {"shard": cj}
    y_places = [{"replica": y_peer(me, d)} for d in (1, 2, 3)]
    z_places = [{"replica": z_peer(me, d)} for d in (1, 2, 3)]
    greet([x_place, c_place] + y_places + z_places)

    def rows(start, count):
        return pl.ds(pl.multiple_of(start, 16), count)

    waits = []
    x_pieces, x_directs = [], []
    for a, (r, n) in enumerate(W_SHAPES):
        u = r // 17
        most = pl.ds(0, W_ENDS[a])
        piece = remote(ins[a].at[rows(me * u, u), most], outs[a].at[rows(j * r + me * u, u), most], xp_s.at[a], xp_r.at[a], x_place)
        piece.start()
        x_pieces.append(piece)
    for a, (r, n) in enumerate(W_SHAPES):
        u = r // 17
        most, rest = pl.ds(0, W_ENDS[a]), pl.ds(W_ENDS[a], n - W_ENDS[a])
        direct = remote(ins[a].at[rows(16 * u, u), most], outs[a].at[rows(j * r + 16 * u, u), most], xd_s.at[a], xd_r.at[a], x_place)
        direct.start()
        x_directs.append(direct)
        direct = remote(ins[a].at[:, rest], outs[a].at[rows(j * r, r), rest], xe_s.at[a], xe_r.at[a], x_place)
        direct.start()
        x_directs.append(direct)
    for a, (r, n) in enumerate(W_SHAPES):
        copy = remote(ins[a], outs[a].at[rows(j * r, r)], own_s.at[a], own_r.at[a], c_place)
        copy.start()
        waits.append(copy)
    all_docs[pl.ds(me, 1)] = docs[...][None]
    ours = all_docs.at[me]
    doc_firsts = [remote(ours, ours, doc1_s.at[i], doc1_r.at[i], y_places[i]) for i in range(3)]
    for copy in doc_firsts:
        copy.start()
    loads = [pltpu.make_async_copy(ins[a], held[a], local.at[a]) for a in range(4)]
    for copy in loads:
        copy.start()
    for a, (r, n) in enumerate(W_SHAPES):
        loads[a].wait()
        copy = pltpu.make_async_copy(held[a], outs[a].at[rows(j * r, r)], back.at[a])
        copy.start()
        waits.append(copy)
    for copy in doc_firsts:
        copy.wait()
    ours = all_docs.at[pl.ds(z * 4, 4)]
    for i in range(3):
        copy = remote(ours, ours, doc2_s.at[i], doc2_r.at[i], z_places[i])
        copy.start()
        waits.append(copy)
    firsts = []
    for a, (r, n) in enumerate(W_SHAPES):
        u, cut = r // 17, W_CUTS[a]
        x_pieces[a].wait()
        here = rows(xj * r + me * u, u)
        part_a = outs[a].at[here, pl.ds(0, cut)]
        part_b = outs[a].at[here, pl.ds(cut, W_ENDS[a] - cut)]
        group = []
        for i in range(3):
            group.append(remote(part_a, part_a, a1_s.at[a, i], a1_r.at[a, i], y_places[i]))
            group.append(remote(part_b, part_b, b1_s.at[a, i], b1_r.at[a, i], z_places[i]))
        for copy in group:
            copy.start()
        firsts.append(group)
    def row_part(a, first, half):
        r, u = W_SHAPES[a][0], W_SHAPES[a][0] // 17
        start = xj * r + lax.rem(first + 4, 4) * (4 * u) + half * (2 * u)
        return outs[a].at[rows(start, 2 * u), pl.ds(0, W_CUTS[a])]

    def column_part(a, first, k):
        r, u = W_SHAPES[a][0], W_SHAPES[a][0] // 17
        start = xj * r + (4 * k + lax.rem(first + 4, 4)) * u
        return outs[a].at[rows(start, u), pl.ds(W_CUTS[a], W_ENDS[a] - W_CUTS[a])]

    heres = []
    for a in range(4):
        for copy in firsts[a]:
            copy.wait()
        rights, lefts = [], []
        for k in range(2):
            ref = row_part(a, z, k)
            rights.append(remote(ref, ref, a2_s.at[a, k], a2_r.at[a, k], z_places[0]))
            ref = row_part(a, z, 1 - k)
            lefts.append(remote(ref, ref, a2_s.at[a, 2 + k], a2_r.at[a, 2 + k], z_places[2]))
        for k in range(4):
            ref = column_part(a, y, k)
            rights.append(remote(ref, ref, b2_s.at[a, k], b2_r.at[a, k], y_places[0]))
            ref = column_part(a, y, 3 - k)
            lefts.append(remote(ref, ref, b2_s.at[a, 4 + k], b2_r.at[a, 4 + k], y_places[2]))
        for copy in rights + lefts:
            copy.start()
        heres.append((rights, lefts))
    for a, (r, n) in enumerate(W_SHAPES):
        rights, lefts = heres[a]
        passed = []
        rights[0].wait()
        ref = row_part(a, z - 1, 0)
        passed.append(remote(ref, ref, a3_s.at[a, 0], a3_r.at[a, 0], z_places[0]))
        lefts[0].wait()
        ref = row_part(a, z + 1, 1)
        passed.append(remote(ref, ref, a3_s.at[a, 1], a3_r.at[a, 1], z_places[2]))
        for k in range(2):
            rights[2 + k].wait()
            ref = column_part(a, y - 1, k)
            passed.append(remote(ref, ref, b3_s.at[a, k], b3_r.at[a, k], y_places[0]))
            lefts[2 + k].wait()
            ref = column_part(a, y + 1, 3 - k)
            passed.append(remote(ref, ref, b3_s.at[a, 2 + k], b3_r.at[a, 2 + k], y_places[2]))
        for copy in passed:
            copy.start()
        for copy in rights[1:2] + rights[4:] + lefts[1:2] + lefts[4:] + passed:
            copy.wait()
        x_directs[2 * a].wait()
        x_directs[2 * a + 1].wait()
        whole = outs[a].at[rows(xj * r, r)]
        copy = remote(whole, whole, f_s.at[a], f_r.at[a], c_place)
        copy.start()
        waits.append(copy)
    for copy in waits:
        copy.wait()


def gather_weights(weights, docs):
    dma = pltpu.SemaphoreType.DMA
    outs = [jax.ShapeDtypeStruct((4 * r, n), jnp.bfloat16) for r, n in W_SHAPES]
    return pl.pallas_call(
        weights_kernel,
        out_shape=outs + [jax.ShapeDtypeStruct((NR, 8, 128), jnp.int32)],
        in_specs=[pl.BlockSpec(memory_space=pl.ANY)] * 4 + vmem_specs(1),
        out_specs=[pl.BlockSpec(memory_space=pl.ANY)] * 4 + vmem_specs(1),
        scratch_shapes=[pltpu.VMEM(shape, jnp.bfloat16) for shape in W_SHAPES]
        + [dma((4,))] * 12
        + [dma((4, 3))] * 4
        + [dma((4, 4))] * 2
        + [dma((4, 8))] * 2
        + [dma((4, 2))] * 2
        + [dma((4, 4))] * 2
        + [dma((3,))] * 4,
        compiler_params=pltpu.CompilerParams(
            collective_id=1, has_side_effects=True, vmem_limit_bytes=VMEM_BYTES
        ),
        name="gather_weights",
    )(*weights, docs)


def lane_mask(shape, micro):
    lane = lax.broadcasted_iota(jnp.int32, shape, len(shape) - 1)
    return (lane >= HD) if micro else (lane < HD)


def allowed_block(n0, n2, first_query, queries, keys):
    i = lax.broadcasted_iota(jnp.int32, (queries, keys), 0) + first_query
    j = lax.broadcasted_iota(jnp.int32, (queries, keys), 1)
    row = lax.broadcasted_iota(jnp.int32, (queries, 1), 0) + first_query
    start = jnp.where(row >= n2, n2, jnp.where(row >= n0, n0, 0))
    return (j <= i) & (j >= start)


def scores_of(q, k, micro, allowed):
    zero = jnp.zeros((), jnp.bfloat16)
    q = jnp.where(lane_mask(q.shape, micro), q, zero)
    s = lax.dot_general(q, k, (((1,), (1,)), ((), ())), preferred_element_type=jnp.float32)
    return jnp.where(allowed, s * SCALE, masked_score)


def take(x, entry, start, count):
    return x[pl.ds(start, count), entry].reshape(count * TQ, 2 * HD)


def forward_kernel(bounds, x, q16, o, o16, lse, lse16):
    zero = jnp.zeros((), jnp.bfloat16)
    me = lax.axis_index("replica")

    def attend(q, k, v, micro, first_query):
        allowed = allowed_block(bounds[micro], bounds[2 + micro], first_query, q.shape[0], k.shape[0])
        s = scores_of(q, k, micro, allowed)
        largest = jnp.max(s, axis=-1, keepdims=True)
        e = jnp.exp(s - largest)
        summed = jnp.sum(e, axis=-1, keepdims=True)
        p = (e * (1.0 / summed)).astype(jnp.bfloat16)
        v = jnp.where(lane_mask(v.shape, micro), v, zero)
        return times(p, v), largest + jnp.log(summed)

    per = BQ // TQ
    for b in range(SEQ // BQ):
        count = (b + 1) * per
        q = take(x, 0, b * per, per)
        k = take(x, 1, 0, count)
        v = take(x, 2, 0, count)
        o0, l0 = attend(q, k, v, 0, b * BQ)
        o1, l1 = attend(q, k, v, 1, b * BQ)
        o[pl.ds(b * per, per)] = (o0 + o1).astype(jnp.bfloat16).reshape(per, TQ, 2 * HD)
        lse[pl.ds(b * BQ, BQ)] = jnp.where(lane_mask((BQ, 2 * HD), 0), l0, l1)
    q = q16[...]
    k = take(x, 3, 0, NR)
    v = take(x, 4, 0, NR)
    o0, l0 = attend(q, k, v, 0, me * TQ)
    o1, l1 = attend(q, k, v, 1, me * TQ)
    o16[...] = (o0 + o1).astype(jnp.bfloat16)
    lse16[...] = jnp.where(lane_mask((TQ, 2 * HD), 0), l0, l1)


def vmem_specs(count):
    return [pl.BlockSpec(memory_space=pltpu.VMEM)] * count


def attention_forward(bounds, x, q16):
    f32, bf16 = jnp.float32, jnp.bfloat16
    return pl.pallas_call(
        forward_kernel,
        out_shape=[
            jax.ShapeDtypeStruct((NR, TQ, 2 * HD), bf16),
            jax.ShapeDtypeStruct((TQ, 2 * HD), bf16),
            jax.ShapeDtypeStruct((SEQ, 2 * HD), f32),
            jax.ShapeDtypeStruct((TQ, 2 * HD), f32),
        ],
        in_specs=[pl.BlockSpec(memory_space=pltpu.SMEM)] + vmem_specs(2),
        out_specs=vmem_specs(4),
        compiler_params=pltpu.CompilerParams(vmem_limit_bytes=VMEM_BYTES),
        cost_estimate=cost(5),
        name="attention_forward",
    )(bounds, x, q16)


def backward_kernel(bounds, x, q16, lse, lse16, do, do16, dx, dq16, dk, dv):
    zero = jnp.zeros((), jnp.bfloat16)
    me = lax.axis_index("replica")
    bf16 = jnp.bfloat16

    def pull(q, k, v, grad, logs, micro, first_query):
        allowed = allowed_block(bounds[micro], bounds[2 + micro], first_query, q.shape[0], k.shape[0])
        s = scores_of(q, k, micro, allowed)
        soft = jnp.exp(s - logs[:, micro * HD : micro * HD + 1])
        grad = jnp.where(lane_mask(grad.shape, micro), grad, zero)
        dp = times_transposed(grad, v)
        along = jnp.sum(soft * dp, axis=-1, keepdims=True)
        ds = (soft * (dp - along)).astype(bf16)
        q = jnp.where(lane_mask(q.shape, micro), q, zero)
        k = jnp.where(lane_mask(k.shape, micro), k, zero)
        return times(ds, k), outer_sum(ds, q), outer_sum(soft.astype(bf16), grad)

    per = BQ // TQ
    for b in reversed(range(SEQ // BQ)):
        count = (b + 1) * per
        q = take(x, 0, b * per, per)
        k = take(x, 1, 0, count)
        v = take(x, 2, 0, count)
        grad = do[pl.ds(b * per, per)].reshape(BQ, 2 * HD)
        logs = lse[pl.ds(b * BQ, BQ)]
        q0, k0, v0 = pull(q, k, v, grad, logs, 0, b * BQ)
        q1, k1, v1 = pull(q, k, v, grad, logs, 1, b * BQ)
        dx[pl.ds(b * per, per), 0] = ((q0 + q1) * SCALE).astype(bf16).reshape(per, TQ, 2 * HD)
        keys = pl.ds(0, (b + 1) * BQ)
        if b == SEQ // BQ - 1:
            dk[keys] = k0 + k1
            dv[keys] = v0 + v1
        else:
            dk[keys] += k0 + k1
            dv[keys] += v0 + v1
    dx[:, 1] = (dk[...] * SCALE).astype(bf16).reshape(NR, TQ, 2 * HD)
    dx[:, 2] = dv[...].astype(bf16).reshape(NR, TQ, 2 * HD)
    q = q16[...]
    k = take(x, 3, 0, NR)
    v = take(x, 4, 0, NR)
    q0, k0, v0 = pull(q, k, v, do16[...], lse16[...], 0, me * TQ)
    q1, k1, v1 = pull(q, k, v, do16[...], lse16[...], 1, me * TQ)
    dq16[...] = ((q0 + q1) * SCALE).astype(bf16)
    dx[:, 3] = ((k0 + k1) * SCALE).astype(bf16).reshape(NR, TQ, 2 * HD)
    dx[:, 4] = (v0 + v1).astype(bf16).reshape(NR, TQ, 2 * HD)


def attention_backward(bounds, x, q16, lse, lse16, do, do16):
    f32, bf16 = jnp.float32, jnp.bfloat16
    return pl.pallas_call(
        backward_kernel,
        out_shape=[
            jax.ShapeDtypeStruct((NR, 5, TQ, 2 * HD), bf16),
            jax.ShapeDtypeStruct((TQ, 2 * HD), bf16),
        ],
        in_specs=[pl.BlockSpec(memory_space=pltpu.SMEM)] + vmem_specs(6),
        out_specs=vmem_specs(2),
        scratch_shapes=[pltpu.VMEM((SEQ, 2 * HD), f32), pltpu.VMEM((SEQ, 2 * HD), f32)],
        compiler_params=pltpu.CompilerParams(vmem_limit_bytes=VMEM_BYTES),
        cost_estimate=cost(8),
        name="attention_backward",
    )(bounds, x, q16, lse, lse16, do, do16)


QKV = 3 * D
ENTER_BLOCK, LEAVE_BLOCK, BACK_ENTER_BLOCK = 1664, 2176, 640
LEFT_AT, LEFT_WIDTH = (0, 384, 768, 1152), 2304
EARLY_AT, EARLY_WIDTH = (0, 4352, 5504), 6656
LATE_WIDTH = 3328
SMALL = 1152


def low_lanes(shape):
    return lane_mask(shape, 0)


def to_blocks(upper, lower, odd):
    half = low_lanes(upper.shape)
    if odd:
        return jnp.where(half, pltpu.roll(upper, HD, 1), lower)
    return jnp.where(half, upper, pltpu.roll(lower, HD, 1))


def from_blocks(first, second):
    half = low_lanes(first.shape)
    upper = jnp.where(half, first, pltpu.roll(second, HD, 1))
    return upper, jnp.where(half, pltpu.roll(first, HD, 1), second)


def lines(start, count):
    return pl.ds(start, count)


def enter_kernel(x, gains, biases, w, message, q16, act, mixed, held, sems):
    halves = [pl.ds(0, ENTER_BLOCK), pl.ds(ENTER_BLOCK, QKV - ENTER_BLOCK)]
    loads = [pltpu.make_async_copy(w.at[:, p], held.at[:, p], sems.at[i]) for i, p in enumerate(halves)]
    for load in loads:
        load.start()
    normed, _, _ = layer_norm(x[...].astype(jnp.float32), gains[0:1], biases[0:1])
    act[...] = normed.astype(jnp.bfloat16)
    for i, p in enumerate(halves):
        loads[i].wait()
        mixed[i, :, 0 : p.size] = times(act[...], held[:, p])

    def pack():
        for b in range(3 * H):
            kind, head = divmod(b, H)
            i, t = divmod(b // 2, ENTER_BLOCK // 128)
            part = pl.ds(t * 128, 128)
            block = to_blocks(mixed[i, 0:TQ, part], mixed[i, TQ : 2 * TQ, part], b % 2)
            if kind != 1:
                row = 1 if kind == 0 else 2
                shift = biases[row : row + 1, head * HD : (head + 1) * HD]
                block = block + jnp.concatenate([shift, shift], axis=1)
            block = block.astype(jnp.bfloat16)
            if head < H - 1:
                message[head, kind * TQ : (kind + 1) * TQ] = block
            elif kind == 0:
                q16[...] = block
            else:
                for p in range(NR):
                    message[p, (kind + 2) * TQ : (kind + 3) * TQ] = block

    pack()


def fixed(shape):
    return pl.BlockSpec(shape, lambda i: (0,) * len(shape))


def enter(x, gains, biases, w_qkv):
    bf16 = jnp.bfloat16
    shapes = [(NR, 5 * TQ, 2 * HD), (TQ, 2 * HD), (2 * TQ, D)]
    return pl.pallas_call(
        enter_kernel,
        out_shape=[jax.ShapeDtypeStruct(shape, bf16) for shape in shapes],
        in_specs=vmem_specs(3) + [pl.BlockSpec(memory_space=pl.ANY)],
        out_specs=vmem_specs(3),
        scratch_shapes=[
            pltpu.VMEM((2, 2 * TQ, ENTER_BLOCK), jnp.float32),
            pltpu.VMEM((D, QKV), bf16),
            pltpu.SemaphoreType.DMA((2,)),
        ],
        compiler_params=pltpu.CompilerParams(vmem_limit_bytes=VMEM_BYTES),
        cost_estimate=cost(5),
        name="enter",
    )(x, gains, biases, w_qkv)


CURVE = 0.044715
ROOT = 0.7978845608028654


def weight_loads(w_out, w_up, w_down, v_out, v_up, v_down, sems):
    load_up, load_down = [], []
    for i in range(2):
        part = pl.ds(i * LEAVE_BLOCK, LEAVE_BLOCK)
        load_up.append(pltpu.make_async_copy(w_up.at[:, part], v_up.at[i], sems.at[1 + i]))
        load_down.append(pltpu.make_async_copy(w_down.at[part], v_down.at[i], sems.at[3 + i]))
    return pltpu.make_async_copy(w_out, v_out, sems.at[0]), load_up, load_down


def weight_buffers():
    bf16 = jnp.bfloat16
    return [
        pltpu.VMEM((D, D), bf16),
        pltpu.VMEM((2, D, LEAVE_BLOCK), bf16),
        pltpu.VMEM((2, LEAVE_BLOCK, D), bf16),
        pltpu.SemaphoreType.DMA((5,)),
    ]


def leave_kernel(
    x, o, o16, act1, gains, biases, up_shift, w_out, w_up, w_down,
    result, resid, pre, lefts, act2, total, v_out, v_up, v_down, sems,
):
    bf16 = jnp.bfloat16
    load_out, load_up, load_down = weight_loads(w_out, w_up, w_down, v_out, v_up, v_down, sems)
    load_out.start()
    for i in range(2):
        load_up[i].start()
        load_down[i].start()

    def attention_out():
        tiles = []
        for t in range(H // 2 + 1):
            first = o[2 * t] if 2 * t < H - 1 else o16[...]
            second = o[2 * t + 1] if 2 * t + 1 < H - 1 else o16[...]
            upper, lower = from_blocks(first.astype(jnp.float32), second.astype(jnp.float32))
            tiles.append(jnp.concatenate([upper, lower], axis=0))
        attended = jnp.concatenate(tiles, axis=1)[:, :D].astype(bf16)
        load_out.wait()
        r = x[...].astype(jnp.float32) + times(attended, v_out[...]) + biases[3:4]
        resid[...] = r
        normed, _, _ = layer_norm(r, gains[1:2], biases[4:5])
        act2[...] = normed.astype(bf16)
        for s in range(4):
            part = slice(s * 272, (s + 1) * 272)
            for at, value in zip(LEFT_AT, (act1, attended, act2)):
                lefts[s, :, at : at + 272] = value[:, part]
        total[...] = r + biases[5:6]

    attention_out()
    for i in range(2):
        part = slice(i * LEAVE_BLOCK, (i + 1) * LEAVE_BLOCK)
        load_up[i].wait()
        u = times(act2[...], v_up[i]) + up_shift[:, part]
        pre[:, part] = u
        g = (0.5 * u * (1.0 + jnp.tanh(ROOT * (u + CURVE * u * u * u)))).astype(bf16)
        for s in range(2):
            lefts[2 * i + s, :, LEFT_AT[3] : LEFT_AT[3] + D] = g[:, s * D : (s + 1) * D]
        load_down[i].wait()
        total[...] += times(g, v_down[i])
    result[...] = total[...].astype(bf16)


def leave(x, o, o16, act1, gains, biases, up_shift, weights):
    _, w_out, w_up, w_down = weights
    f32, bf16 = jnp.float32, jnp.bfloat16
    rows = 2 * TQ
    return pl.pallas_call(
        leave_kernel,
        out_shape=[
            jax.ShapeDtypeStruct((rows, D), bf16),
            jax.ShapeDtypeStruct((rows, D), f32),
            jax.ShapeDtypeStruct((rows, FF), f32),
            jax.ShapeDtypeStruct((4, rows, LEFT_WIDTH), bf16),
        ],
        in_specs=vmem_specs(7) + [pl.BlockSpec(memory_space=pl.ANY)] * 3,
        out_specs=vmem_specs(4),
        scratch_shapes=[pltpu.VMEM((rows, D), bf16), pltpu.VMEM((rows, D), f32)] + weight_buffers(),
        compiler_params=pltpu.CompilerParams(vmem_limit_bytes=VMEM_BYTES),
        cost_estimate=cost(12),
        name="leave",
    )(x, o, o16, act1, gains, biases, up_shift, w_out, w_up, w_down)


def column_sum(value):
    return jnp.sum(value, axis=0, keepdims=True)


def back_leave_kernel(
    dy, resid, pre, gains, w_out, w_up, w_down,
    early, grad_resid, do, do16, sums, total, v_out, v_up, v_down, sems,
):
    f32, bf16 = jnp.float32, jnp.bfloat16
    load_out, load_up, load_down = weight_loads(w_out, w_up, w_down, v_out, v_up, v_down, sems)
    for i in range(2):
        load_down[i].start()
        load_up[i].start()
    load_out.start()
    total[...] = jnp.zeros_like(total)
    for i in range(2):
        part = slice(i * LEAVE_BLOCK, (i + 1) * LEAVE_BLOCK)
        u = pre[:, part]
        load_down[i].wait()
        grad_hidden = times_transposed(dy[...], v_down[i])
        t = jnp.tanh(ROOT * (u + CURVE * u * u * u))
        slope = 0.5 * (1.0 + t) + 0.5 * u * (1.0 - t * t) * (ROOT * (1.0 + 3.0 * CURVE * u * u))
        du = (grad_hidden * slope).astype(bf16)
        early[:, part] = du
        du_sum = column_sum(du.astype(f32))
        for s in range(2):
            sums[4 + 2 * i + s : 5 + 2 * i + s, 0:D] = du_sum[:, s * D : (s + 1) * D]
        load_up[i].wait()
        total[...] += times_transposed(du, v_up[i])
    load_out.wait()

    def norm_and_heads():
        da2 = total[...]
        _, normed, inverse = layer_norm(resid[...], gains[1:2], 0.0)
        dr = dy[...].astype(f32) + norm_back(da2, normed, inverse, gains[1:2])
        grad_resid[...] = dr
        db = dr.astype(bf16)
        for at in EARLY_AT[1:]:
            early[:, at + 1024 : at + 1152] = jnp.zeros((2 * TQ, 128), bf16)
        early[:, EARLY_AT[1] : EARLY_AT[1] + D] = db
        early[:, EARLY_AT[2] : EARLY_AT[2] + D] = dy[...]
        sums[0:1, 0:D] = column_sum(da2 * normed)
        sums[1:2, 0:D] = column_sum(da2)
        sums[2:3, 0:D] = column_sum(db.astype(f32))
        sums[3:4, 0:D] = column_sum(dy[...].astype(f32))
        heads = times_transposed(db, v_out[...])
        heads = jnp.concatenate([heads, jnp.zeros((2 * TQ, HD), f32)], axis=1)
        for b in range(H):
            tile = heads[:, (b // 2) * 128 : (b // 2 + 1) * 128]
            block = to_blocks(tile[0:TQ], tile[TQ : 2 * TQ], b % 2).astype(bf16)
            if b < H - 1:
                do[b] = block
            else:
                do16[...] = block

    norm_and_heads()


def back_leave(dy, resid, pre, gains, weights):
    _, w_out, w_up, w_down = weights
    f32, bf16 = jnp.float32, jnp.bfloat16
    rows = 2 * TQ
    shapes = [(rows, EARLY_WIDTH), (rows, D), (NR, TQ, 2 * HD), (TQ, 2 * HD), (8, SMALL)]
    types = [bf16, f32, bf16, bf16, f32]
    return pl.pallas_call(
        back_leave_kernel,
        out_shape=[jax.ShapeDtypeStruct(shape, t) for shape, t in zip(shapes, types)],
        in_specs=vmem_specs(4) + [pl.BlockSpec(memory_space=pl.ANY)] * 3,
        out_specs=vmem_specs(5),
        scratch_shapes=[pltpu.VMEM((rows, D), f32)] + weight_buffers(),
        compiler_params=pltpu.CompilerParams(vmem_limit_bytes=VMEM_BYTES),
        cost_estimate=cost(14),
        name="back_leave",
    )(dy, resid, pre, gains, w_out, w_up, w_down)


def back_enter_kernel(x, back, dq16, grad_resid, before, gains, w, late, grad_in, sums, held, sems):
    f32, bf16 = jnp.float32, jnp.bfloat16
    pieces = [pl.ds(0, BACK_ENTER_BLOCK), pl.ds(BACK_ENTER_BLOCK, D - BACK_ENTER_BLOCK)]
    loads = [pltpu.make_async_copy(w.at[p], held.at[p], sems.at[i]) for i, p in enumerate(pieces)]
    for load in loads:
        load.start()

    def unpack():
        def last(kind):
            total = back[0, (kind + 2) * TQ : (kind + 3) * TQ].astype(f32)
            for p in range(1, NR):
                total = total + back[p, (kind + 2) * TQ : (kind + 3) * TQ].astype(f32)
            return total

        def block(b):
            kind, head = divmod(b, H)
            if head < H - 1:
                return back[head, kind * TQ : (kind + 1) * TQ].astype(f32)
            return dq16[...].astype(f32) if kind == 0 else last(kind)

        for t in range(3 * H // 2 + 1):
            first = block(2 * t)
            second = block(2 * t + 1) if 2 * t + 1 < 3 * H else jnp.zeros_like(first)
            upper, lower = from_blocks(first, second)
            late[0:TQ, t * 128 : (t + 1) * 128] = upper.astype(bf16)
            late[TQ : 2 * TQ, t * 128 : (t + 1) * 128] = lower.astype(bf16)

    unpack()
    products = []
    for load, piece in zip(loads, pieces):
        load.wait()
        products.append(times_transposed(late[:, 0:QKV], held[piece]))

    def finish():
        da1 = jnp.concatenate(products, axis=1)
        _, normed, inverse = layer_norm(x[...].astype(f32), gains[0:1], 0.0)
        dx = grad_resid[...] + norm_back(da1, normed, inverse, gains[0:1])
        grad_in[...] = dx.astype(bf16)
        sums[...] = jnp.zeros_like(sums)
        sums[0:1, 0:D] = column_sum(da1 * normed)
        sums[1:2, 0:D] = column_sum(da1)
        sums[2:3, 0:D] = column_sum(late[:, 0:D].astype(f32))
        sums[3:4, 0:D] = column_sum(late[:, 2 * D : QKV].astype(f32))
        sums[4:12, 0:D] = before[:, 0:D]

    finish()


def back_enter(x, back, dq16, grad_resid, before, gains, w_qkv):
    f32, bf16 = jnp.float32, jnp.bfloat16
    rows = 2 * TQ
    return pl.pallas_call(
        back_enter_kernel,
        out_shape=[
            jax.ShapeDtypeStruct((rows, LATE_WIDTH), bf16),
            jax.ShapeDtypeStruct((rows, D), bf16),
            jax.ShapeDtypeStruct((16, SMALL), f32),
        ],
        in_specs=vmem_specs(6) + [pl.BlockSpec(memory_space=pl.ANY)],
        out_specs=vmem_specs(3),
        scratch_shapes=[pltpu.VMEM((D, QKV), bf16), pltpu.SemaphoreType.DMA((2,))],
        compiler_params=pltpu.CompilerParams(vmem_limit_bytes=VMEM_BYTES),
        cost_estimate=cost(5),
        name="back_enter",
    )(x, back, dq16, grad_resid, before, gains, w_qkv)


AT_OUT, AT_UP, AT_DOWN, DOWN_STEP = 3584, 4736, 9088, 1152
LATE_FREE, LATE_CHUNK = 3328, 256
EARLY_FREE, EARLY_CHUNK = 13696, 640


def weight_sums_kernel(
    l0, l1, l2, l3, e0, e1, e2, late, small, out,
    lefts, early, mixed, got, strip, g, tr, ins, ad, part, mid, fin,
    loc, late_s, late_r, small_s, small_r,
    p_s, p_r, q_s, q_r, m_s, m_r, n_s, n_r, e_s, e_r, w_s, w_r, last,
):
    f32, bf16 = jnp.float32, jnp.bfloat16
    rows = 2 * TQ
    j = lax.axis_index("shard")
    me = lax.axis_index("replica")
    z, y = me // 4, lax.rem(me, 4)
    xj = lax.rem(j + 2, 4)
    cj = j + 1 - 2 * lax.rem(j, 2)
    places = [{"shard": xj}, {"shard": cj}, {"shard": lax.rem(cj + 2, 4)}]
    y_places = [{"replica": y_peer(me, d)} for d in (1, 2, 3)]
    z_places = [{"replica": z_peer(me, d)} for d in (1, 2, 3)]
    greet(places + y_places + z_places)

    def slot(ref, k):
        return ref.at[pl.ds(k * rows, rows)]

    across = remote(late, slot(mixed, 1), late_s.at[0], late_r.at[0], places[0])
    across.start()
    beside = remote(late, slot(mixed, 2), late_s.at[1], late_r.at[1], places[1])
    beside.start()
    early_relay = remote(e1, slot(early, 3), late_s.at[3], late_r.at[3], places[1])
    early_relay.start()
    smalls = [remote(small, got.at[k], small_s.at[k], small_r.at[k], places[k]) for k in range(3)]
    for copy in smalls:
        copy.start()
    loads = [pltpu.make_async_copy(late, slot(mixed, 0), loc.at[0])]
    loads.append(pltpu.make_async_copy(l0.at[j], slot(lefts, 0), loc.at[1]))
    for k, ref in enumerate((l1, l2, l3)):
        loads.append(pltpu.make_async_copy(ref, slot(lefts, k + 1), loc.at[2 + k]))
    for k, ref in enumerate((e0, e1, e2)):
        loads.append(pltpu.make_async_copy(ref, slot(early, k), loc.at[5 + k]))
    for copy in loads:
        copy.start()
    for copy in loads:
        copy.wait()
    early_relay.wait()

    def keep(product, put_at):
        g[:, put_at] = product[0:RED_ROWS]
        strip[:, put_at] = product[RED_ROWS:272]

    def stripe(left_at, right, right_at, at, columns, width):
        @pl.loop(0, columns // width)
        def _(i):
            take_at = pl.ds(pl.multiple_of(right_at + i * width, 128), width)
            put_at = pl.ds(pl.multiple_of(at + i * width, 128), width)
            product = outer_sum(lefts[:, left_at : left_at + 272], right[:, take_at])
            keep(product.astype(bf16), put_at)

    stripe(LEFT_AT[2], early, EARLY_AT[0], AT_UP, FF, 2176)
    product = outer_sum(lefts[:, LEFT_AT[1] : LEFT_AT[1] + 272], early[:, EARLY_AT[1] : EARLY_AT[2]])
    keep(product.astype(bf16), slice(AT_OUT, AT_UP))
    for s in range(4):
        at = AT_DOWN + s * DOWN_STEP
        first = LEFT_AT[3] + s * 272
        product = outer_sum(lefts[:, first : first + 272], early[:, EARLY_AT[2] : EARLY_WIDTH])
        keep(product.astype(bf16), slice(at, at + DOWN_STEP))
    g[:, EARLY_FREE:] = jnp.zeros((RED_ROWS, EARLY_CHUNK), bf16)
    for c in range(16):
        first = AT_OUT + c * EARLY_CHUNK
        width = min(EARLY_CHUNK, EARLY_FREE - first)
        g[16 * c : 16 * c + 16, EARLY_FREE : EARLY_FREE + width] = strip[:, first : first + width]

    firsts, seconds = (y_places, z_places), (z_places, y_places)
    here, there = (y, z), (z, y)

    def at(side, first, second):
        piece = 4 * second + lax.rem(first + 4, 4)
        return (pl.ds(side * HALF, HALF), pl.ds(pl.multiple_of(piece * PIECE, 128), PIECE))

    def piece_of(ref, side, first, second):
        return ref.at[at(side, first, second)]

    def value_of(side, first, second):
        return g[at(side, first, second)].astype(f32)

    opened, direct, added = {}, {}, {}

    def open_piece(s, k):
        t, right, left = here[s], firsts[s][0], firsts[s][2]
        copy = remote(piece_of(g, s, t + 2, k), tr.at[s, k], p_s.at[s, k], p_r.at[s, k], right if k < 2 else left)
        copy.start()
        opened[s, k] = copy

    def direct_piece(s, k):
        t, right, left = here[s], firsts[s][0], firsts[s][2]
        if k < 2:
            copy = remote(piece_of(g, s, t - 1, k), ins.at[s, 1, k], p_s.at[s, 4 + k], p_r.at[s, 4 + k], left)
        else:
            copy = remote(piece_of(g, s, t + 1, k), ins.at[s, 0, k], p_s.at[s, 4 + k], p_r.at[s, 4 + k], right)
        copy.start()
        direct[s, k] = copy

    def add_piece(s, k):
        t, right, left = here[s], firsts[s][0], firsts[s][2]
        opened[s, k].wait()
        mine = value_of(s, t + 1 if k < 2 else t - 1, k)
        ad[s, k] = (tr[s, k].astype(f32) + mine).astype(bf16)
        to, side = (right, 0) if k < 2 else (left, 1)
        copy = remote(ad.at[s, k], ins.at[s, side, k], q_s.at[s, k], q_r.at[s, k], to)
        copy.start()
        added[s, k] = copy

    for k in (1, 2, 3):
        for s in range(2):
            open_piece(s, k)
    for k in (1, 2, 3):
        for s in range(2):
            direct_piece(s, k)
    for k in (1, 2):
        for s in range(2):
            add_piece(s, k)
    across.wait()
    relay = remote(slot(mixed, 1), slot(mixed, 3), late_s.at[2], late_r.at[2], places[1])
    relay.start()
    beside.wait()
    for s in range(2):
        add_piece(s, 3)
    relay.wait()
    stripe(LEFT_AT[0], mixed, 0, 0, LATE_WIDTH, 1664)
    for copy in smalls:
        copy.wait()
    for c in range(13):
        g[16 * c : 16 * c + 16, LATE_FREE:AT_OUT] = strip[:, c * LATE_CHUNK : (c + 1) * LATE_CHUNK]
    sums = (small[...] + got[0] + got[1] + got[2]).astype(bf16)
    for c in range(3):
        row = 208 + 16 * c
        g[row : row + 16, LATE_FREE:AT_OUT] = sums[:, c * LATE_CHUNK : (c + 1) * LATE_CHUNK]
    for c in range(5):
        first = 3 * LATE_CHUNK + c * 64
        g[16 * c : 16 * c + 16, QKV:LATE_FREE] = sums[:, first : first + 64]
    for s in range(2):
        open_piece(s, 0)
        direct_piece(s, 0)
    for s in range(2):
        add_piece(s, 0)

    middles = []
    for s in range(2):
        for k in range(4):
            direct[s, k].wait()
            added[s, k].wait()
            part[s, k] = (value_of(s, here[s], k) + ins[s, 0, k].astype(f32) + ins[s, 1, k].astype(f32)).astype(bf16)
        group = []
        for i in range(3):
            to = lax.rem(there[s] + 1 + i, 4)
            group.append(remote(part.at[s, to], mid.at[s, i], m_s.at[s, i], m_r.at[s, i], seconds[s][i]))
        for copy in group:
            copy.start()
        middles.append(group)
    backs = []
    for s in range(2):
        for copy in middles[s]:
            copy.wait()
        total = part[s, there[s]].astype(f32)
        for i in range(3):
            total = total + mid[s, i].astype(f32)
        fin[s] = total.astype(bf16)
        where = piece_of(out, s, here[s], there[s])
        group = [remote(fin.at[s], where, n_s.at[s, i], n_r.at[s, i], seconds[s][i]) for i in range(3)]
        group.append(pltpu.make_async_copy(fin.at[s], where, last.at[s]))
        for copy in group:
            copy.start()
        backs.append(group)
    to_rights, to_lefts = [], []
    for s in range(2):
        t, right, left = here[s], firsts[s][0], firsts[s][2]
        for copy in backs[s]:
            copy.wait()
        to_right, to_left = [], []
        for k in range(4):
            ref = piece_of(out, s, t, k)
            to_right.append(remote(ref, ref, e_s.at[s, k], e_r.at[s, k], right))
            ref = piece_of(out, s, t, 3 - k)
            to_left.append(remote(ref, ref, e_s.at[s, 4 + k], e_r.at[s, 4 + k], left))
        for k in range(4):
            to_right[k].start()
            to_left[k].start()
        to_rights.append(to_right)
        to_lefts.append(to_left)
    passed = []
    for k in range(2):
        for s in range(2):
            t, right, left = here[s], firsts[s][0], firsts[s][2]
            to_rights[s][k].wait()
            ref = piece_of(out, s, t - 1, k)
            copy = remote(ref, ref, w_s.at[s, k], w_r.at[s, k], right)
            copy.start()
            passed.append(copy)
            to_lefts[s][k].wait()
            ref = piece_of(out, s, t + 1, 3 - k)
            copy = remote(ref, ref, w_s.at[s, 2 + k], w_r.at[s, 2 + k], left)
            copy.start()
            passed.append(copy)
    for s in range(2):
        for copy in to_rights[s][2:] + to_lefts[s][2:]:
            copy.wait()
    for copy in passed:
        copy.wait()


def weight_sums(lefts, early, late, small):
    dma = pltpu.SemaphoreType.DMA
    f32, bf16 = jnp.float32, jnp.bfloat16
    anywhere = pl.BlockSpec(memory_space=pl.ANY)
    piece = (HALF, PIECE)
    return pl.pallas_call(
        weight_sums_kernel,
        out_shape=jax.ShapeDtypeStruct((RED_ROWS, NR * PIECE), bf16),
        in_specs=[anywhere] * 8 + vmem_specs(1),
        out_specs=anywhere,
        scratch_shapes=[
            pltpu.VMEM((8 * TQ, LEFT_WIDTH), bf16),
            pltpu.VMEM((8 * TQ, EARLY_WIDTH), bf16),
            pltpu.VMEM((8 * TQ, LATE_WIDTH), bf16),
            pltpu.VMEM((3, 16, SMALL), f32),
            pltpu.VMEM((16, NR * PIECE), bf16),
            pltpu.VMEM((RED_ROWS, NR * PIECE), bf16),
            pltpu.VMEM((2, 4) + piece, bf16),
            pltpu.VMEM((2, 2, 4) + piece, bf16),
            pltpu.VMEM((2, 4) + piece, bf16),
            pltpu.VMEM((2, 4) + piece, bf16),
            pltpu.VMEM((2, 3) + piece, bf16),
            pltpu.VMEM((2,) + piece, bf16),
            dma((8,)),
            dma((4,)), dma((4,)), dma((3,)), dma((3,)),
        ]
        + [dma((2, 8))] * 2
        + [dma((2, 4))] * 2
        + [dma((2, 3))] * 4
        + [dma((2, 8))] * 2
        + [dma((2, 4))] * 2
        + [dma((2,))],
        compiler_params=pltpu.CompilerParams(
            collective_id=2, has_side_effects=True, vmem_limit_bytes=VMEM_BYTES
        ),
        name="weight_sums",
    )(*lefts, *early, late, small)


def widen_kernel(g, qkv, out, up, down, small, late_free, early_free):
    i = pl.program_id(0)
    f32 = jnp.float32

    @pl.when(i < 4)
    def _():
        qkv[...] = g[:, 0:QKV].astype(f32)
        out[...] = g[:, AT_OUT : AT_OUT + D].astype(f32)
        up[...] = g[:, AT_UP : AT_UP + FF].astype(f32)
        for s in range(4):
            at = AT_DOWN + s * DOWN_STEP
            down[s] = g[:, at : at + D].astype(f32)
        rows = pl.ds(pl.multiple_of(i * 64, 64), 64)
        late_free[rows] = g[:, LATE_FREE - 128 : AT_OUT]
        early_free[rows] = g[:, EARLY_FREE:]

    @pl.when(i == 4)
    def _():
        late = [late_free[16 * c : 16 * c + 16, 128:].astype(f32) for c in range(16)]
        qkv[0:16] = jnp.concatenate(late[:13], axis=1)[:, :QKV]
        early = [early_free[16 * c : 16 * c + 16, :].astype(f32) for c in range(16)]
        rest = jnp.concatenate(early, axis=1)
        out[0:16] = rest[:, 0:D]
        first = AT_UP - AT_OUT
        up[0:16] = rest[:, first : first + FF]
        for s in range(4):
            at = AT_DOWN - AT_OUT + s * DOWN_STEP
            down[s, 0:16] = rest[:, at : at + D]
        small[:, 0:768] = jnp.concatenate(late[13:], axis=1)
        for c in range(5):
            small[:, 768 + 64 * c : 832 + 64 * c] = late_free[16 * c : 16 * c + 16, 64:128].astype(f32)
        small[:, 1088:SMALL] = jnp.zeros((16, SMALL - 1088), f32)


def widen(g):
    f32, bf16 = jnp.float32, jnp.bfloat16
    return pl.pallas_call(
        widen_kernel,
        grid=(5,),
        out_shape=[
            jax.ShapeDtypeStruct((272, QKV), f32),
            jax.ShapeDtypeStruct((272, D), f32),
            jax.ShapeDtypeStruct((272, FF), f32),
            jax.ShapeDtypeStruct((4, 272, D), f32),
            jax.ShapeDtypeStruct((16, SMALL), f32),
        ],
        in_specs=[pl.BlockSpec((64, NR * PIECE), lambda i: (jnp.minimum(i, 3), 0))],
        out_specs=[
            pl.BlockSpec((64, QKV), lambda i: (i, 0)),
            pl.BlockSpec((64, D), lambda i: (i, 0)),
            pl.BlockSpec((64, FF), lambda i: (i, 0)),
            pl.BlockSpec((4, 64, D), lambda i: (0, i, 0)),
            fixed((16, SMALL)),
        ],
        scratch_shapes=[
            pltpu.VMEM((RED_ROWS, 384), bf16),
            pltpu.VMEM((RED_ROWS, EARLY_CHUNK), bf16),
        ],
        compiler_params=pltpu.CompilerParams(vmem_limit_bytes=VMEM_BYTES),
        name="widen",
    )(g)


def layer_forward(x, bounds, gains, biases, up_shift, weights):
    message, q16, act1 = enter(x, gains, biases, weights[0])
    whole = swap(message, 3).reshape(NR, 5, TQ, 2 * HD)
    o, o16, lse, lse16 = attention_forward(bounds, whole, q16)
    result, resid, pre, lefts = leave(x, swap(o, 4), o16, act1, gains, biases, up_shift, weights)
    return result, (whole, q16, lse, lse16, resid, pre), lefts


def layer_backward(dy, x, kept, bounds, gains, weights, tie=None):
    whole, q16, lse, lse16, resid, pre = kept
    early, grad_resid, do, do16, sums = back_leave(dy, resid, pre, gains, weights)
    dx, dq16 = attention_backward(bounds, whole, q16, lse, lse16, swap(do, 4), do16)
    dx, tie = lax.optimization_barrier((dx, tie))
    back = swap(dx.reshape(NR, 5 * TQ, 2 * HD), 3)
    late, grad_in, small = back_enter(x, back, dq16, grad_resid, sums, gains, weights[0])
    return grad_in, early, late, small, tie


X_ROUTE = [(j, j ^ 2) for j in range(4)]
C_ROUTE = [(j, j ^ 1) for j in range(4)]


CX_ROUTE = [(j, j ^ 3) for j in range(4)]


def everyone(value):
    return value, lax.ppermute(value, "shard", X_ROUTE), lax.ppermute(value, "shard", C_ROUTE)


def own_columns(cut):
    j = lax.axis_index("shard")

    def of(shard):
        return lax.dynamic_index_in_dim(cut, shard, 0, keepdims=False)

    across, beside = lax.rem(j + 2, 4), j + 1 - 2 * lax.rem(j, 2)
    return (
        cut,
        lax.ppermute(of(across), "shard", X_ROUTE),
        lax.ppermute(of(beside), "shard", C_ROUTE),
        lax.ppermute(of(lax.rem(beside + 2, 4)), "shard", CX_ROUTE),
    )


def shards(tokens, cotangent, doc_ids, gains, biases, up_bias, w_qkv, w_out, w_up, w_down):
    is_first = lax.axis_index("section") == 0
    ids = doc_ids[:, 0]
    counts = jnp.stack([jnp.sum((ids == n).astype(jnp.int32), axis=1) for n in (0, 2)])
    counts = jnp.pad(counts, ((0, 6), (0, 126)))
    *weights, counts = gather_weights((w_qkv[0], w_out[0], w_up[0], w_down[0]), counts)
    counts = jnp.sum(counts[:, :2, :2], axis=0)
    bounds = jnp.concatenate([counts[0], SEQ - counts[1]])
    gains, biases = gains[0], biases[0]
    own_in = tokens.reshape(2 * TQ, D)
    own_cot = cotangent.reshape(2 * TQ, D)
    result, _, _ = layer_forward(own_in, bounds, gains, biases, up_bias, weights)
    inbox = lax.ppermute(result, "section", [(0, 1)])
    inputs = jnp.where(is_first, own_in, inbox)
    layer_out, kept, lefts = layer_forward(inputs, bounds, gains, biases, up_bias, weights)
    lefts = own_columns(lefts)
    grad_in, _, _, _, others = layer_backward(own_cot, inputs, kept, bounds, gains, weights, lefts[1:])
    lefts = (lefts[0], *others)
    inbox = lax.ppermute(grad_in, "section", [(1, 0)])
    dy = jnp.where(is_first, inbox, own_cot)
    grad_in, early, late, small, _ = layer_backward(dy, inputs, kept, bounds, gains, weights)
    summed = weight_sums(lefts, everyone(early), late, small)
    qkv, out, up, down, small = widen(summed)
    small = small[:, :D]
    return (
        layer_out.reshape(1, 2, 1, TQ, D),
        grad_in.reshape(1, 2, 1, TQ, D),
        jnp.stack([small[0], small[4]])[None],
        jnp.stack([small[k] for k in (1, 2, 3, 6, 5, 7)])[None],
        small[8:12].reshape(1, FF),
        qkv[None],
        out[None],
        up[None],
        down.reshape(1, 1088, D),
    )


def solution(mesh):
    placed = (
        P(None, "shard", "replica", None),
        P(None, "shard", "replica", None),
        P(None, "shard", "replica"),
        P("section", None, None),
        P("section", None, None),
        P("section", None),
        P("section", "shard", None),
        P("section", "shard", None),
        P("section", "shard", None),
        P("section", "shard", None),
    )
    return jax.shard_map(
        shards,
        mesh=mesh,
        in_specs=placed,
        out_specs=(
            P("section", None, "shard", "replica", None),
            P("section", None, "shard", "replica", None),
            P("section", None, None),
            P("section", None, None),
            P("section", None),
            P("section", "shard", None),
            P("section", "shard", None),
            P("section", "shard", None),
            P("section", "shard", None),
        ),
        check_vma=False,
    )
```
